32 devices in a mesh: req: 8 (over z, y), tp: 4 (over x, core).
Axes of the slice: x: 2, y: 2, z: 4, core: 2. Of those that a mesh axis runs over, the one named last changes fastest.
Arguments:
- hidden_in: bfloat16 [2048, 1024], P('req'), may hold values from -42 to 42
- prompt_kv: bfloat16 [2, 64, 512, 1024], P(None, 'req', None, 'tp'), may hold values from -9 to 9
- tail_kv: bfloat16 [2, 2048, 64, 1024], P(None, 'req', None, 'tp'), may hold values from -9 to 9
- group_of: int32 [2048], P('req'), may hold values from 0 to 7
- prompt_len: int32 [64], P('req'), may hold values from 64 to 512, as said below
- tail_len: int32 [2048], P('req'), may hold values from 0 to 63, as said below
- bucket_of: int32 [577], replicated, may hold values from 0 to 31, never falling along the last dimension, each value on 1 to 38 neighbouring positions
- bias_table: float32 [32, 16], P(None, 'tp'), may hold values from -6 to 302
- attn_gain: float32 [1024], replicated, may hold values from 0.1 to 1.9
- w_query: bfloat16 [1024, 1024], P(None, 'tp'), may hold values from -0.1875 to 0.1875
- w_key: bfloat16 [1024, 1024], P(None, 'tp'), may hold values from -0.1875 to 0.1875
- w_value: bfloat16 [1024, 1024], P(None, 'tp'), may hold values from -0.1875 to 0.1875
- w_out: bfloat16 [1024, 1024], P('tp'), may hold values from -0.75 to 0.75
- ffn_gain: float32 [1024], replicated, may hold values from 0.1 to 1.9
- router_weight: bfloat16 [1024, 8], replicated, may hold values from -0.1875 to 0.1875
- expert_ids: int32 [2048, 2], P('req'), may hold values from 0 to 7, all different within a row; in each aligned block of 256 rows (0 to 255, 256 to 511, ...) at most 80 rows name the same one
- w_gate: bfloat16 [8, 1024, 2816], P('req', None, 'tp'), may hold values from -0.1875 to 0.1875
- w_up: bfloat16 [8, 1024, 2816], P('req', None, 'tp'), may hold values from -0.1875 to 0.1875
- w_down: bfloat16 [8, 2816, 1024], P('req', 'tp'), may hold values from -0.109375 to 0.109375
- new_slot: int32 [2048], replicated, may hold values from 0 to 2047, as said below
Outputs:
- out_hidden: bfloat16 [2048, 1024], P('req')
- new_tail_kv: bfloat16 [2, 2048, 64, 1024], P(None, 'req', None, 'tp')
The draws below stay inside these ranges and needn't reach their ends.
Inputs may be any that keep to these rules, and one draw needn't show every extreme that they name: `expert_ids`: in each replica's aligned block of 256 tokens no expert is named by more than 80 of them, a bound that some block reaches. `new_slot`: A permutation. Exactly 4 requests of each replica are movers; all movers of one replica go to one replica (possibly itself), each taking a slot that a mover of that replica leaves; every other request keeps its slot. `prompt_len`: each replica has a group of 512 rows. `tail_len`: each replica has a request of 63 own rows and one of none.
All inputs are finite; a program needn't handle non-finite values.
Results may differ from the reference program's by a relative error of at most 0.013.
Values may be sent and summed in bfloat16 or wider, within the bound.
No kernel may reach another device: no remote copies, remote signals or barrier semaphores. Data moves between devices by JAX's collectives and lax.ppermute only.
A program may use at most 128 MiB of HBM per device.

```python
import math
import jax
import jax.numpy as jnp
import numpy as np
from jax import lax

D = 1024
HEADS = 16
HD = 64
FF = 2816
BUCKETS = 32
TOP = 2
R_DEV = 256
G_DEV = 8
PRE = 512
TAIL = 64
MIG = 4
EXPERTS = 8
CAP = 80
REQS = 2048
GROUPS = 64
MAXDIST = 577
N_REQ = 8


def draw_hidden_in(key, part):
    k1, k2, k3 = jax.random.split(jax.random.fold_in(key, 5), 3)
    row_scale = jnp.exp(jax.random.uniform(k1, (REQS, 1), minval=math.log(0.4), maxval=math.log(4.0)))
    col_scale = jnp.exp(jax.random.uniform(k2, (1, D), minval=math.log(0.6), maxval=math.log(1.7)))
    base = jnp.clip(jax.random.normal(k3, (REQS, D)), -6.0, 6.0)
    return (base * row_scale * col_scale).astype(jnp.float32).astype(jnp.bfloat16)


def draw_prompt_len(key, part):
    k1, k2 = jax.random.split(jax.random.fold_in(key, 3))
    lens = jax.random.randint(k1, (N_REQ, G_DEV), PRE // 8, PRE + 1)
    order = jax.vmap(lambda k: jax.random.permutation(k, G_DEV))(jax.random.split(k2, N_REQ))
    cols = jnp.arange(G_DEV)[None, :]
    lens = jnp.where(cols == order[:, :1], PRE, lens)
    lens = jnp.where(cols == order[:, 1:2], PRE // 8, lens)
    return lens.reshape(-1).astype(jnp.int32)


def draw_tail_len(key, part):
    k1, k2 = jax.random.split(jax.random.fold_in(key, 4))
    lens = jax.random.randint(k1, (N_REQ, R_DEV), 0, TAIL)
    order = jax.vmap(lambda k: jax.random.permutation(k, R_DEV))(jax.random.split(k2, N_REQ))
    cols = jnp.arange(R_DEV)[None, :]
    lens = jnp.where(cols == order[:, :1], TAIL - 1, lens)
    lens = jnp.where(cols == order[:, 1:2], 0, lens)
    return lens.reshape(-1).astype(jnp.int32)


def draw_bias_table(key, part):
    k1 = jax.random.fold_in(jax.random.fold_in(key, 7), 0)
    return jnp.clip(1.5 * jax.random.normal(k1, (BUCKETS, HEADS)), -6.0, 6.0).astype(jnp.float32)


def draw_new_slot(key, part):
    k1, k2 = jax.random.split(jax.random.fold_in(key, 11))
    order = jax.vmap(lambda k: jax.random.permutation(k, R_DEV))(jax.random.split(k1, N_REQ))
    movers = order[:, :MIG].astype(jnp.int32)
    dest = jax.random.permutation(k2, N_REQ).astype(jnp.int32)
    base = jnp.arange(N_REQ, dtype=jnp.int32)[:, None] * R_DEV
    sources = (base + movers).reshape(-1)
    targets = (dest[:, None] * R_DEV + movers[dest]).reshape(-1)
    slots = jnp.arange(REQS, dtype=jnp.int32)
    return slots.at[sources].set(targets.astype(jnp.int32))


def set_ends(entries, stream_key, least, top_value):
    extent = entries.shape
    place = [jax.random.randint(jax.random.fold_in(stream_key, axis), (), 0, extent[axis]) for axis in range(len(extent))]
    entries = entries.at[tuple(place)].set(least)
    longest = extent.index(max(extent))
    place[longest] = (place[longest] + 1) % extent[longest]
    return entries.at[tuple(place)].set(top_value)


def shard_levels(own_key, extent, cuts, smallest, top_value):
    factor_of, own = 1.0, jax.random.fold_in(own_key, 6)
    for dim, parts in cuts:
        steps = jnp.exp(jax.random.uniform(jax.random.fold_in(own, dim), (parts,), jnp.float32, smallest / len(cuts), top_value / len(cuts)))
        factor_of = factor_of * jnp.repeat(steps, extent[dim] // parts).reshape([-1 if axis == dim else 1 for axis in range(len(extent))])
    return factor_of


def split_up(number_of, total, reach, lean):
    weights = [(1 << 20) // math.isqrt(rank ** lean) + 1 for rank in range(2, number_of + 1)]
    spare, counts = total - reach - (number_of - 1), [1] * (number_of - 1)
    while spare > 0:
        candidates = [i for i in range(number_of - 1) if counts[i] < reach]
        whole, budget = sum([weights[i] for i in candidates]), spare
        for i in candidates:
            extra = min(reach - counts[i], max(1, budget * weights[i] // whole), spare)
            counts[i] = counts[i] + extra
            spare = spare - extra
    return np.array([reach] + counts)


def ragged_sizes(rng, count, total, most, lean):
    if count == 2:
        one = jax.random.randint(rng, (), max(1, total - most), min(most, total - 1) + 1)
        return jnp.stack([one, total - one])
    lengths = jnp.asarray(split_up(count, total, most, lean), jnp.int32)
    twos = (count - 1) // 2
    donor, taker = lengths[1:1 + 2 * twos:2], lengths[2:2 + 2 * twos:2]
    slack = jnp.minimum(donor - 1, most - taker)
    moved = jax.random.randint(jax.random.fold_in(rng, 1), (twos,), 0, 1 << 20) % (slack + 1)
    lengths = lengths.at[1:1 + 2 * twos:2].set(donor - moved).at[2:2 + 2 * twos:2].set(taker + moved)
    return lengths[jax.random.permutation(jax.random.fold_in(rng, 2), count)]


def assign_block(own_key, own, number, rows, count, top, most, lean):
    order = jax.random.permutation(own_key, count)
    packed, ordinary = portions_of(count, rows * top, most, lean, True), portions_of(count, rows * top, most, lean, False)
    places = jnp.arange(count)

    def named(tallies, offset_by):
        used = int((tallies > 0).sum())
        fixed = max(1, used // 4)
        moved = fixed + (places - fixed + offset_by * (used - fixed)) % max(1, count - fixed)
        return jnp.zeros((count,), jnp.int32).at[order[jnp.where(places < fixed, places, moved)]].set(jnp.asarray(tallies, jnp.int32))

    tallies = jnp.where(number % 4 == 0, named(packed, number // 4), named(ordinary, number - number // 4 - 1))
    mixed = jax.random.permutation(jax.random.fold_in(own, 3), count)
    giver, receiver = mixed[0:count // 2 * 2:2], mixed[1:count // 2 * 2:2]
    margin = jnp.minimum(tallies[giver] - 1, most - tallies[receiver]) // 2
    margin = jnp.where((giver == order[0]) | (receiver == order[0]) | (tallies[receiver] == 0), 0, jnp.maximum(margin, 0))
    moved = jax.random.randint(jax.random.fold_in(own, 4), (count // 2,), 0, 1 << 20) % (margin + 1)
    tallies = tallies.at[giver].add(-moved).at[receiver].add(moved)
    labels = jnp.searchsorted(jnp.cumsum(tallies), jnp.arange(rows * top), side="right").astype(jnp.int32)
    grid = labels.reshape(top, rows).T
    grid = grid[jax.random.permutation(jax.random.fold_in(own, 1), rows)]
    offset_by = jax.random.randint(jax.random.fold_in(own, 2), (rows, 1), 0, top)
    return jnp.take_along_axis(grid, (jnp.arange(top)[None, :] + offset_by) % top, axis=1)


def portions_of(amount, total, reach, skew, full):
    weights = [(1 << 20) // math.isqrt(standing ** skew) + 1 for standing in range(1, amount + 1)]
    largest = reach if full else min(reach, max(-(-total // amount), total * weights[0] // sum(weights)))
    least = 1 if total - largest >= amount - 1 else 0
    holding, surplus = [largest] + [least] * (amount - 1), total - largest - least * (amount - 1)
    while surplus > 0:
        candidates = [i for i in range(1, amount) if holding[i] < largest] or [i for i in range(1, amount) if holding[i] < reach]
        pool, budget = sum([weights[i] for i in candidates]), surplus
        for i in candidates:
            addition = min(reach - holding[i], max(1, budget * weights[i] // pool), surplus)
            holding[i] = holding[i] + addition
            surplus = surplus - addition
    return np.array(holding)


def noise(stream_key, dims, deviation, limit, cuts=(), held_as=jnp.bfloat16):
    entries = jax.random.normal(stream_key, dims, jnp.float32) * deviation
    if len(cuts) > 0:
        entries = shard_levels(stream_key, dims, cuts, -0.22, 0.18) * entries
    return jnp.clip(entries, min=-limit, max=limit).astype(held_as)


def setup_inputs(seed: int = 0) -> dict:
    keys = jax.random.split(jax.random.key(seed), 21)
    hidden_in = draw_hidden_in(jax.random.fold_in(keys[20], 71), 0)
    prompt_kv = noise(keys[1], (2, GROUPS, PRE, HEADS * HD), 1.5, 9.0, ((1, 8), (3, 4)))
    tail_kv = noise(keys[2], (2, REQS, TAIL, HEADS * HD), 1.5, 9.0, ((1, 8), (3, 4)))
    group_of = set_ends(jax.random.randint(keys[3], (REQS,), 0, G_DEV), jax.random.fold_in(keys[3], 1), 0, G_DEV - 1).astype(jnp.int32)
    prompt_len = draw_prompt_len(jax.random.fold_in(keys[20], 71), 0)
    tail_len = draw_tail_len(jax.random.fold_in(keys[20], 71), 0)
    bucket_of = jnp.searchsorted(jnp.cumsum(ragged_sizes(keys[6], BUCKETS, MAXDIST, (PRE + TAIL + BUCKETS) // BUCKETS * 2, 2)), jnp.arange(MAXDIST), side="right").astype(jnp.int32)
    bias_table = draw_bias_table(jax.random.fold_in(keys[20], 71), 0)
    attn_gain = jnp.clip(1.0 + 0.18 * jax.random.normal(keys[8], (D,), jnp.float32), 0.1, 1.9)
    w_query = noise(keys[9], (D, HEADS * HD), D ** -0.5, 0.1875, ((1, 4),))
    w_key = noise(keys[10], (D, HEADS * HD), D ** -0.5, 0.1875, ((1, 4),))
    w_value = noise(keys[11], (D, HEADS * HD), D ** -0.5, 0.1875, ((1, 4),))
    w_out = noise(keys[12], (HEADS * HD, D), HD ** -0.5, 0.75, ((0, 4),))
    ffn_gain = jnp.clip(1.0 + 0.18 * jax.random.normal(keys[13], (D,), jnp.float32), 0.1, 1.9)
    router_weight = noise(keys[14], (D, EXPERTS), D ** -0.5, 0.1875)
    expert_ids_keys = jax.random.split(jax.random.fold_in(keys[15], 1), REQS // R_DEV)
    expert_ids_turns = jax.random.permutation(jax.random.fold_in(keys[15], 3), REQS // R_DEV)
    expert_ids = jax.vmap(lambda own, number: assign_block(jax.random.fold_in(keys[15], 2), own, number, R_DEV, EXPERTS, TOP, CAP, 2))(expert_ids_keys, expert_ids_turns).reshape((REQS, TOP))
    w_gate = noise(keys[16], (EXPERTS, D, FF), D ** -0.5, 0.1875, ((0, 8), (2, 4)))
    w_up = noise(keys[17], (EXPERTS, D, FF), D ** -0.5, 0.1875, ((0, 8), (2, 4)))
    w_down = noise(keys[18], (EXPERTS, FF, D), FF ** -0.5, 0.109375, ((0, 8), (1, 4)))
    new_slot = draw_new_slot(jax.random.fold_in(keys[20], 71), 0)
    return {"hidden_in": hidden_in, "prompt_kv": prompt_kv, "tail_kv": tail_kv, "group_of": group_of, "prompt_len": prompt_len, "tail_len": tail_len, "bucket_of": bucket_of, "bias_table": bias_table, "attn_gain": attn_gain, "w_query": w_query, "w_key": w_key, "w_value": w_value, "w_out": w_out, "ffn_gain": ffn_gain, "router_weight": router_weight, "expert_ids": expert_ids, "w_gate": w_gate, "w_up": w_up, "w_down": w_down, "new_slot": new_slot}


EPS = 1e-06

def rms_scale(values, gain):
    v = values.astype(jnp.float32)
    return (v * lax.rsqrt(lax.optimization_barrier(jnp.mean(v * v, axis=-1, keepdims=True)) + EPS) * gain).astype(jnp.bfloat16)

def round_keep(values):
    return lax.optimization_barrier(values.astype(jnp.bfloat16)).astype(jnp.float32)

def reference(hidden_in, prompt_kv, tail_kv, group_of, prompt_len, tail_len, bucket_of, bias_table, attn_gain, w_query, w_key, w_value, w_out, ffn_gain, router_weight, expert_ids, w_gate, w_up, w_down, new_slot):
    dist_bias = bias_table[bucket_of]
    scale = HD ** (-0.5)

    def one_replica(index):
        start_req = (index * R_DEV).astype(jnp.int32)
        start_grp = (index * G_DEV).astype(jnp.int32)
        rows_in = lax.dynamic_slice_in_dim(hidden_in, start_req, R_DEV, 0)
        prompts = lax.dynamic_slice_in_dim(prompt_kv, start_grp, G_DEV, 1)
        tails = lax.dynamic_slice_in_dim(tail_kv, start_req, R_DEV, 1)
        groups = lax.dynamic_slice_in_dim(group_of, start_req, R_DEV, 0)
        plens = lax.dynamic_slice_in_dim(prompt_len, start_grp, G_DEV, 0)
        tlens = lax.dynamic_slice_in_dim(tail_len, start_req, R_DEV, 0)
        normed = rms_scale(rows_in, attn_gain)
        query = jnp.dot(normed, w_query, preferred_element_type=jnp.float32).astype(jnp.bfloat16)
        key_new = jnp.dot(normed, w_key, preferred_element_type=jnp.float32).astype(jnp.bfloat16)
        value_new = jnp.dot(normed, w_value, preferred_element_type=jnp.float32).astype(jnp.bfloat16)
        q = query.astype(jnp.float32).reshape(R_DEV, HEADS, HD)
        pk = prompts[0].astype(jnp.float32).reshape(G_DEV, PRE, HEADS, HD)
        pv = prompts[1].astype(jnp.float32).reshape(G_DEV, PRE, HEADS, HD)
        tk = tails[0].astype(jnp.float32).reshape(R_DEV, TAIL, HEADS, HD)
        tv = tails[1].astype(jnp.float32).reshape(R_DEV, TAIL, HEADS, HD)
        kn = key_new.astype(jnp.float32).reshape(R_DEV, HEADS, HD)
        vn = value_new.astype(jnp.float32).reshape(R_DEV, HEADS, HD)
        own_len = plens[groups]
        pos = own_len + tlens
        jpos = jnp.arange(PRE, dtype=jnp.int32)
        pidx = jnp.clip(pos[:, None] - jpos[None, :], 0, MAXDIST - 1)
        pbias = jnp.transpose(dist_bias[pidx], (2, 0, 1))
        pmask = (jnp.arange(G_DEV, dtype=jnp.int32)[None, :, None] == groups[:, None, None]) & (jpos[None, None, :] < own_len[:, None, None])
        ps = jnp.einsum('rhd,gjhd->hrgj', q, pk) * scale + pbias[:, :, None, :]
        ps = jnp.where(pmask[None], ps, -jnp.inf)
        tpos = jnp.arange(TAIL, dtype=jnp.int32)
        tidx = jnp.clip(tlens[:, None] - tpos[None, :], 0, MAXDIST - 1)
        tbias = jnp.transpose(dist_bias[tidx], (2, 0, 1))
        tmask = tpos[None, :] < tlens[:, None]
        ts = jnp.einsum('rhd,rthd->hrt', q, tk) * scale + tbias
        ts = jnp.where(tmask[None], ts, -jnp.inf)
        ns = jnp.einsum('rhd,rhd->hr', q, kn) * scale + dist_bias[0][:, None]
        top = jnp.maximum(jnp.maximum(lax.optimization_barrier(jnp.max(ps, axis=(2, 3))), lax.optimization_barrier(jnp.max(ts, axis=2))), ns)
        pe = jnp.exp(ps - top[:, :, None, None])
        te = jnp.exp(ts - top[:, :, None])
        ne = jnp.exp(ns - top)
        total = lax.optimization_barrier(jnp.sum(pe, axis=(2, 3))) + lax.optimization_barrier(jnp.sum(te, axis=2)) + ne
        pw = round_keep(pe / total[:, :, None, None])
        tw = round_keep(te / total[:, :, None])
        nw = round_keep(ne / total)
        head = jnp.einsum('hrgj,gjhd->rhd', pw, pv) + jnp.einsum('hrt,rthd->rhd', tw, tv) + jnp.einsum('hr,rhd->rhd', nw, vn)
        head_out = head.reshape(R_DEV, HEADS * HD).astype(jnp.bfloat16)
        attn = jnp.dot(head_out, w_out, preferred_element_type=jnp.float32)
        resid = (rows_in.astype(jnp.float32) + attn).astype(jnp.bfloat16)
        return (resid, key_new, value_new)
    resid, key_new, value_new = lax.map(one_replica, jnp.arange(N_REQ, dtype=jnp.int32))
    resid = resid.reshape(REQS, D)
    key_new = key_new.reshape(REQS, HEADS * HD)
    value_new = value_new.reshape(REQS, HEADS * HD)
    normed2 = rms_scale(resid, ffn_gain)
    logits = jnp.dot(normed2, router_weight, preferred_element_type=jnp.float32)
    picked = jnp.take_along_axis(logits, expert_ids, axis=1)
    gate_first = jax.nn.sigmoid(picked[:, 0] - picked[:, 1])
    flat_e = expert_ids.reshape(-1)
    onehot = (flat_e[:, None] == jnp.arange(EXPERTS, dtype=jnp.int32)[None, :]).astype(jnp.int32)
    per = onehot.reshape(N_REQ, R_DEV * TOP, EXPERTS)
    pos = lax.optimization_barrier(jnp.sum((jnp.cumsum(per, axis=1) - 1) * per, axis=2)).reshape(-1)
    pair = jnp.arange(REQS * TOP, dtype=jnp.int32)
    slot = pair // (R_DEV * TOP) * CAP + pos
    tok_table = jnp.zeros((EXPERTS, N_REQ * CAP), jnp.int32).at[flat_e, slot].set(pair // TOP)
    used = jnp.zeros((EXPERTS, N_REQ * CAP), jnp.int32).at[flat_e, slot].set(1)

    def one_expert(items):
        wg, wu, wd, tok, live = items
        rows = jnp.where(live[:, None] > 0, normed2[tok], jnp.zeros((), jnp.bfloat16))
        gate_h = jnp.dot(rows, wg, preferred_element_type=jnp.float32)
        up_h = jnp.dot(rows, wu, preferred_element_type=jnp.float32)
        act = (jax.nn.gelu(gate_h, approximate=True) * up_h).astype(jnp.bfloat16)
        return jnp.dot(act, wd, preferred_element_type=jnp.float32).astype(jnp.bfloat16)
    outputs = lax.map(one_expert, (w_gate, w_up, w_down, tok_table, used))
    pair_out = outputs[flat_e, slot].astype(jnp.float32).reshape(REQS, TOP, D)
    mixed = (resid.astype(jnp.float32) + gate_first[:, None] * pair_out[:, 0] + (1.0 - gate_first)[:, None] * pair_out[:, 1]).astype(jnp.bfloat16)
    everyone = jnp.arange(REQS, dtype=jnp.int32)
    tail_new = tail_kv.at[0, everyone, tail_len].set(key_new).at[1, everyone, tail_len].set(value_new)
    out_hidden = jnp.zeros_like(mixed).at[new_slot].set(mixed)
    new_tail_kv = jnp.zeros_like(tail_new).at[:, new_slot].set(tail_new)
    return (out_hidden, new_tail_kv)
```

```python
import functools
import jax
import jax.numpy as jnp
from jax import lax
from jax.experimental import pallas as pl
from jax.experimental.pallas import tpu as pltpu

HD = 64
EPS = 1e-06
F32 = jnp.float32
BF16 = jnp.bfloat16
NT = (((1,), (1,)), ((), ()))
LANES = 128
CHUNK = 16
TILE = 64


def attention_kernel(
    group_sm, plen_sm, tlen_sm, group_row, bucket_rev, bias_rows,
    hidden_hbm, gain_ref, wq_hbm, wk_hbm, wv_hbm, prompt_hbm, tail_hbm,
    head_ref, tail_out,
    hidden_v, wq_v, wk_v, wv_v, pk_v, pv_v, kbuf, vbuf,
    q_v, knew_v, vnew_v, table, bias_p, bias_t, s_t, o_v,
    w_sem, p_sem, in_sem, out_sem,
):
    rows = hidden_v.shape[0]
    groups, prompt_rows, cols = pv_v.shape
    tail_rows = kbuf.shape[1]
    heads = cols // HD
    per8 = 8 // heads
    width_t = per8 * tail_rows
    span_end = bias_p.shape[1] + tail_rows
    tile_rows = TILE * heads
    chunks = rows // CHUNK

    def weight_copies():
        return [
            pltpu.make_async_copy(hidden_hbm, hidden_v, w_sem.at[0]),
            pltpu.make_async_copy(wq_hbm, wq_v, w_sem.at[1]),
            pltpu.make_async_copy(wk_hbm, wk_v, w_sem.at[2]),
            pltpu.make_async_copy(wv_hbm, wv_v, w_sem.at[3]),
        ]

    def prompt_copies():
        return [
            pltpu.make_async_copy(
                prompt_hbm.at[0, g], pk_v.at[:, pl.ds(g * cols, cols)], p_sem.at[g]
            )
            for g in range(groups)
        ]

    def value_copy():
        return pltpu.make_async_copy(prompt_hbm.at[1], pv_v, p_sem.at[groups])

    def chunk_in(c):
        at = pl.ds(c * CHUNK, CHUNK)
        return [
            pltpu.make_async_copy(tail_hbm.at[0, at], kbuf.at[at], in_sem.at[0, c]),
            pltpu.make_async_copy(tail_hbm.at[1, at], vbuf.at[at], in_sem.at[1, c]),
        ]

    def chunk_out(c):
        at = pl.ds(c * CHUNK, CHUNK)
        return [
            pltpu.make_async_copy(kbuf.at[at], tail_out.at[0, at], out_sem.at[0, c]),
            pltpu.make_async_copy(vbuf.at[at], tail_out.at[1, at], out_sem.at[1, c]),
        ]

    for copy in weight_copies() + prompt_copies() + [value_copy()]:
        copy.start()
    for c in range(chunks):
        for copy in chunk_in(c):
            copy.start()

    buckets = bias_rows.shape[1]
    ids = bucket_rev[...]
    found = jnp.zeros(table.shape, F32)
    for k in range(buckets):
        found = jnp.where(ids == k, bias_rows[:, k : k + 1], found)
    table[...] = found

    for copy in weight_copies():
        copy.wait()
    v = hidden_v[...].astype(F32)
    normed = (
        v * lax.rsqrt(jnp.mean(v * v, axis=-1, keepdims=True) + EPS) * gain_ref[...]
    ).astype(BF16)
    query = jnp.dot(normed, wq_v[...], preferred_element_type=F32).astype(BF16)
    q_v[...] = query * jnp.asarray(HD ** (-0.5), BF16)
    knew_v[...] = jnp.dot(normed, wk_v[...], preferred_element_type=F32).astype(BF16).astype(F32)
    vnew_v[...] = jnp.dot(normed, wv_v[...], preferred_element_type=F32).astype(BF16).astype(F32)

    lane = lax.broadcasted_iota(jnp.int32, (8, LANES), 1)
    sub = lax.broadcasted_iota(jnp.int32, (8, LANES), 0)
    row16 = lax.broadcasted_iota(jnp.int32, (16, cols), 0)
    minus = jnp.float32(-jnp.inf)

    def build_bias(tile):
        def step(i, carry):
            base = tile * TILE + i * per8
            out_p = [jnp.full((8, LANES), minus) for _ in range(prompt_rows // LANES)]
            out_t = [jnp.full((8, LANES), minus) for _ in range(width_t // LANES)]
            for j in range(per8):
                r = base + j
                length = tlen_sm[r]
                plen = plen_sm[group_sm[r]]
                start = span_end - plen - length
                block = start // LANES
                off = start - block * LANES
                mine = (sub >= j * heads) & (sub < (j + 1) * heads)
                window = table[:, pl.ds(pl.multiple_of(block * LANES, LANES), prompt_rows + LANES)]
                turn = jnp.where(off == 0, 0, LANES - off)
                turned = [
                    pltpu.roll(window[:, k * LANES : (k + 1) * LANES], turn, 1)
                    for k in range(prompt_rows // LANES + 1)
                ]
                for k in range(prompt_rows // LANES):
                    here = jnp.where(lane < LANES - off, turned[k], turned[k + 1])
                    out_p[k] = jnp.where(mine & (lane + k * LANES < plen), here, out_p[k])
                place = j * tail_rows
                k = place // LANES
                place = place - k * LANES
                own = table[:, prompt_rows : prompt_rows + LANES]
                shift = place - (tail_rows - length)
                shift = jnp.where(shift < 0, shift + LANES, shift)
                own = pltpu.roll(own, shift, 1)
                live = mine & (lane >= place) & (lane <= place + length)
                out_t[k] = jnp.where(live, own, out_t[k])
            at = pl.ds(pl.multiple_of(i * 8, 8), 8)
            for k in range(prompt_rows // LANES):
                bias_p[at, k * LANES : (k + 1) * LANES] = out_p[k]
            for k in range(width_t // LANES):
                bias_t[at, k * LANES : (k + 1) * LANES] = out_t[k]
            return carry

        lax.fori_loop(0, TILE // per8, step, 0, unroll=4)

    def insert(c):
        def step(i, carry):
            r = c * CHUNK + i
            length = tlen_sm[r]
            first = pl.multiple_of(length // 16 * 16, 16)
            hit = row16 == length - first
            for new, buf in ((knew_v, kbuf), (vnew_v, vbuf)):
                fresh = jnp.broadcast_to(new[pl.ds(r, 1), :], (16, cols))
                old = buf[r, pl.ds(first, 16), :].astype(F32)
                buf[r, pl.ds(first, 16), :] = jnp.where(hit, fresh, old).astype(BF16)
            return carry

        lax.fori_loop(0, CHUNK, step, 0, unroll=4)

    rr = lax.broadcasted_iota(jnp.int32, (tile_rows, rows), 0) // heads
    rc = lax.broadcasted_iota(jnp.int32, (tile_rows, rows), 1)
    hrow = lax.broadcasted_iota(jnp.int32, (tile_rows, cols), 0) % heads
    hcol = lax.broadcasted_iota(jnp.int32, (tile_rows, cols), 1) // HD
    own_head = hrow == hcol
    group_hot = (
        lax.broadcasted_iota(jnp.int32, (groups, rows), 0) == group_row[...]
    ).astype(BF16)
    first_head = lax.broadcasted_iota(jnp.int32, (TILE, LANES), 1) < HD
    per16 = 16 // heads

    def do_tile(tile, carry):
        build_bias(tile)
        spread = (rr + tile * TILE == rc).astype(BF16)
        member = lax.dot_general(
            spread, group_hot, NT, preferred_element_type=F32
        )
        qrep = jnp.dot(spread, q_v[...], preferred_element_type=F32)
        qbd = jnp.where(own_head, qrep, 0.0).astype(BF16)

        @pl.when(tile == 0)
        def _():
            for copy in prompt_copies():
                copy.wait()

        spread_q = jnp.concatenate(
            [jnp.where(member[:, g : g + 1] > 0.5, qbd, jnp.zeros_like(qbd)) for g in range(groups)],
            axis=1,
        )
        s_p = (
            lax.dot_general(spread_q, pk_v[...], NT, preferred_element_type=F32) + bias_p[...]
        )
        for n in range(TILE // CHUNK):
            c = tile * (TILE // CHUNK) + n
            for copy in chunk_in(c):
                copy.wait()
            insert(c)
            for copy in chunk_out(c):
                copy.start()
            for i in range(CHUNK // per16):
                at = n * CHUNK * heads + i * 16
                keys = kbuf[pl.ds(c * CHUNK + i * per16, per16)].reshape(per16 * tail_rows, cols)
                got = lax.dot_general(qbd[at : at + 16], keys, NT, preferred_element_type=F32)
                s_t[at : at + 8, :] = got[:8, :width_t]
                s_t[at + 8 : at + 16, :] = got[8:, width_t:]
        tail_s = s_t[...] + bias_t[...]
        top = jnp.maximum(
            jnp.max(s_p, axis=1, keepdims=True), jnp.max(tail_s, axis=1, keepdims=True)
        )
        pe = jnp.exp(s_p - top)
        te = jnp.exp(tail_s - top)
        total = jnp.sum(pe, axis=1, keepdims=True) + jnp.sum(te, axis=1, keepdims=True)
        part = 1.0 / total
        pw = (pe * part).astype(BF16)
        tw = te * part

        @pl.when(tile == 0)
        def _():
            value_copy().wait()

        spread_p = jnp.concatenate(
            [jnp.where(member[:, g : g + 1] > 0.5, pw, jnp.zeros_like(pw)) for g in range(groups)],
            axis=1,
        )
        o_p = jnp.dot(
            spread_p, pv_v[...].reshape(groups * prompt_rows, cols), preferred_element_type=F32
        )
        none = jnp.zeros((8, width_t), F32)
        for i in range(TILE // per16):
            at = i * 16
            upper = jnp.concatenate([tw[at : at + 8], none], axis=1)
            lower = jnp.concatenate([none, tw[at + 8 : at + 16]], axis=1)
            both = jnp.concatenate([upper, lower], axis=0).astype(BF16)
            vals = vbuf[pl.ds(tile * TILE + i * per16, per16)].reshape(per16 * tail_rows, cols)
            o_t = jnp.dot(both, vals, preferred_element_type=F32) + o_p[at : at + 16]
            for b in range(cols // LANES):
                o_v[b, at : at + 16, :] = o_t[:, b * LANES : (b + 1) * LANES]
        for b in range(cols // LANES):
            low = o_v[b, pl.ds(2 * b, TILE, stride=heads), :]
            high = o_v[b, pl.ds(2 * b + 1, TILE, stride=heads), :]
            head_ref[
                pl.ds(pl.multiple_of(tile * TILE, TILE), TILE), b * LANES : (b + 1) * LANES
            ] = jnp.where(first_head, low, high).astype(BF16)
        return carry

    lax.fori_loop(0, rows // TILE, do_tile, 0)
    for c in range(chunks):
        for copy in chunk_out(c):
            copy.wait()


def attention(
    hidden_in, prompt_kv, tail_kv, group_of, prompt_len, tail_len, bucket_of, bias_table,
    attn_gain, w_query, w_key, w_value,
):
    rows, width = hidden_in.shape
    cols = w_query.shape[1]
    heads = cols // HD
    groups, prompt_rows = prompt_kv.shape[1:3]
    tail_rows = tail_kv.shape[2]
    span = bucket_of.shape[0]
    table_width = 2 * prompt_rows + LANES
    bucket_rev = jnp.pad(bucket_of[::-1], (0, table_width - span))[None, :]
    bias_rows = jnp.tile(bias_table.T, (8 // heads, 1))
    per8 = 8 // heads
    tile_rows = TILE * heads
    vm = pl.BlockSpec(memory_space=pltpu.VMEM)
    sm = pl.BlockSpec(memory_space=pltpu.SMEM)
    hbm = pl.BlockSpec(memory_space=pl.ANY)
    chunks = rows // CHUNK
    return pl.pallas_call(
        attention_kernel,
        out_shape=(
            jax.ShapeDtypeStruct((rows, cols), BF16),
            jax.ShapeDtypeStruct(tail_kv.shape, BF16),
        ),
        in_specs=[sm, sm, sm, vm, vm, vm, hbm, vm, hbm, hbm, hbm, hbm, hbm],
        out_specs=(vm, hbm),
        scratch_shapes=[
            pltpu.VMEM((rows, width), BF16),
            pltpu.VMEM((width, cols), BF16),
            pltpu.VMEM((width, cols), BF16),
            pltpu.VMEM((width, cols), BF16),
            pltpu.VMEM((prompt_rows, groups * cols), BF16),
            pltpu.VMEM((groups, prompt_rows, cols), BF16),
            pltpu.VMEM((rows, tail_rows, cols), BF16),
            pltpu.VMEM((rows, tail_rows, cols), BF16),
            pltpu.VMEM((rows, cols), BF16),
            pltpu.VMEM((rows, cols), F32),
            pltpu.VMEM((rows, cols), F32),
            pltpu.VMEM((8, table_width), F32),
            pltpu.VMEM((tile_rows, prompt_rows), F32),
            pltpu.VMEM((tile_rows, per8 * tail_rows), F32),
            pltpu.VMEM((tile_rows, per8 * tail_rows), F32),
            pltpu.VMEM((cols // LANES, tile_rows, LANES), F32),
            pltpu.SemaphoreType.DMA((4,)),
            pltpu.SemaphoreType.DMA((groups + 1,)),
            pltpu.SemaphoreType.DMA((2, chunks)),
            pltpu.SemaphoreType.DMA((2, chunks)),
        ],
        compiler_params=pltpu.CompilerParams(vmem_limit_bytes=48 * 1024 * 1024),
        cost_estimate=pl.CostEstimate(flops=8_000_000_000, bytes_accessed=45_000_000, transcendentals=700_000),
        name="attention",
    )(
        group_of, prompt_len, tail_len, group_of[None, :], bucket_rev, bias_rows,
        hidden_in, attn_gain[None, :], w_query, w_key, w_value, prompt_kv, tail_kv,
    )
TOP = 2
MIG = 4
EXTRA = 16
TN = (((0,), (0,)), ((), ()))


def iota(shape, dim):
    return lax.broadcasted_iota(jnp.int32, shape, dim)


def block_rows(cap):
    return cap + EXTRA


def plan_kernel(cap, slots_ref, ids_ref, place_ref, wide_ref, kron_ref, plan_ref, slot_s):
    replicas, rows = slots_ref.shape
    experts = slot_s.shape[0]
    size = place_ref.shape[0] // replicas
    me = lax.axis_index("req")
    ns = slots_ref[...]
    at_sub = iota((replicas, rows), 0)
    at_lane = iota((replicas, rows), 1)
    moved = ns != at_sub * rows + at_lane
    tri = (iota((rows, rows), 0) < iota((rows, rows), 1)).astype(BF16)
    rank = jnp.dot(moved.astype(F32).astype(BF16), tri, preferred_element_type=F32).astype(jnp.int32)
    going_to = ns // rows
    mine = at_sub == me

    def own(values):
        return jnp.sum(jnp.where(mine, values, 0), axis=0, keepdims=True)

    moved_me = own(moved.astype(jnp.int32))
    rank_me = own(rank)
    to_me = own(going_to)
    ids = ids_ref[...]
    pick = (iota((8, TOP), 0) == iota((8, TOP), 1)).astype(BF16)
    ids_rows = lax.dot_general(
        pick, ids.astype(F32).astype(BF16), NT, preferred_element_type=F32
    ).astype(jnp.int32)
    at_e = iota((experts, rows), 0)
    hit = (ids_rows[0:1] == at_e) | (ids_rows[1:2] == at_e)
    normal = (hit & (moved_me == 0)).astype(F32).astype(BF16)
    slot = jnp.dot(normal, tri, preferred_element_type=F32).astype(jnp.int32)
    slot_s[...] = jnp.where(hit, jnp.where(moved_me > 0, cap + rank_me, slot), -1)
    at_row = iota((size, rows), 0)
    for k in range(replicas):
        e = me ^ k
        block = pl.ds(k * size, size)
        row = slot_s[pl.ds(e, 1), :]
        leaving = jnp.where((moved_me > 0) & (to_me == e), cap + rank_me, -100)
        place_ref[block, 0:rows] = (at_row == row).astype(F32).astype(BF16)
        place_ref[block, rows : 2 * rows] = (at_row == leaving + MIG).astype(F32).astype(BF16)
        place_ref[block, 2 * rows :] = (at_row == leaving + 2 * MIG).astype(F32).astype(BF16)
    lane = iota(wide_ref.shape, 1)
    idf = ids.astype(F32)
    wide_ref[...] = jnp.where(
        lane == 0, idf[:, 0:1], jnp.where(lane == 1, idf[:, 1:2], 0.0)
    ).astype(BF16)
    dest = jnp.max(jnp.where(moved, going_to, -1), axis=1, keepdims=True)
    dest = jnp.where(dest < 0, iota((replicas, 1), 0), dest)
    hot = (dest == iota((replicas, replicas), 1)).astype(F32).astype(BF16)
    span = replicas * EXTRA
    mixed_row = (iota((span, replicas), 0) // EXTRA) ^ me
    a = (mixed_row == iota((span, replicas), 1)).astype(F32).astype(BF16)
    by_source = lax.dot_general(a, hot, NT, preferred_element_type=F32).astype(BF16)
    pairs = lax.dot_general(by_source, a, NT, preferred_element_type=F32)
    same = iota((span, span), 0) % EXTRA == iota((span, span), 1) % EXTRA
    kron_ref[...] = jnp.where(same, pairs, 0.0).astype(BF16)
    sub1 = iota((replicas, 1), 0)

    def source_of(who):
        return jnp.sum(jnp.where(dest == who, sub1, 0), axis=0, keepdims=True)

    bits = replicas.bit_length() - 1

    def held(diff):
        found = jnp.zeros_like(diff)
        for i in range(bits - 1):
            found = found + (((diff >> (bits - 1 - i)) & 1) << i)
        return found

    diff = source_of(me) ^ me
    final = jnp.where((diff & 1) == 1, 1 << (bits - 1), held(diff))
    send = held(source_of(me ^ 1) ^ (me ^ 1))
    lane8 = iota((8, LANES), 1)
    plan = jnp.where(lane8 == 0, final, jnp.where(lane8 == 1, send, -1))
    lane1 = iota((1, rows), 1)
    for m in range(MIG):
        is_m = (moved_me > 0) & (rank_me == m)
        mover = jnp.sum(jnp.where(is_m, lane1, 0), axis=1, keepdims=True)
        plan = jnp.where(lane8 == 8 + m, mover, plan)
        come = moved & (going_to == me) & (rank == m)
        to = jnp.sum(jnp.where(come, ns - me * rows + 1, 0), axis=1, keepdims=True)
        to = jnp.sum(to, axis=0, keepdims=True) - 1
        plan = jnp.where(lane8 == 16 + m, to, plan)
    plan_ref[...] = plan


def make_plan(slots, expert_ids, experts, cap, half):
    replicas, rows = slots.shape
    size = block_rows(cap)
    vm = pl.BlockSpec(memory_space=pltpu.VMEM)
    span = replicas * EXTRA
    return pl.pallas_call(
        functools.partial(plan_kernel, cap),
        out_shape=(
            jax.ShapeDtypeStruct((replicas * size, 3 * rows), BF16),
            jax.ShapeDtypeStruct((rows, half), BF16),
            jax.ShapeDtypeStruct((span, span), BF16),
            jax.ShapeDtypeStruct((8, LANES), jnp.int32),
        ),
        in_specs=[vm, vm],
        out_specs=(vm, vm, vm, vm),
        scratch_shapes=[pltpu.VMEM((experts, rows), jnp.int32)],
        cost_estimate=pl.CostEstimate(flops=20_000_000, bytes_accessed=4_000_000, transcendentals=0),
        name="plan",
    )(slots, expert_ids)


def norm(values, gain):
    v = values.astype(F32)
    return (v * lax.rsqrt(jnp.mean(v * v, axis=-1, keepdims=True) + EPS) * gain).astype(BF16)


def dispatch_kernel(pieces, replicas, *refs):
    heads_hbm = refs[:pieces]
    wout_hbm = refs[pieces : 2 * pieces]
    hidden_ref, gain_ref, place_ref, wide_ref = refs[2 * pieces : 2 * pieces + 4]
    refs = refs[2 * pieces + 4 :]
    resid_ref = refs[0]
    outs = refs[1 : 1 + replicas]
    head_v, wout_v, stack, sem = refs[1 + replicas :]
    tp = lax.axis_index("tp")
    core = tp & 1
    rows, width = hidden_ref.shape
    cols = width // pieces
    half = width // 2

    def copies():
        made = []
        for k in range(pieces):
            at = pl.ds(pl.multiple_of((tp ^ k) * cols, cols), cols)
            made.append(pltpu.make_async_copy(wout_hbm[k], wout_v.at[at], sem.at[0, k]))
            made.append(pltpu.make_async_copy(heads_hbm[k], head_v.at[:, at], sem.at[1, k]))
        return made

    for copy in copies():
        copy.start()
    for copy in copies():
        copy.wait()
    attn = jnp.dot(head_v[...], wout_v[...], preferred_element_type=F32)
    resid = (hidden_ref[...].astype(F32) + attn).astype(BF16)
    resid_ref[...] = resid
    normed = norm(resid, gain_ref[...])
    first = core == 0
    stack[0:rows, :] = jnp.where(first, normed[:, :half], normed[:, half:])
    stack[rows : 2 * rows, :] = jnp.where(first, resid[:, :half], resid[:, half:])
    stack[2 * rows :, :] = wide_ref[...]
    size = place_ref.shape[0] // replicas
    for k in range(replicas):
        outs[k][...] = jnp.dot(
            place_ref[k * size : (k + 1) * size], stack[...], preferred_element_type=F32
        ).astype(BF16)


def dispatch(heads, wouts, hidden, gain, place, wide, replicas):
    rows, width = hidden.shape
    pieces = len(heads)
    half = width // 2
    size = place.shape[0] // replicas
    vm = pl.BlockSpec(memory_space=pltpu.VMEM)
    hbm = pl.BlockSpec(memory_space=pl.ANY)
    return pl.pallas_call(
        functools.partial(dispatch_kernel, pieces, replicas),
        out_shape=(jax.ShapeDtypeStruct((rows, width), BF16),)
        + tuple(jax.ShapeDtypeStruct((size, half), BF16) for _ in range(replicas)),
        in_specs=[hbm] * (2 * pieces) + [vm] * 4,
        out_specs=(vm,) * (1 + replicas),
        scratch_shapes=[
            pltpu.VMEM((rows, width), BF16),
            pltpu.VMEM((width, width), BF16),
            pltpu.VMEM((3 * rows, half), BF16),
            pltpu.SemaphoreType.DMA((2, pieces)),
        ],
        compiler_params=pltpu.CompilerParams(vmem_limit_bytes=32 * 1024 * 1024),
        cost_estimate=pl.CostEstimate(flops=1_200_000_000, bytes_accessed=6_000_000, transcendentals=0),
        name="dispatch",
    )(*heads, *wouts, hidden, gain[None, :], place, wide)


def expert_kernel(replicas, *refs):
    own = refs[:replicas]
    pair = refs[replicas : 2 * replicas]
    wg_hbm, wu_hbm, wd_hbm, keep_ref, give_ref, x_own, x_pair, wg, wu, wd, sem, xsem = refs[2 * replicas :]
    core = lax.axis_index("tp") & 1
    size, half = own[0].shape

    def weight_copies():
        return [
            pltpu.make_async_copy(wg_hbm.at[0], wg, sem.at[0]),
            pltpu.make_async_copy(wu_hbm.at[0], wu, sem.at[1]),
            pltpu.make_async_copy(wd_hbm.at[0], wd, sem.at[2]),
        ]

    def block_copies():
        made = []
        for k in range(replicas):
            at = pl.ds(k * size, size)
            made.append(pltpu.make_async_copy(own[k], x_own.at[at], xsem.at[0, k]))
            made.append(pltpu.make_async_copy(pair[k], x_pair.at[at], xsem.at[1, k]))
        return made

    for copy in weight_copies() + block_copies():
        copy.start()
    for copy in block_copies() + weight_copies():
        copy.wait()
    here = pl.ds(pl.multiple_of(core * half, half), half)
    there = pl.ds(pl.multiple_of((1 - core) * half, half), half)
    total = replicas * size
    step = 256 if total % 256 == 0 else size

    def tile(i, carry):
        at = pl.ds(pl.multiple_of(i * step, step), step)
        a, b = x_own[at, :], x_pair[at, :]
        gate = jnp.dot(a, wg[here, :], preferred_element_type=F32) + jnp.dot(
            b, wg[there, :], preferred_element_type=F32
        )
        up = jnp.dot(a, wu[here, :], preferred_element_type=F32) + jnp.dot(
            b, wu[there, :], preferred_element_type=F32
        )
        act = (jax.nn.gelu(gate, approximate=True) * up).astype(BF16)
        give_ref[at, :] = jnp.dot(act, wd[:, there], preferred_element_type=F32).astype(BF16)
        keep_ref[at, :] = jnp.dot(act, wd[:, here], preferred_element_type=F32).astype(BF16)
        return carry

    lax.fori_loop(0, total // step, tile, 0)


def expert(own, pair, w_gate, w_up, w_down):
    replicas = len(own)
    size, half = own[0].shape
    _, width, hidden = w_gate.shape
    total = replicas * size
    vm = pl.BlockSpec(memory_space=pltpu.VMEM)
    hbm = pl.BlockSpec(memory_space=pl.ANY)
    shape = jax.ShapeDtypeStruct((total, half), BF16)
    return pl.pallas_call(
        functools.partial(expert_kernel, replicas),
        out_shape=(shape, shape),
        in_specs=[hbm] * (2 * replicas + 3),
        out_specs=(vm, vm),
        scratch_shapes=[
            pltpu.VMEM((total, half), BF16),
            pltpu.VMEM((total, half), BF16),
            pltpu.VMEM((width, hidden), BF16),
            pltpu.VMEM((width, hidden), BF16),
            pltpu.VMEM((hidden, width), BF16),
            pltpu.SemaphoreType.DMA((3,)),
            pltpu.SemaphoreType.DMA((2, replicas)),
        ],
        compiler_params=pltpu.CompilerParams(vmem_limit_bytes=32 * 1024 * 1024),
        cost_estimate=pl.CostEstimate(flops=3_400_000_000, bytes_accessed=8_000_000, transcendentals=600_000),
        name="expert",
    )(*own, *pair, w_gate, w_up, w_down)


def give_back_kernel(cap, keep_ref, got_ref, kron_ref, *refs):
    replicas = len(refs) - 1
    outs, rows_v = refs[:replicas], refs[replicas]
    size = outs[0].shape[0]
    for k in range(replicas):
        at = slice(k * size, (k + 1) * size)
        both = keep_ref[at, :].astype(F32) + got_ref[at, :].astype(F32)
        outs[k][...] = both.astype(BF16)
        rows_v[k * EXTRA : (k + 1) * EXTRA, :] = both[size - EXTRA :].astype(BF16)
    moved = jnp.dot(kron_ref[...], rows_v[...], preferred_element_type=F32)
    first = iota((EXTRA, 1), 0) >= cap - (size - EXTRA)
    for k in range(replicas):
        at = slice(k * EXTRA, (k + 1) * EXTRA)
        outs[k][size - EXTRA :, :] = jnp.where(
            first, moved[at], rows_v[at, :].astype(F32)
        ).astype(BF16)


def give_back(keep, got, kron, cap, replicas):
    total, half = keep.shape
    size = total // replicas
    vm = pl.BlockSpec(memory_space=pltpu.VMEM)
    return pl.pallas_call(
        functools.partial(give_back_kernel, cap),
        out_shape=tuple(jax.ShapeDtypeStruct((size, half), BF16) for _ in range(replicas)),
        in_specs=[vm] * 3,
        out_specs=(vm,) * replicas,
        scratch_shapes=[pltpu.VMEM((replicas * EXTRA, half), BF16)],
        compiler_params=pltpu.CompilerParams(vmem_limit_bytes=32 * 1024 * 1024),
        cost_estimate=pl.CostEstimate(flops=30_000_000, bytes_accessed=2_500_000, transcendentals=0),
        name="give_back",
    )(keep, got, kron)


def gates_kernel(cap, replicas, *refs):
    own = refs[:replicas]
    pair = refs[replicas : 2 * replicas]
    (resid_ref, slots_ref, ids_ref, gain_ref, router_ref, first_ref, second_ref, gate_ref, new_ref) = refs[
        2 * replicas :
    ]
    me = lax.axis_index("req")
    core = lax.axis_index("tp") & 1
    rows, width = resid_ref.shape
    half = width // 2
    size = own[0].shape[0]
    low = size - EXTRA
    skip = cap - low
    ns = slots_ref[...]
    count = ns.shape[0]
    at_sub = iota((count, rows), 0)
    moved = ns != at_sub * rows + iota((count, rows), 1)
    before = (iota((rows, rows), 0) < iota((rows, rows), 1)).astype(BF16)
    movedf = moved.astype(F32)
    rank = jnp.dot(movedf.astype(BF16), before, preferred_element_type=F32)
    coming = moved & (ns // rows == me)
    slot_to = jnp.sum(jnp.where(coming, ns - me * rows + 1, 0), axis=0, keepdims=True) - 1
    rank_in = jnp.sum(jnp.where(coming, rank, 0.0), axis=0, keepdims=True).astype(jnp.int32)
    landing = (iota((rows, rows), 0) == slot_to).astype(F32).astype(BF16)
    at16 = iota((EXTRA, rows), 0)

    def taken(offset):
        hot = (at16 == rank_in + (skip + offset)) & (slot_to >= 0)
        return lax.dot_general(landing, hot.astype(F32).astype(BF16), NT, preferred_element_type=F32)

    take_resid = taken(MIG)
    take_ids = taken(2 * MIG)
    vacated = jnp.sum(take_resid, axis=1, keepdims=True) > 0.5
    in_own = own[0][low:, :].astype(F32)
    in_pair = pair[0][low:, :].astype(F32)
    for k in range(1, replicas):
        in_own = in_own + own[k][low:, :].astype(F32)
        in_pair = in_pair + pair[k][low:, :].astype(F32)
    in_own, in_pair = in_own.astype(BF16), in_pair.astype(BF16)
    first_core = core == 0
    in_low = jnp.where(first_core, in_own, in_pair)
    in_high = jnp.where(first_core, in_pair, in_own)
    picked = take_resid.astype(BF16)
    resid = resid_ref[...]
    new_low = jnp.where(
        vacated, jnp.dot(picked, in_low, preferred_element_type=F32), resid[:, :half].astype(F32)
    ).astype(BF16)
    new_high = jnp.where(
        vacated, jnp.dot(picked, in_high, preferred_element_type=F32), resid[:, half:].astype(F32)
    ).astype(BF16)
    new_ref[...] = jnp.where(first_core, new_low, new_high)
    normed = norm(jnp.concatenate([new_low, new_high], axis=1), gain_ref[...])
    logits = jnp.dot(normed, router_ref[...], preferred_element_type=F32)
    experts = logits.shape[1]
    ids_in = jnp.dot(take_ids.astype(BF16), in_low[:, :LANES], preferred_element_type=F32)
    ids = ids_ref[...].astype(F32)
    id1 = jnp.where(vacated, ids_in[:, 0:1], ids[:, 0:1]).astype(jnp.int32)
    id2 = jnp.where(vacated, ids_in[:, 1:2], ids[:, 1:2]).astype(jnp.int32)
    at_e = iota((rows, experts), 1)
    hit1, hit2 = id1 == at_e, id2 == at_e
    picked1 = jnp.sum(jnp.where(hit1, logits, 0.0), axis=1, keepdims=True)
    picked2 = jnp.sum(jnp.where(hit2, logits, 0.0), axis=1, keepdims=True)
    gate = jax.nn.sigmoid(picked1 - picked2)
    gate_ref[...] = jnp.broadcast_to(gate, gate_ref.shape)
    mine = at_sub == me
    moved_me = jnp.sum(jnp.where(mine, movedf, 0.0), axis=0, keepdims=True)
    eye = (iota((rows, rows), 0) == iota((rows, rows), 1)).astype(BF16)
    moved_col = lax.dot_general(
        eye, jnp.broadcast_to(moved_me, (8, rows)).astype(BF16), NT, preferred_element_type=F32
    )[:, 0:1]
    old1 = ids_ref[:, 0:1] == at_e
    old2 = ids_ref[:, 1:2] == at_e
    normal = ((old1 | old2) & (moved_col < 0.5)).astype(F32).astype(BF16)
    after = (iota((rows, rows), 0) > iota((rows, rows), 1)).astype(BF16)
    slot = jnp.dot(after, normal, preferred_element_type=F32)
    slot1 = jnp.sum(jnp.where(hit1, slot, 0.0), axis=1, keepdims=True)
    slot2 = jnp.sum(jnp.where(hit2, slot, 0.0), axis=1, keepdims=True)
    in_rank = jnp.sum(
        jnp.where(take_resid > 0.5, iota((rows, EXTRA), 1), 0), axis=1, keepdims=True
    ) - (skip + MIG)
    slot1 = jnp.where(vacated, cap + in_rank, slot1.astype(jnp.int32))
    slot2 = jnp.where(vacated, cap + in_rank, slot2.astype(jnp.int32))
    lane = iota((rows, replicas * size), 1)
    first_ref[...] = (lane == (id1 ^ me) * size + slot1).astype(F32).astype(BF16)
    second_ref[...] = (lane == (id2 ^ me) * size + slot2).astype(F32).astype(BF16)


def make_gates(own, pair, resid, slots, ids, gain, router, cap):
    replicas = len(own)
    size, half = own[0].shape
    rows, width = resid.shape
    vm = pl.BlockSpec(memory_space=pltpu.VMEM)
    hot = jax.ShapeDtypeStruct((rows, replicas * size), BF16)
    return pl.pallas_call(
        functools.partial(gates_kernel, cap, replicas),
        out_shape=(
            hot,
            hot,
            jax.ShapeDtypeStruct((rows, LANES), F32),
            jax.ShapeDtypeStruct((rows, half), BF16),
        ),
        in_specs=[vm] * (2 * replicas + 5),
        out_specs=(vm,) * 4,
        compiler_params=pltpu.CompilerParams(vmem_limit_bytes=32 * 1024 * 1024),
        cost_estimate=pl.CostEstimate(flops=200_000_000, bytes_accessed=6_000_000, transcendentals=0),
        name="gates",
    )(*own, *pair, resid, slots, ids, gain[None, :], router)


def combine_kernel(replicas, *refs):
    blocks = refs[:replicas]
    first_ref, second_ref, gate_ref, out_ref, all_v = refs[replicas:]
    size = blocks[0].shape[0]
    for k in range(replicas):
        all_v[k * size : (k + 1) * size, :] = blocks[k][...]
    gate = gate_ref[:, 0:1]
    one = jnp.dot(first_ref[...], all_v[...], preferred_element_type=F32)
    two = jnp.dot(second_ref[...], all_v[...], preferred_element_type=F32)
    out_ref[...] = (gate * one + (1.0 - gate) * two).astype(BF16)


def combine(blocks, first, second, gate):
    replicas = len(blocks)
    size, half = blocks[0].shape
    rows = first.shape[0]
    vm = pl.BlockSpec(memory_space=pltpu.VMEM)
    return pl.pallas_call(
        functools.partial(combine_kernel, replicas),
        out_shape=jax.ShapeDtypeStruct((rows, half), BF16),
        in_specs=[vm] * (replicas + 3),
        out_specs=vm,
        scratch_shapes=[pltpu.VMEM((replicas * size, half), BF16)],
        compiler_params=pltpu.CompilerParams(vmem_limit_bytes=32 * 1024 * 1024),
        cost_estimate=pl.CostEstimate(flops=400_000_000, bytes_accessed=2_500_000, transcendentals=0),
        name="combine",
    )(*blocks, first, second, gate)


def pack_kernel(plan_ref, tail_hbm, out_hbm, sem):
    tail_rows = tail_hbm.shape[2]

    def copies():
        made = []
        for m in range(MIG):
            r = jnp.maximum(plan_ref[0, 8 + m], 0)
            for side in range(2):
                made.append(
                    pltpu.make_async_copy(
                        tail_hbm.at[side, r], out_hbm.at[2 * m + side], sem.at[2 * m + side]
                    )
                )
        return made

    for copy in copies():
        copy.start()
    for copy in copies():
        copy.wait()


def pack(plan, tail_new):
    _, _, tail_rows, cols = tail_new.shape
    hbm = pl.BlockSpec(memory_space=pl.ANY)
    return pl.pallas_call(
        pack_kernel,
        out_shape=jax.ShapeDtypeStruct((2 * MIG, tail_rows, cols), BF16),
        in_specs=[pl.BlockSpec(memory_space=pltpu.SMEM), hbm],
        out_specs=hbm,
        scratch_shapes=[pltpu.SemaphoreType.DMA((2 * MIG,))],
        cost_estimate=pl.CostEstimate(flops=0, bytes_accessed=500_000, transcendentals=0),
        name="pack",
    )(plan, tail_new)


def choose_kernel(plan_ref, *refs):
    choices = refs[:-2]
    out_hbm, sem = refs[-2:]
    index = plan_ref[0, 1]
    for i, choice in enumerate(choices):
        @pl.when(index == i)
        def _():
            copy = pltpu.make_async_copy(choice, out_hbm, sem)
            copy.start()
            copy.wait()


def choose(plan, held):
    hbm = pl.BlockSpec(memory_space=pl.ANY)
    return pl.pallas_call(
        choose_kernel,
        out_shape=jax.ShapeDtypeStruct(held[0].shape, BF16),
        in_specs=[pl.BlockSpec(memory_space=pltpu.SMEM)] + [hbm] * len(held),
        out_specs=hbm,
        scratch_shapes=[pltpu.SemaphoreType.DMA],
        cost_estimate=pl.CostEstimate(flops=0, bytes_accessed=500_000, transcendentals=0),
        name="choose",
    )(plan, *held)


def patch_kernel(plan_ref, *refs):
    choices = refs[:-3]
    out_hbm, sem = refs[-2:]
    index = plan_ref[0, 0]
    for i, choice in enumerate(choices):
        @pl.when(index == i)
        def _():
            for m in range(MIG):
                to = plan_ref[0, 16 + m]

                @pl.when(to >= 0)
                def _():
                    made = [
                        pltpu.make_async_copy(
                            choice.at[2 * m + side], out_hbm.at[side, to], sem.at[side]
                        )
                        for side in range(2)
                    ]
                    for copy in made:
                        copy.start()
                    for copy in made:
                        copy.wait()


def patch(plan, held, tail_new):
    hbm = pl.BlockSpec(memory_space=pl.ANY)
    return pl.pallas_call(
        patch_kernel,
        out_shape=jax.ShapeDtypeStruct(tail_new.shape, BF16),
        in_specs=[pl.BlockSpec(memory_space=pltpu.SMEM)] + [hbm] * (len(held) + 1),
        out_specs=hbm,
        scratch_shapes=[pltpu.SemaphoreType.DMA((2,))],
        input_output_aliases={len(held) + 1: 0},
        cost_estimate=pl.CostEstimate(flops=0, bytes_accessed=500_000, transcendentals=0),
        name="patch",
    )(plan, *held, tail_new)


def body(
    hidden_in, prompt_kv, tail_kv, group_of, prompt_len, tail_len, bucket_of, bias_table,
    attn_gain, w_query, w_key, w_value, w_out, ffn_gain, router_weight, expert_ids,
    w_gate, w_up, w_down, new_slot,
):
    rows, width = hidden_in.shape
    replicas = lax.axis_size("req")
    pieces = lax.axis_size("tp")
    experts = router_weight.shape[1]
    cap = -(-(5 * rows * TOP // (4 * experts)) // 16) * 16
    half = width // 2

    def across(axis, size, k):
        return lambda v: lax.ppermute(v, axis, [(i, i ^ k) for i in range(size)])

    def over_req(k):
        return across("req", replicas, k)

    def over_tp(k):
        return across("tp", pieces, k)

    wouts = [w_out] + [over_tp(k)(w_out) for k in range(1, pieces)]
    head_out, tail_new = attention(
        hidden_in, prompt_kv, tail_kv, group_of, prompt_len, tail_len, bucket_of, bias_table,
        attn_gain, w_query, w_key, w_value,
    )
    heads = [head_out] + [over_tp(k)(head_out) for k in range(1, pieces)]
    slots = new_slot.reshape(replicas, rows)
    place, wide, kron, plan = make_plan(slots, expert_ids, experts, cap, half)
    held = [pack(plan, tail_new)]
    bits = replicas.bit_length() - 1
    for i in range(bits - 1):
        held = held + [over_req(1 << (bits - 1 - i))(p) for p in held]
    held.append(over_req(1)(choose(plan, held)))
    new_tail_kv = patch(plan, held, tail_new)

    resid, *blocks = dispatch(heads, wouts, hidden_in, ffn_gain, place, wide, replicas)
    own = [blocks[0]] + [over_req(k)(blocks[k]) for k in range(1, replicas)]
    pair = [over_tp(1)(b) for b in own]
    keep, give = expert(own, pair, w_gate, w_up, w_down)
    back = give_back(keep, over_tp(1)(give), kron, cap, replicas)
    first, second, gate, resid_new = make_gates(
        own, pair, resid, slots, expert_ids, ffn_gain, router_weight, cap
    )
    result = [back[0]] + [over_req(k)(back[k]) for k in range(1, replicas)]
    mixed = combine(result, first, second, gate)
    k = 2
    while k < pieces:
        other = over_tp(k)(mixed)
        mixed = mixed.astype(F32) + other.astype(F32)
        k *= 2
        if k < pieces:
            mixed = mixed.astype(BF16)
    out_half = (resid_new.astype(F32) + mixed.astype(F32)).astype(BF16)
    out_other = over_tp(1)(out_half)
    core = lax.axis_index("tp") & 1
    out_hidden = jnp.where(
        core == 0,
        jnp.concatenate([out_half, out_other], axis=1),
        jnp.concatenate([out_other, out_half], axis=1),
    )
    return (out_hidden, new_tail_kv)


def solution(mesh):
    from jax.sharding import PartitionSpec as P

    return jax.shard_map(
        body,
        mesh=mesh,
        in_specs=(
            P("req", None), P(None, "req", None, "tp"), P(None, "req", None, "tp"),
            P("req"), P("req"), P("req"), P(), P(None, "tp"), P(),
            P(None, "tp"), P(None, "tp"), P(None, "tp"), P("tp", None), P(), P(),
            P("req", None), P("req", None, "tp"), P("req", None, "tp"), P("req", "tp", None), P(),
        ),
        out_specs=(P("req", None), P(None, "req", None, "tp")),
        check_vma=False,
    )
```

```python
import functools
import jax
import jax.numpy as jnp
from jax import lax
from jax.experimental import pallas as pl
from jax.experimental.pallas import tpu as pltpu
from jax.sharding import PartitionSpec as P

HD = 64
EPS = 1e-06
F32 = jnp.float32
BF16 = jnp.bfloat16
NT = (((1,), (1,)), ((), ()))
LANES = 128
TILE = 64
TOP = 2
MIG = 4
EXTRA = 16
VMEM_BYTES = 60 * 1024 * 1024


def iota(shape, dim):
    return lax.broadcasted_iota(jnp.int32, shape, dim)


def onehot(hit):
    return hit.astype(F32).astype(BF16)


def attention_kernel(
    group_hbm, plen_hbm, tlen_hbm, group_row_hbm, bucket_hbm, bias_hbm, gain_hbm,
    hidden_hbm, wq_hbm, wk_hbm, wv_hbm, prompt_hbm, tail_hbm, slots_hbm,
    head_ref, tail_out, packet_out,
    group_sm, plen_sm, tlen_sm, perm_sm, slots_sm, mover_sm, group_row, bucket_row, bias_rows, gain_v, perm_v,
    hidden_v, wq_v, wk_v, wv_v, pk_v, pv_v, kbuf, vbuf,
    q_v, knew_v, vnew_v, table, s_p, s_t, w_p, o_v, sorted_v, qbd_v,
    small_sem, w_sem, p_sem, in_sem, out_sem, perm_sem, packet_sem,
):
    rows, width = hidden_v.shape
    groups, prompt_rows, cols = pv_v.shape
    tail_rows = kbuf.shape[1]
    heads = cols // HD
    per8 = 8 // heads
    per16 = 16 // heads
    width_t = per8 * tail_rows
    span_end = prompt_rows + tail_rows
    tile_rows = TILE * heads
    tiles = rows // TILE

    small = [
        pltpu.make_async_copy(src, dst, small_sem.at[i])
        for i, (src, dst) in enumerate(
            (
                (group_hbm, group_sm), (plen_hbm, plen_sm), (tlen_hbm, tlen_sm),
                (group_row_hbm, group_row), (bucket_hbm, bucket_row),
                (bias_hbm, bias_rows), (gain_hbm, gain_v), (slots_hbm, slots_sm),
            )
        )
    ]
    weights = [
        pltpu.make_async_copy(src, dst, w_sem.at[i])
        for i, (src, dst) in enumerate(
            ((hidden_hbm, hidden_v), (wq_hbm, wq_v), (wk_hbm, wk_v), (wv_hbm, wv_v))
        )
    ]
    prompts = [
        pltpu.make_async_copy(prompt_hbm.at[0], pk_v, p_sem.at[0]),
        pltpu.make_async_copy(prompt_hbm.at[1], pv_v, p_sem.at[1]),
    ]

    def tile_in(t):
        at = pl.ds(t * TILE, TILE)
        return [
            pltpu.make_async_copy(tail_hbm.at[0, at], kbuf.at[at], in_sem.at[0, t]),
            pltpu.make_async_copy(tail_hbm.at[1, at], vbuf.at[at], in_sem.at[1, t]),
        ]

    def tile_out(t):
        at = pl.ds(t * TILE, TILE)
        return [
            pltpu.make_async_copy(kbuf.at[at], tail_out.at[0, at], out_sem.at[0, t]),
            pltpu.make_async_copy(vbuf.at[at], tail_out.at[1, at], out_sem.at[1, t]),
        ]

    for copy in small + weights + prompts[:1]:
        copy.start()
    for copy in small:
        copy.wait()

    eye = onehot(iota((rows, rows), 0) == iota((rows, rows), 1))
    g_row = group_row[...]
    g_col = lax.dot_general(
        eye, jnp.broadcast_to(g_row.astype(F32), (8, rows)).astype(BF16), NT,
        preferred_element_type=F32,
    )[:, 0:1].astype(jnp.int32)
    key_row = g_row * rows + iota((1, rows), 1)
    key_col = g_col * rows + iota((rows, 1), 0)
    rank_row = jnp.sum((key_col < key_row).astype(jnp.int32), axis=0, keepdims=True)
    rank_col = jnp.sum((key_row < key_col).astype(jnp.int32), axis=1, keepdims=True)
    perm_row = jnp.sum(
        jnp.where(rank_col == iota((rows, rows), 1), iota((rows, rows), 0), 0), axis=0, keepdims=True
    )
    perm_v[...] = jnp.broadcast_to(perm_row, perm_v.shape)
    perm_copy = pltpu.make_async_copy(perm_v, perm_sm, perm_sem)
    perm_copy.start()

    span = bucket_row.shape[1]
    buckets = bias_rows.shape[1]
    below = (bucket_row[...] < iota((buckets, span), 0)).astype(jnp.int32)
    starts = jnp.sum(below, axis=1, keepdims=True)
    bias = jnp.concatenate([bias_rows[...]] * per8, axis=0)
    distance = span_end - iota(table.shape, 1)
    found = jnp.broadcast_to(bias[:, 0:1], table.shape)
    for k in range(1, buckets):
        found = jnp.where(distance >= starts[k : k + 1, 0:1], bias[:, k : k + 1], found)
    table[...] = found

    base = lax.axis_index("req") * rows
    for m in range(MIG + 1):
        mover_sm[m] = 0

    def look(i, count):
        away = slots_sm[base + i] != base + i

        @pl.when(away)
        def _():
            mover_sm[jnp.minimum(count, MIG)] = i

        return count + away.astype(jnp.int32)

    lax.fori_loop(0, rows, look, 0, unroll=16)
    for copy in weights:
        copy.wait()
    for t in range(tiles):
        for copy in tile_in(t):
            copy.start()
    prompts[1].start()
    v = hidden_v[...].astype(F32)
    normed = (
        v * lax.rsqrt(jnp.mean(v * v, axis=-1, keepdims=True) + EPS) * gain_v[...]
    ).astype(BF16)
    query = jnp.dot(normed, wq_v[...], preferred_element_type=F32).astype(BF16)
    q_v[...] = query * jnp.asarray(HD ** (-0.5), BF16)
    key_new = jnp.dot(normed, wk_v[...], preferred_element_type=F32).astype(BF16)
    value_new = jnp.dot(normed, wv_v[...], preferred_element_type=F32).astype(BF16)
    knew_v[...] = key_new.astype(F32)
    vnew_v[...] = value_new.astype(F32)
    perm_copy.wait()

    lane = iota((8, LANES), 1)
    sub = iota((8, LANES), 0)
    row16 = iota((16, cols), 0)
    minus = jnp.float32(-jnp.inf)
    pieces = prompt_rows // LANES

    def build_bias(tile):
        def step(i, carry):
            base = tile * TILE + i * per8
            out_p = [jnp.full((8, LANES), minus) for _ in range(pieces)]
            out_t = [jnp.full((8, LANES), minus) for _ in range(width_t // LANES)]
            for j in range(per8):
                r = perm_sm[0, base + j]
                length = tlen_sm[r]
                plen = plen_sm[group_sm[r]]
                start = span_end - plen - length
                block = start // LANES
                off = start - block * LANES
                mine = (sub >= j * heads) & (sub < (j + 1) * heads)
                window = table[:, pl.ds(pl.multiple_of(block * LANES, LANES), prompt_rows + LANES)]
                turn = jnp.where(off == 0, 0, LANES - off)
                turned = [
                    pltpu.roll(window[:, k * LANES : (k + 1) * LANES], turn, 1)
                    for k in range(pieces + 1)
                ]
                for k in range(pieces):
                    here = jnp.where(lane < LANES - off, turned[k], turned[k + 1])
                    out_p[k] = jnp.where(mine & (lane < plen - k * LANES), here, out_p[k])
                place = j * tail_rows
                k = place // LANES
                place = place - k * LANES
                own = table[:, prompt_rows : prompt_rows + LANES]
                shift = place - (tail_rows - length)
                shift = jnp.where(shift < 0, shift + LANES, shift)
                own = pltpu.roll(own, shift, 1)
                live = mine & (lane >= place) & (lane <= place + length)
                out_t[k] = jnp.where(live, own, out_t[k])
            at = pl.ds(pl.multiple_of(tile * tile_rows + i * 8, 8), 8)
            for k in range(pieces):
                s_p[at, k * LANES : (k + 1) * LANES] = out_p[k]
            for k in range(width_t // LANES):
                s_t[at, k * LANES : (k + 1) * LANES] = out_t[k]
            return carry

        lax.fori_loop(0, TILE // per8, step, 0, unroll=8)

    def insert(t):
        def step(i, carry):
            r = t * TILE + i
            length = tlen_sm[r]
            first = pl.multiple_of(length // 16 * 16, 16)
            hit = row16 == length - first
            for new, buf in ((knew_v, kbuf), (vnew_v, vbuf)):
                fresh = jnp.broadcast_to(new[pl.ds(r, 1), :], (16, cols))
                old = buf[r, pl.ds(first, 16), :].astype(F32)
                buf[r, pl.ds(first, 16), :] = jnp.where(hit, fresh, old).astype(BF16)
            return carry

        lax.fori_loop(0, TILE, step, 0, unroll=8)

    own_head = iota((tile_rows, cols), 0) % heads == iota((tile_rows, cols), 1) // HD
    spread_row = iota((tile_rows, rows), 0) // heads
    first_head = iota((TILE, LANES), 1) < HD

    def spread_of(tile):
        return onehot(rank_row == spread_row + tile * TILE)

    def member_of(tile):
        group8 = jnp.broadcast_to(g_row.astype(F32), (8, rows)).astype(BF16)
        return lax.dot_general(
            spread_of(tile), group8, NT, preferred_element_type=F32
        )[:, 0:1].astype(jnp.int32)

    def group_range(tile):
        low = group_sm[perm_sm[0, tile * TILE]]
        high = group_sm[perm_sm[0, tile * TILE + TILE - 1]]
        return low, high + 1

    def scores(tile, carry):
        build_bias(tile)
        at = pl.ds(pl.multiple_of(tile * tile_rows, tile_rows), tile_rows)
        qrep = jnp.dot(spread_of(tile), q_v[...], preferred_element_type=F32)
        qbd = jnp.where(own_head, qrep, 0.0)
        qbd_v[at, :] = qbd.astype(BF16)
        member = member_of(tile)

        @pl.when(tile == 0)
        def _():
            prompts[0].wait()

        def one_group(g, carry):
            part = jnp.where(member == g, qbd, 0.0).astype(BF16)
            s_p[at, :] += lax.dot_general(part, pk_v[g], NT, preferred_element_type=F32)
            return carry

        low, high = group_range(tile)
        lax.fori_loop(low, high, one_group, 0)
        for copy in tile_in(tile):
            copy.wait()
        insert(tile)
        for copy in tile_out(tile):
            copy.start()
        return carry

    lax.fori_loop(0, tiles, scores, 0)
    packet = [
        pltpu.make_async_copy(
            buf.at[mover_sm[m]], packet_out.at[2 * m + side], packet_sem.at[2 * m + side]
        )
        for m in range(MIG)
        for side, buf in enumerate((kbuf, vbuf))
    ]
    for copy in packet:
        copy.start()
    prompts[1].wait()

    def gathered(buf, first):
        return jnp.concatenate([buf[perm_sm[0, first + j]] for j in range(per16)], axis=0)

    def values(tile, carry):
        base = pl.multiple_of(tile * tile_rows, tile_rows)
        at = pl.ds(base, tile_rows)
        for i in range(TILE // per16):
            keys = gathered(kbuf, tile * TILE + i * per16)
            here = pl.ds(pl.multiple_of(base + i * 16, 16), 16)
            got = lax.dot_general(qbd_v[here, :], keys, NT, preferred_element_type=F32)
            upper = pl.ds(pl.multiple_of(base + i * 16, 8), 8)
            lower = pl.ds(pl.multiple_of(base + i * 16 + 8, 8), 8)
            s_t[upper, :] += got[:8, :width_t]
            s_t[lower, :] += got[8:, width_t:]
        prompt_s = s_p[at, :]
        tail_s = s_t[at, :]
        top = jnp.maximum(
            jnp.max(prompt_s, axis=1, keepdims=True), jnp.max(tail_s, axis=1, keepdims=True)
        )
        pe = jnp.exp(prompt_s - top)
        te = jnp.exp(tail_s - top)
        total = jnp.sum(pe, axis=1, keepdims=True) + jnp.sum(te, axis=1, keepdims=True)
        part = 1.0 / total
        w_p[...] = (pe * part).astype(BF16)
        tw = te * part
        none = jnp.zeros((8, width_t), F32)
        for i in range(TILE // per16):
            row = i * 16
            upper = jnp.concatenate([tw[row : row + 8], none], axis=1)
            lower = jnp.concatenate([none, tw[row + 8 : row + 16]], axis=1)
            both = jnp.concatenate([upper, lower], axis=0).astype(BF16)
            vals = gathered(vbuf, tile * TILE + i * per16)
            o_t = jnp.dot(both, vals, preferred_element_type=F32)
            for b in range(cols // LANES):
                o_v[b, row : row + 16, :] = o_t[:, b * LANES : (b + 1) * LANES]
        member = member_of(tile)

        def one_group(g, carry):
            w = jnp.where(member == g, w_p[...].astype(F32), 0.0).astype(BF16)
            o_p = jnp.dot(w, pv_v[g], preferred_element_type=F32)
            for b in range(cols // LANES):
                o_v[b] += o_p[:, b * LANES : (b + 1) * LANES]
            return carry

        low, high = group_range(tile)
        lax.fori_loop(low, high, one_group, 0)
        to = pl.ds(pl.multiple_of(tile * TILE, TILE), TILE)
        for b in range(cols // LANES):
            even = o_v[b, pl.ds(2 * b, TILE, stride=heads), :]
            odd = o_v[b, pl.ds(2 * b + 1, TILE, stride=heads), :]
            sorted_v[to, b * LANES : (b + 1) * LANES] = jnp.where(first_head, even, odd).astype(BF16)
        return carry

    lax.fori_loop(0, tiles, values, 0)
    unsort = onehot(rank_col == iota((rows, rows), 1))
    head_ref[...] = jnp.dot(unsort, sorted_v[...], preferred_element_type=F32).astype(BF16)
    for copy in packet:
        copy.wait()
    for t in range(tiles):
        for copy in tile_out(t):
            copy.wait()


def attention(
    hidden_in, prompt_kv, tail_kv, group_of, prompt_len, tail_len, bucket_of, bias_table,
    attn_gain, w_query, w_key, w_value, new_slot,
):
    rows, width = hidden_in.shape
    cols = w_query.shape[1]
    heads = cols // HD
    groups, prompt_rows = prompt_kv.shape[1:3]
    tail_rows = tail_kv.shape[2]
    span = bucket_of.shape[0]
    buckets = bias_table.shape[0]
    table_width = 2 * prompt_rows + LANES
    width_t = 8 // heads * tail_rows
    tiles = rows // TILE
    vm = pl.BlockSpec(memory_space=pltpu.VMEM)
    hbm = pl.BlockSpec(memory_space=pl.ANY)
    return pl.pallas_call(
        attention_kernel,
        out_shape=(
            jax.ShapeDtypeStruct((rows, cols), BF16),
            jax.ShapeDtypeStruct(tail_kv.shape, BF16),
            jax.ShapeDtypeStruct((2 * MIG, tail_rows, cols), BF16),
        ),
        in_specs=[hbm] * 14,
        out_specs=(vm, hbm, hbm),
        scratch_shapes=[
            pltpu.SMEM((rows,), jnp.int32),
            pltpu.SMEM((groups,), jnp.int32),
            pltpu.SMEM((rows,), jnp.int32),
            pltpu.SMEM((8, rows), jnp.int32),
            pltpu.SMEM(new_slot.shape, jnp.int32),
            pltpu.SMEM((MIG + 1,), jnp.int32),
            pltpu.VMEM((1, rows), jnp.int32),
            pltpu.VMEM((1, span), jnp.int32),
            pltpu.VMEM((heads, buckets), F32),
            pltpu.VMEM((1, width), F32),
            pltpu.VMEM((8, rows), jnp.int32),
            pltpu.VMEM((rows, width), BF16),
            pltpu.VMEM((width, cols), BF16),
            pltpu.VMEM((width, cols), BF16),
            pltpu.VMEM((width, cols), BF16),
            pltpu.VMEM((groups, prompt_rows, cols), BF16),
            pltpu.VMEM((groups, prompt_rows, cols), BF16),
            pltpu.VMEM((rows, tail_rows, cols), BF16),
            pltpu.VMEM((rows, tail_rows, cols), BF16),
            pltpu.VMEM((rows, cols), BF16),
            pltpu.VMEM((rows, cols), F32),
            pltpu.VMEM((rows, cols), F32),
            pltpu.VMEM((8, table_width), F32),
            pltpu.VMEM((rows * heads, prompt_rows), F32),
            pltpu.VMEM((rows * heads, width_t), F32),
            pltpu.VMEM((TILE * heads, prompt_rows), BF16),
            pltpu.VMEM((cols // LANES, TILE * heads, LANES), F32),
            pltpu.VMEM((rows, cols), BF16),
            pltpu.VMEM((rows * heads, cols), BF16),
            pltpu.SemaphoreType.DMA((8,)),
            pltpu.SemaphoreType.DMA((4,)),
            pltpu.SemaphoreType.DMA((2,)),
            pltpu.SemaphoreType.DMA((2, tiles)),
            pltpu.SemaphoreType.DMA((2, tiles)),
            pltpu.SemaphoreType.DMA,
            pltpu.SemaphoreType.DMA((2 * MIG,)),
        ],
        compiler_params=pltpu.CompilerParams(vmem_limit_bytes=VMEM_BYTES),
        cost_estimate=pl.CostEstimate(flops=8_000_000_000, bytes_accessed=45_000_000, transcendentals=700_000),
        name="attention",
    )(
        group_of, prompt_len, tail_len, group_of[None, :], bucket_of[None, :], bias_table.T,
        attn_gain[None, :], hidden_in, w_query, w_key, w_value, prompt_kv, tail_kv, new_slot,
    )


def block_rows(cap):
    return cap + EXTRA


def plan_kernel(cap, slots_ref, ids_ref, *refs):
    place_ref, extra_ref, wide_ref, kron_ref, plan_ref, slot_s = refs[-6:]
    replicas, rows = slots_ref.shape
    experts = slot_s.shape[0]
    size = place_ref.shape[0] // replicas
    me = lax.axis_index("req")
    ns = slots_ref[...]
    at_sub = iota((replicas, rows), 0)
    at_lane = iota((replicas, rows), 1)
    moved = ns != at_sub * rows + at_lane
    tri = (iota((rows, rows), 0) < iota((rows, rows), 1)).astype(BF16)
    rank = jnp.dot(moved.astype(F32).astype(BF16), tri, preferred_element_type=F32).astype(jnp.int32)
    going_to = ns // rows
    mine = at_sub == me

    def own(values):
        return jnp.sum(jnp.where(mine, values, 0), axis=0, keepdims=True)

    moved_me = own(moved.astype(jnp.int32))
    rank_me = own(rank)
    to_me = own(going_to)
    ids_rows = ids_ref[...]
    at_e = iota((experts, rows), 0)
    hit = (ids_rows[0:1] == at_e) | (ids_rows[1:2] == at_e)
    normal = (hit & (moved_me == 0)).astype(F32).astype(BF16)
    slot = jnp.dot(normal, tri, preferred_element_type=F32).astype(jnp.int32)
    slot_s[...] = jnp.where(hit, jnp.where(moved_me > 0, cap + rank_me, slot), -1)
    at_row = iota((size, rows), 0)
    at_extra = iota((EXTRA, rows), 0)
    for k in range(replicas):
        e = me ^ k
        block = pl.ds(k * size, size)
        row = slot_s[pl.ds(e, 1), :]
        leaving = jnp.where((moved_me > 0) & (to_me == e), rank_me, -100)
        place_ref[block, :] = onehot(at_row == row)
        more = pl.ds(k * EXTRA, EXTRA)
        extra_ref[more, 0:rows] = onehot(at_extra == leaving + MIG)
        extra_ref[more, rows:] = onehot(at_extra == leaving + 2 * MIG)
    lane = iota(wide_ref.shape, 1)
    eye = onehot(iota((rows, rows), 0) == iota((rows, rows), 1))
    facts = jnp.concatenate([ids_rows, jnp.zeros((6, rows), jnp.int32)], axis=0)
    columns = lax.dot_general(
        eye, facts.astype(F32).astype(BF16), NT, preferred_element_type=F32
    )
    wide_ref[...] = jnp.where(
        lane == 0, columns[:, 0:1], jnp.where(lane == 1, columns[:, 1:2], 0.0)
    ).astype(BF16)
    dest = jnp.max(jnp.where(moved, going_to, -1), axis=1, keepdims=True)
    dest = jnp.where(dest < 0, iota((replicas, 1), 0), dest)
    hot = (dest == iota((replicas, replicas), 1)).astype(F32).astype(BF16)
    span = replicas * EXTRA
    mixed_row = (iota((span, replicas), 0) // EXTRA) ^ me
    a = (mixed_row == iota((span, replicas), 1)).astype(F32).astype(BF16)
    by_source = lax.dot_general(a, hot, NT, preferred_element_type=F32).astype(BF16)
    pairs = lax.dot_general(by_source, a, NT, preferred_element_type=F32)
    same = iota((span, span), 0) % EXTRA == iota((span, span), 1) % EXTRA
    kron_ref[...] = jnp.where(same, pairs, 0.0).astype(BF16)
    sub1 = iota((replicas, 1), 0)

    def source_of(who):
        return jnp.sum(jnp.where(dest == who, sub1, 0), axis=0, keepdims=True)

    bits = replicas.bit_length() - 1

    def held(diff):
        found = jnp.zeros_like(diff)
        for i in range(bits - 1):
            found = found + (((diff >> (bits - 1 - i)) & 1) << i)
        return found

    diff = source_of(me) ^ me
    final = jnp.where((diff & 1) == 1, 1 << (bits - 1), held(diff))
    send = held(source_of(me ^ 1) ^ (me ^ 1))
    lane8 = iota((8, LANES), 1)
    plan = jnp.where(lane8 == 0, final, jnp.where(lane8 == 1, send, -1))
    lane1 = iota((1, rows), 1)
    for m in range(MIG):
        is_m = (moved_me > 0) & (rank_me == m)
        mover = jnp.sum(jnp.where(is_m, lane1, 0), axis=1, keepdims=True)
        plan = jnp.where(lane8 == 8 + m, mover, plan)
        come = moved & (going_to == me) & (rank == m)
        to = jnp.sum(jnp.where(come, ns - me * rows + 1, 0), axis=1, keepdims=True)
        to = jnp.sum(to, axis=0, keepdims=True) - 1
        plan = jnp.where(lane8 == 16 + m, to, plan)
    plan_ref[...] = plan


def make_plan(slots, expert_ids, experts, cap, after):
    replicas, rows = slots.shape
    size = block_rows(cap)
    vm = pl.BlockSpec(memory_space=pltpu.VMEM)
    span = replicas * EXTRA
    return pl.pallas_call(
        functools.partial(plan_kernel, cap),
        out_shape=(
            jax.ShapeDtypeStruct((replicas * size, rows), BF16),
            jax.ShapeDtypeStruct((replicas * EXTRA, 2 * rows), BF16),
            jax.ShapeDtypeStruct((rows, LANES), BF16),
            jax.ShapeDtypeStruct((span, span), BF16),
            jax.ShapeDtypeStruct((8, LANES), jnp.int32),
        ),
        in_specs=[vm, vm] + [pl.BlockSpec(memory_space=pl.ANY)] * len(after),
        out_specs=(vm,) * 5,
        scratch_shapes=[pltpu.VMEM((experts, rows), jnp.int32)],
        compiler_params=pltpu.CompilerParams(vmem_limit_bytes=VMEM_BYTES),
        cost_estimate=pl.CostEstimate(flops=0, bytes_accessed=0, transcendentals=0),
        name="plan",
    )(slots, expert_ids.T, *after)


def load(sem, *pairs):
    made = [pltpu.make_async_copy(src, dst, sem.at[i]) for i, (src, dst) in enumerate(pairs)]
    for copy in made:
        copy.start()
    for copy in made:
        copy.wait()


def norm(values, gain):
    v = values.astype(F32)
    return (v * lax.rsqrt(jnp.mean(v * v, axis=-1, keepdims=True) + EPS) * gain).astype(BF16)


def dispatch_kernel(pieces, replicas, *refs):
    heads_hbm = refs[:pieces]
    wout_hbm = refs[pieces : 2 * pieces]
    hidden_hbm, gain_ref, place_hbm, extra_hbm, wide_hbm = refs[2 * pieces : 2 * pieces + 5]
    refs = refs[2 * pieces + 6 :]
    resid_ref = refs[0]
    outs = refs[1 : 1 + replicas]
    head_v, wout_v, stack, hidden_ref, place_ref, extra_ref, wide_ref, sem, more = refs[1 + replicas :]
    tp = lax.axis_index("tp")
    core = tp & 1
    rows, width = hidden_ref.shape
    cols = width // pieces
    half = width // 2

    def copies():
        made = []
        for k in range(pieces):
            at = pl.ds(pl.multiple_of((tp ^ k) * cols, cols), cols)
            made.append(pltpu.make_async_copy(wout_hbm[k], wout_v.at[at], sem.at[0, k]))
            made.append(pltpu.make_async_copy(heads_hbm[k], head_v.at[:, at], sem.at[1, k]))
        made.append(pltpu.make_async_copy(hidden_hbm, hidden_ref, more.at[0]))
        return made

    late = [
        pltpu.make_async_copy(place_hbm, place_ref, more.at[1]),
        pltpu.make_async_copy(extra_hbm, extra_ref, more.at[2]),
        pltpu.make_async_copy(wide_hbm, wide_ref, more.at[3]),
    ]

    for copy in copies() + late:
        copy.start()
    for copy in copies():
        copy.wait()
    attn = jnp.dot(head_v[...], wout_v[...], preferred_element_type=F32)
    resid = (hidden_ref[...].astype(F32) + attn).astype(BF16)
    resid_ref[...] = resid
    normed = norm(resid, gain_ref[...])
    first = core == 0
    stack[0:rows, :] = jnp.where(first, normed[:, :half], normed[:, half:])
    stack[rows : 2 * rows, :] = jnp.where(first, resid[:, :half], resid[:, half:])
    for copy in late:
        copy.wait()
    size = place_ref.shape[0] // replicas
    extra = jnp.dot(extra_ref[:, 0:rows], stack[rows:, :], preferred_element_type=F32)
    names = jnp.dot(extra_ref[:, rows:], wide_ref[...], preferred_element_type=F32)
    for k in range(replicas):
        block = jnp.dot(
            place_ref[k * size : (k + 1) * size], stack[0:rows, :], preferred_element_type=F32
        )
        more_k = slice(k * EXTRA, (k + 1) * EXTRA)
        outs[k][0 : size - EXTRA, :] = block[: size - EXTRA].astype(BF16)
        tail = block[size - EXTRA :] + extra[more_k]
        outs[k][size - EXTRA :, 0:LANES] = (tail[:, :LANES] + names[more_k]).astype(BF16)
        outs[k][size - EXTRA :, LANES:] = tail[:, LANES:].astype(BF16)


def dispatch(heads, wouts, hidden, gain, place, extra, wide, after, replicas):
    rows, width = hidden.shape
    pieces = len(heads)
    half = width // 2
    size = place.shape[0] // replicas
    vm = pl.BlockSpec(memory_space=pltpu.VMEM)
    hbm = pl.BlockSpec(memory_space=pl.ANY)
    return pl.pallas_call(
        functools.partial(dispatch_kernel, pieces, replicas),
        out_shape=(jax.ShapeDtypeStruct((rows, width), BF16),)
        + tuple(jax.ShapeDtypeStruct((size, half), BF16) for _ in range(replicas)),
        in_specs=[hbm] * (2 * pieces) + [hbm, vm, hbm, hbm, hbm, hbm],
        out_specs=(vm,) * (1 + replicas),
        scratch_shapes=[
            pltpu.VMEM((rows, width), BF16),
            pltpu.VMEM((width, width), BF16),
            pltpu.VMEM((2 * rows, half), BF16),
            pltpu.VMEM((rows, width), BF16),
            pltpu.VMEM(place.shape, BF16),
            pltpu.VMEM(extra.shape, BF16),
            pltpu.VMEM(wide.shape, BF16),
            pltpu.SemaphoreType.DMA((2, pieces)),
            pltpu.SemaphoreType.DMA((4,)),
        ],
        compiler_params=pltpu.CompilerParams(vmem_limit_bytes=VMEM_BYTES),
        cost_estimate=pl.CostEstimate(flops=1_200_000_000, bytes_accessed=6_000_000, transcendentals=0),
        name="dispatch",
    )(*heads, *wouts, hidden, gain[None, :], place, extra, wide, after)


def expert_kernel(replicas, *refs):
    own = refs[:replicas]
    pair = refs[replicas : 2 * replicas]
    wg_hbm, wu_hbm, wd_hbm, keep_ref, give_ref, x_own, x_pair, wg, wu, wd, sem, xsem = refs[2 * replicas :]
    core = lax.axis_index("tp") & 1
    size, half = own[0].shape

    def weight_copies():
        return [
            pltpu.make_async_copy(wg_hbm.at[0], wg, sem.at[0]),
            pltpu.make_async_copy(wu_hbm.at[0], wu, sem.at[1]),
            pltpu.make_async_copy(wd_hbm.at[0], wd, sem.at[2]),
        ]

    def block_copies():
        made = []
        for k in range(replicas):
            at = pl.ds(k * size, size)
            made.append(pltpu.make_async_copy(own[k], x_own.at[at], xsem.at[0, k]))
            made.append(pltpu.make_async_copy(pair[k], x_pair.at[at], xsem.at[1, k]))
        return made

    for copy in weight_copies() + block_copies():
        copy.start()
    for copy in block_copies() + weight_copies():
        copy.wait()
    here = pl.ds(pl.multiple_of(core * half, half), half)
    there = pl.ds(pl.multiple_of((1 - core) * half, half), half)
    total = replicas * size
    step = 256 if total % 256 == 0 else size

    def tile(i, carry):
        at = pl.ds(pl.multiple_of(i * step, step), step)
        a, b = x_own[at, :], x_pair[at, :]
        gate = lax.dot_general(a, wg[:, here], NT, preferred_element_type=F32) + lax.dot_general(
            b, wg[:, there], NT, preferred_element_type=F32
        )
        up = lax.dot_general(a, wu[:, here], NT, preferred_element_type=F32) + lax.dot_general(
            b, wu[:, there], NT, preferred_element_type=F32
        )
        act = (jax.nn.gelu(gate, approximate=True) * up).astype(BF16)
        give_ref[at, :] = jnp.dot(act, wd[:, there], preferred_element_type=F32).astype(BF16)
        keep_ref[at, :] = jnp.dot(act, wd[:, here], preferred_element_type=F32).astype(BF16)
        return carry

    lax.fori_loop(0, total // step, tile, 0)


def expert(own, pair, w_gate, w_up, w_down):
    replicas = len(own)
    size, half = own[0].shape
    _, width, hidden = w_gate.shape
    total = replicas * size
    vm = pl.BlockSpec(memory_space=pltpu.VMEM)
    hbm = pl.BlockSpec(memory_space=pl.ANY)
    shape = jax.ShapeDtypeStruct((total, half), BF16)
    return pl.pallas_call(
        functools.partial(expert_kernel, replicas),
        out_shape=(shape, shape),
        in_specs=[hbm] * (2 * replicas + 3),
        out_specs=(vm, vm),
        scratch_shapes=[
            pltpu.VMEM((total, half), BF16),
            pltpu.VMEM((total, half), BF16),
            pltpu.VMEM((hidden, width), BF16),
            pltpu.VMEM((hidden, width), BF16),
            pltpu.VMEM((hidden, width), BF16),
            pltpu.SemaphoreType.DMA((3,)),
            pltpu.SemaphoreType.DMA((2, replicas)),
        ],
        compiler_params=pltpu.CompilerParams(vmem_limit_bytes=VMEM_BYTES),
        cost_estimate=pl.CostEstimate(flops=3_400_000_000, bytes_accessed=8_000_000, transcendentals=600_000),
        name="expert",
    )(*own, *pair, jnp.swapaxes(w_gate, 1, 2), jnp.swapaxes(w_up, 1, 2), w_down)


def give_back_kernel(cap, keep_hbm, got_hbm, kron_hbm, *refs):
    replicas = len(refs) - 5
    outs = refs[:replicas]
    rows_v, keep_ref, got_ref, kron_ref, sem = refs[replicas:]
    load(sem, (keep_hbm, keep_ref), (got_hbm, got_ref), (kron_hbm, kron_ref))
    size = outs[0].shape[0]
    for k in range(replicas):
        at = slice(k * size, (k + 1) * size)
        both = keep_ref[at, :].astype(F32) + got_ref[at, :].astype(F32)
        outs[k][...] = both.astype(BF16)
        rows_v[k * EXTRA : (k + 1) * EXTRA, :] = both[size - EXTRA :].astype(BF16)
    moved = jnp.dot(kron_ref[...], rows_v[...], preferred_element_type=F32)
    first = iota((EXTRA, 1), 0) >= cap - (size - EXTRA)
    for k in range(replicas):
        at = slice(k * EXTRA, (k + 1) * EXTRA)
        outs[k][size - EXTRA :, :] = jnp.where(
            first, moved[at], rows_v[at, :].astype(F32)
        ).astype(BF16)


def give_back(keep, got, kron, cap, replicas):
    total, half = keep.shape
    size = total // replicas
    vm = pl.BlockSpec(memory_space=pltpu.VMEM)
    hbm = pl.BlockSpec(memory_space=pl.ANY)
    return pl.pallas_call(
        functools.partial(give_back_kernel, cap),
        out_shape=tuple(jax.ShapeDtypeStruct((size, half), BF16) for _ in range(replicas)),
        in_specs=[hbm] * 3,
        out_specs=(vm,) * replicas,
        scratch_shapes=[
            pltpu.VMEM((replicas * EXTRA, half), BF16),
            pltpu.VMEM((total, half), BF16),
            pltpu.VMEM((total, half), BF16),
            pltpu.VMEM(kron.shape, BF16),
            pltpu.SemaphoreType.DMA((3,)),
        ],
        compiler_params=pltpu.CompilerParams(vmem_limit_bytes=VMEM_BYTES),
        cost_estimate=pl.CostEstimate(flops=30_000_000, bytes_accessed=2_500_000, transcendentals=0),
        name="give_back",
    )(keep, got, kron)


def gates_kernel(cap, replicas, *refs):
    own = refs[:replicas]
    pair = refs[replicas : 2 * replicas]
    (after_hbm, resid_hbm, slots_ref, ids_ref, gain_ref, router_ref) = refs[
        2 * replicas : 2 * replicas + 6
    ]
    (first_ref, second_ref, gate_ref, new_ref, resid_ref, own_v, pair_v, sem) = refs[2 * replicas + 6 :]
    me = lax.axis_index("req")
    core = lax.axis_index("tp") & 1
    rows, width = resid_ref.shape
    half = width // 2
    size = own[0].shape[0]
    low = pl.ds(size - EXTRA, EXTRA)
    skip = 0
    load(
        sem,
        (resid_hbm, resid_ref),
        *[(own[k].at[low], own_v.at[k]) for k in range(replicas)],
        *[(pair[k].at[low], pair_v.at[k]) for k in range(replicas)],
    )
    ns = slots_ref[...]
    count = ns.shape[0]
    at_sub = iota((count, rows), 0)
    moved = ns != at_sub * rows + iota((count, rows), 1)
    before = (iota((rows, rows), 0) < iota((rows, rows), 1)).astype(BF16)
    movedf = moved.astype(F32)
    rank = jnp.dot(movedf.astype(BF16), before, preferred_element_type=F32)
    coming = moved & (ns // rows == me)
    slot_to = jnp.sum(jnp.where(coming, ns - me * rows + 1, 0), axis=0, keepdims=True) - 1
    rank_in = jnp.sum(jnp.where(coming, rank, 0.0), axis=0, keepdims=True).astype(jnp.int32)
    landing = (iota((rows, rows), 0) == slot_to).astype(F32).astype(BF16)
    at16 = iota((EXTRA, rows), 0)

    def taken(offset):
        hot = (at16 == rank_in + (skip + offset)) & (slot_to >= 0)
        return lax.dot_general(landing, hot.astype(F32).astype(BF16), NT, preferred_element_type=F32)

    take_resid = taken(MIG)
    take_ids = taken(2 * MIG)
    vacated = jnp.sum(take_resid, axis=1, keepdims=True) > 0.5
    in_own = own_v[0].astype(F32)
    in_pair = pair_v[0].astype(F32)
    for k in range(1, replicas):
        in_own = in_own + own_v[k].astype(F32)
        in_pair = in_pair + pair_v[k].astype(F32)
    in_own, in_pair = in_own.astype(BF16), in_pair.astype(BF16)
    first_core = core == 0
    in_low = jnp.where(first_core, in_own, in_pair)
    in_high = jnp.where(first_core, in_pair, in_own)
    picked = take_resid.astype(BF16)
    resid = resid_ref[...]
    new_low = jnp.where(
        vacated, jnp.dot(picked, in_low, preferred_element_type=F32), resid[:, :half].astype(F32)
    ).astype(BF16)
    new_high = jnp.where(
        vacated, jnp.dot(picked, in_high, preferred_element_type=F32), resid[:, half:].astype(F32)
    ).astype(BF16)
    new_ref[...] = jnp.where(first_core, new_low, new_high)
    normed = norm(jnp.concatenate([new_low, new_high], axis=1), gain_ref[...])
    logits = lax.dot_general(normed, router_ref[...], NT, preferred_element_type=F32)
    experts = logits.shape[1]
    ids_in = jnp.dot(take_ids.astype(BF16), in_low[:, :LANES], preferred_element_type=F32)
    eye = onehot(iota((rows, rows), 0) == iota((rows, rows), 1))
    mine = at_sub == me
    moved_me = jnp.sum(jnp.where(mine, movedf, 0.0), axis=0, keepdims=True)
    facts = jnp.concatenate(
        [ids_ref[...].astype(F32), moved_me, jnp.zeros((5, rows), F32)], axis=0
    ).astype(BF16)
    ids = lax.dot_general(eye, facts, NT, preferred_element_type=F32)
    moved_col = ids[:, 2:3]
    id1 = jnp.where(vacated, ids_in[:, 0:1], ids[:, 0:1]).astype(jnp.int32)
    id2 = jnp.where(vacated, ids_in[:, 1:2], ids[:, 1:2]).astype(jnp.int32)
    at_e = iota((rows, experts), 1)
    hit1, hit2 = id1 == at_e, id2 == at_e
    picked1 = jnp.sum(jnp.where(hit1, logits, 0.0), axis=1, keepdims=True)
    picked2 = jnp.sum(jnp.where(hit2, logits, 0.0), axis=1, keepdims=True)
    gate = jax.nn.sigmoid(picked1 - picked2)
    gate_ref[...] = jnp.broadcast_to(gate, gate_ref.shape)
    old1 = ids[:, 0:1].astype(jnp.int32) == at_e
    old2 = ids[:, 1:2].astype(jnp.int32) == at_e
    normal = ((old1 | old2) & (moved_col < 0.5)).astype(F32).astype(BF16)
    after = (iota((rows, rows), 0) > iota((rows, rows), 1)).astype(BF16)
    slot = jnp.dot(after, normal, preferred_element_type=F32)
    slot1 = jnp.sum(jnp.where(hit1, slot, 0.0), axis=1, keepdims=True)
    slot2 = jnp.sum(jnp.where(hit2, slot, 0.0), axis=1, keepdims=True)
    in_rank = jnp.sum(
        jnp.where(take_resid > 0.5, iota((rows, EXTRA), 1), 0), axis=1, keepdims=True
    ) - (skip + MIG)
    slot1 = jnp.where(vacated, cap + in_rank, slot1.astype(jnp.int32))
    slot2 = jnp.where(vacated, cap + in_rank, slot2.astype(jnp.int32))
    lane = iota((rows, replicas * size), 1)
    first_ref[...] = (lane == (id1 ^ me) * size + slot1).astype(F32).astype(BF16)
    second_ref[...] = (lane == (id2 ^ me) * size + slot2).astype(F32).astype(BF16)


def make_gates(own, pair, after, resid, slots, ids, gain, router, cap):
    replicas = len(own)
    size, half = own[0].shape
    rows, width = resid.shape
    vm = pl.BlockSpec(memory_space=pltpu.VMEM)
    hbm = pl.BlockSpec(memory_space=pl.ANY)
    hot = jax.ShapeDtypeStruct((rows, replicas * size), BF16)
    return pl.pallas_call(
        functools.partial(gates_kernel, cap, replicas),
        out_shape=(
            hot,
            hot,
            jax.ShapeDtypeStruct((rows, LANES), F32),
            jax.ShapeDtypeStruct((rows, half), BF16),
        ),
        in_specs=[hbm] * (2 * replicas + 2) + [vm] * 4,
        out_specs=(vm,) * 4,
        scratch_shapes=[
            pltpu.VMEM((rows, width), BF16),
            pltpu.VMEM((replicas, EXTRA, half), BF16),
            pltpu.VMEM((replicas, EXTRA, half), BF16),
            pltpu.SemaphoreType.DMA((2 * replicas + 1,)),
        ],
        compiler_params=pltpu.CompilerParams(vmem_limit_bytes=VMEM_BYTES),
        cost_estimate=pl.CostEstimate(flops=200_000_000, bytes_accessed=6_000_000, transcendentals=0),
        name="gates",
    )(*own, *pair, after, resid, slots, ids.T, gain[None, :], router.T)


def combine_kernel(replicas, *refs):
    blocks = refs[:replicas]
    first_hbm, second_hbm, gate_hbm, out_ref, all_v, first_ref, second_ref, gate_ref, sem = refs[
        replicas:
    ]
    size = blocks[0].shape[0]
    load(
        sem,
        (first_hbm, first_ref),
        (second_hbm, second_ref),
        (gate_hbm, gate_ref),
        *[(blocks[k], all_v.at[pl.ds(k * size, size)]) for k in range(replicas)],
    )
    gate = gate_ref[:, 0:1]
    one = jnp.dot(first_ref[...], all_v[...], preferred_element_type=F32)
    two = jnp.dot(second_ref[...], all_v[...], preferred_element_type=F32)
    out_ref[...] = (gate * one + (1.0 - gate) * two).astype(BF16)


def combine(blocks, first, second, gate):
    replicas = len(blocks)
    size, half = blocks[0].shape
    rows = first.shape[0]
    vm = pl.BlockSpec(memory_space=pltpu.VMEM)
    hbm = pl.BlockSpec(memory_space=pl.ANY)
    return pl.pallas_call(
        functools.partial(combine_kernel, replicas),
        out_shape=jax.ShapeDtypeStruct((rows, half), BF16),
        in_specs=[hbm] * (replicas + 3),
        out_specs=vm,
        scratch_shapes=[
            pltpu.VMEM((replicas * size, half), BF16),
            pltpu.VMEM(first.shape, BF16),
            pltpu.VMEM(second.shape, BF16),
            pltpu.VMEM(gate.shape, F32),
            pltpu.SemaphoreType.DMA((replicas + 3,)),
        ],
        compiler_params=pltpu.CompilerParams(vmem_limit_bytes=VMEM_BYTES),
        cost_estimate=pl.CostEstimate(flops=400_000_000, bytes_accessed=2_500_000, transcendentals=0),
        name="combine",
    )(*blocks, first, second, gate)


def choose_kernel(plan_hbm, *refs):
    choices = refs[:-5]
    out_ref, plan_sm, sem, plan_sem = refs[-4:]
    load(plan_sem, (plan_hbm, plan_sm))
    index = plan_sm[0, 1]
    for i, choice in enumerate(choices):
        @pl.when(index == i)
        def _():
            load(sem, (choice, out_ref))


def choose(plan, held, after):
    hbm = pl.BlockSpec(memory_space=pl.ANY)
    return pl.pallas_call(
        choose_kernel,
        out_shape=jax.ShapeDtypeStruct(held[0].shape, BF16),
        in_specs=[hbm] * (2 + len(held)),
        out_specs=pl.BlockSpec(memory_space=pltpu.VMEM),
        scratch_shapes=[
            pltpu.SMEM(plan.shape, jnp.int32),
            pltpu.SemaphoreType.DMA((1,)),
            pltpu.SemaphoreType.DMA((1,)),
        ],
        compiler_params=pltpu.CompilerParams(vmem_limit_bytes=VMEM_BYTES),
        cost_estimate=pl.CostEstimate(flops=0, bytes_accessed=0, transcendentals=0),
        name="choose",
    )(plan, *held, after)


def patch_kernel(count, plan_hbm, *refs):
    choices = refs[:count]
    after_hbm, tail_hbm, out_hbm, plan_sm, slabs, sem, slab_sem, out_sem = refs[count:]
    load(sem, (plan_hbm, plan_sm))
    index = plan_sm[0, 0]
    for i, choice in enumerate(choices):
        @pl.when(index == i)
        def _():
            load(slab_sem, (choice, slabs))

    def moves(m):
        to = plan_sm[0, 16 + m]
        return to, [
            pltpu.make_async_copy(
                slabs.at[2 * m + side], out_hbm.at[side, to], out_sem.at[2 * m + side]
            )
            for side in range(2)
        ]

    for m in range(MIG):
        to, copies = moves(m)

        @pl.when(to >= 0)
        def _():
            for copy in copies:
                copy.start()
    for m in range(MIG):
        to, copies = moves(m)

        @pl.when(to >= 0)
        def _():
            for copy in copies:
                copy.wait()


def patch(plan, held, after, tail_new):
    hbm = pl.BlockSpec(memory_space=pl.ANY)
    count = len(held)
    return pl.pallas_call(
        functools.partial(patch_kernel, count),
        out_shape=jax.ShapeDtypeStruct(tail_new.shape, BF16),
        in_specs=[hbm] * (3 + count),
        out_specs=hbm,
        scratch_shapes=[
            pltpu.SMEM(plan.shape, jnp.int32),
            pltpu.VMEM(held[0].shape, BF16),
            pltpu.SemaphoreType.DMA((1,)),
            pltpu.SemaphoreType.DMA((1,)),
            pltpu.SemaphoreType.DMA((2 * MIG,)),
        ],
        input_output_aliases={2 + count: 0},
        compiler_params=pltpu.CompilerParams(vmem_limit_bytes=VMEM_BYTES),
        cost_estimate=pl.CostEstimate(flops=0, bytes_accessed=0, transcendentals=0),
        name="patch",
    )(plan, *held, after, tail_new)


def body(
    hidden_in, prompt_kv, tail_kv, group_of, prompt_len, tail_len, bucket_of, bias_table,
    attn_gain, w_query, w_key, w_value, w_out, ffn_gain, router_weight, expert_ids,
    w_gate, w_up, w_down, new_slot,
):
    rows, width = hidden_in.shape
    replicas = lax.axis_size("req")
    pieces = lax.axis_size("tp")
    experts = router_weight.shape[1]
    cap = -(-(5 * rows * TOP // (4 * experts)) // 16) * 16
    half = width // 2

    def across(axis, size, k):
        return lambda v: lax.ppermute(v, axis, [(i, i ^ k) for i in range(size)])

    def over_req(k):
        return across("req", replicas, k)

    def over_tp(k):
        return across("tp", pieces, k)

    wouts = [w_out] + [over_tp(k)(w_out) for k in range(1, pieces)]
    head_out, tail_new, packet = attention(
        hidden_in, prompt_kv, tail_kv, group_of, prompt_len, tail_len, bucket_of, bias_table,
        attn_gain, w_query, w_key, w_value, new_slot,
    )
    heads = [head_out] + [over_tp(k)(head_out) for k in range(1, pieces)]
    slots = new_slot.reshape(replicas, rows)
    place, extra, wide, kron, plan = make_plan(
        slots, expert_ids, experts, cap, [head_out] + wouts[1:]
    )
    bits = replicas.bit_length() - 1
    held = [packet, over_req(1 << (bits - 1))(packet)]
    resid, *blocks = dispatch(
        heads, wouts, hidden_in, ffn_gain, place, extra, wide, held[1], replicas
    )
    own = [blocks[0]] + [over_req(k)(blocks[k]) for k in range(1, replicas)]
    pair = [over_tp(1)(b) for b in own]
    keep, give = expert(own, pair, w_gate, w_up, w_down)
    back = give_back(keep, over_tp(1)(give), kron, cap, replicas)
    for i in range(1, bits - 1):
        held = held + [over_req(1 << (bits - 1 - i))(p) for p in held]
    last = choose(plan, held, back[0])
    held.append(over_req(1)(last))
    first, second, gate, resid_new = make_gates(
        own, pair, last, resid, slots, expert_ids, ffn_gain, router_weight, cap
    )
    result = [back[0]] + [over_req(k)(back[k]) for k in range(1, replicas)]
    mixed = combine(result, first, second, gate)
    new_tail_kv = patch(plan, held, mixed, tail_new)
    k = 2
    while k < pieces:
        other = over_tp(k)(mixed)
        mixed = mixed.astype(F32) + other.astype(F32)
        k *= 2
        if k < pieces:
            mixed = mixed.astype(BF16)
    out_half = (resid_new.astype(F32) + mixed.astype(F32)).astype(BF16)
    out_other = over_tp(1)(out_half)
    core = lax.axis_index("tp") & 1
    out_hidden = jnp.where(
        core == 0,
        jnp.concatenate([out_half, out_other], axis=1),
        jnp.concatenate([out_other, out_half], axis=1),
    )
    return (out_hidden, new_tail_kv)


def solution(mesh):
    return jax.shard_map(
        body,
        mesh=mesh,
        in_specs=(
            P("req", None), P(None, "req", None, "tp"), P(None, "req", None, "tp"),
            P("req"), P("req"), P("req"), P(), P(None, "tp"), P(),
            P(None, "tp"), P(None, "tp"), P(None, "tp"), P("tp", None), P(), P(),
            P("req", None), P("req", None, "tp"), P("req", None, "tp"), P("req", "tp", None), P(),
        ),
        out_specs=(P("req", None), P(None, "req", None, "tp")),
        check_vma=False,
    )
```

```python
import functools
import jax
import jax.numpy as jnp
from jax import lax
from jax.experimental import pallas as pl
from jax.experimental.pallas import tpu as pltpu
from jax.sharding import PartitionSpec as P

HD = 64
EPS = 1e-06
F32 = jnp.float32
BF16 = jnp.bfloat16
NT = (((1,), (1,)), ((), ()))
LANES = 128
TILE = 64
TOP = 2
MIG = 4
EXTRA = 16
VMEM_BYTES = 64 * 1024 * 1024


def iota(shape, dim):
    return lax.broadcasted_iota(jnp.int32, shape, dim)


def onehot(hit):
    return hit.astype(F32).astype(BF16)


def attention_kernel(
    group_hbm, plen_hbm, tlen_hbm, group_row_hbm, bucket_hbm, bias_hbm,
    q_hbm, knew_hbm, vnew_hbm, prompt_hbm, tail_hbm,
    head_ref, tail_out,
    group_sm, plen_sm, tlen_sm, perm_sm, group_row, bucket_row, bias_rows, perm_v,
    pk_v, pv_v, kbuf, vbuf,
    q_v, knew_v, vnew_v, table, s_p, s_t, w_p, o_v, sorted_v, qbd_v,
    small_sem, w_sem, p_sem, in_sem, out_sem, perm_sem,
):
    rows = q_v.shape[0]
    groups, prompt_rows, cols = pv_v.shape
    tail_rows = kbuf.shape[1]
    heads = cols // HD
    per8 = 8 // heads
    per16 = 16 // heads
    width_t = per8 * tail_rows
    span_end = prompt_rows + tail_rows
    tile_rows = TILE * heads
    tiles = rows // TILE

    small = [
        pltpu.make_async_copy(src, dst, small_sem.at[i])
        for i, (src, dst) in enumerate(
            (
                (group_hbm, group_sm), (plen_hbm, plen_sm), (tlen_hbm, tlen_sm),
                (group_row_hbm, group_row), (bucket_hbm, bucket_row.at[0]),
                (bias_hbm, bias_rows),
            )
        )
    ]
    weights = [
        pltpu.make_async_copy(src, dst, w_sem.at[i])
        for i, (src, dst) in enumerate(
            ((q_hbm, q_v), (knew_hbm, knew_v), (vnew_hbm, vnew_v))
        )
    ]
    prompts = [
        pltpu.make_async_copy(prompt_hbm.at[0], pk_v, p_sem.at[0]),
        pltpu.make_async_copy(prompt_hbm.at[1], pv_v, p_sem.at[1]),
    ]

    def tile_in(t):
        at = pl.ds(t * TILE, TILE)
        return [
            pltpu.make_async_copy(tail_hbm.at[0, at], kbuf.at[at], in_sem.at[0, t]),
            pltpu.make_async_copy(tail_hbm.at[1, at], vbuf.at[at], in_sem.at[1, t]),
        ]

    def tile_out(t):
        at = pl.ds(t * TILE, TILE)
        return [
            pltpu.make_async_copy(kbuf.at[at], tail_out.at[0, at], out_sem.at[0, t]),
            pltpu.make_async_copy(vbuf.at[at], tail_out.at[1, at], out_sem.at[1, t]),
        ]

    for copy in small + weights + prompts[:1]:
        copy.start()
    for copy in small:
        copy.wait()

    for t in range(tiles):
        for copy in tile_in(t):
            copy.start()
    prompts[1].start()

    eye = onehot(iota((rows, rows), 0) == iota((rows, rows), 1))
    g_row = group_row[...]
    g_col = lax.dot_general(
        eye, jnp.broadcast_to(g_row.astype(F32), (8, rows)).astype(BF16), NT,
        preferred_element_type=F32,
    )[:, 0:1].astype(jnp.int32)
    key_row = g_row * rows + iota((1, rows), 1)
    key_col = g_col * rows + iota((rows, 1), 0)
    rank_row = jnp.sum((key_col < key_row).astype(jnp.int32), axis=0, keepdims=True)
    rank_col = jnp.sum((key_row < key_col).astype(jnp.int32), axis=1, keepdims=True)
    perm_row = jnp.sum(
        jnp.where(rank_col == iota((rows, rows), 1), iota((rows, rows), 0), 0), axis=0, keepdims=True
    )
    perm_v[...] = jnp.broadcast_to(perm_row, perm_v.shape)
    perm_copy = pltpu.make_async_copy(perm_v, perm_sm, perm_sem)
    perm_copy.start()

    span = bucket_row.shape[1]
    buckets = bias_rows.shape[1]
    below = (bucket_row[...] < iota((buckets, span), 0)).astype(jnp.int32)
    starts = jnp.sum(below, axis=1, keepdims=True)
    bias = jnp.concatenate([bias_rows[...]] * per8, axis=0)
    distance = span_end - iota(table.shape, 1)
    found = jnp.broadcast_to(bias[:, 0:1], table.shape)
    for k in range(1, buckets):
        found = jnp.where(distance >= starts[k : k + 1, 0:1], bias[:, k : k + 1], found)
    table[...] = found

    for copy in weights:
        copy.wait()
    perm_copy.wait()

    lane = iota((8, LANES), 1)
    sub = iota((8, LANES), 0)
    row16 = iota((16, cols), 0)
    minus = jnp.float32(-jnp.inf)
    pieces = prompt_rows // LANES

    def build_bias(tile):
        def step(i, carry):
            base = tile * TILE + i * per8
            out_p = [jnp.full((8, LANES), minus) for _ in range(pieces)]
            out_t = [jnp.full((8, LANES), minus) for _ in range(width_t // LANES)]
            for j in range(per8):
                r = perm_sm[0, base + j]
                length = tlen_sm[r]
                plen = plen_sm[group_sm[r]]
                start = span_end - plen - length
                block = start // LANES
                off = start - block * LANES
                mine = (sub >= j * heads) & (sub < (j + 1) * heads)
                window = table[:, pl.ds(pl.multiple_of(block * LANES, LANES), prompt_rows + LANES)]
                turn = jnp.where(off == 0, 0, LANES - off)
                turned = [
                    pltpu.roll(window[:, k * LANES : (k + 1) * LANES], turn, 1)
                    for k in range(pieces + 1)
                ]
                for k in range(pieces):
                    here = jnp.where(lane < LANES - off, turned[k], turned[k + 1])
                    out_p[k] = jnp.where(mine & (lane < plen - k * LANES), here, out_p[k])
                place = j * tail_rows
                k = place // LANES
                place = place - k * LANES
                own = table[:, prompt_rows : prompt_rows + LANES]
                shift = place - (tail_rows - length)
                shift = jnp.where(shift < 0, shift + LANES, shift)
                own = pltpu.roll(own, shift, 1)
                live = mine & (lane >= place) & (lane <= place + length)
                out_t[k] = jnp.where(live, own, out_t[k])
            at = pl.ds(pl.multiple_of(tile * tile_rows + i * 8, 8), 8)
            for k in range(pieces):
                s_p[at, k * LANES : (k + 1) * LANES] = out_p[k]
            for k in range(width_t // LANES):
                s_t[at, k * LANES : (k + 1) * LANES] = out_t[k]
            return carry

        lax.fori_loop(0, TILE // per8, step, 0, unroll=8)

    def insert(t):
        def step(i, carry):
            r = t * TILE + i
            length = tlen_sm[r]
            first = pl.multiple_of(length // 16 * 16, 16)
            hit = row16 == length - first
            for new, buf in ((knew_v, kbuf), (vnew_v, vbuf)):
                fresh = jnp.broadcast_to(new[pl.ds(r, 1), :], (16, cols))
                old = buf[r, pl.ds(first, 16), :].astype(F32)
                buf[r, pl.ds(first, 16), :] = jnp.where(hit, fresh, old).astype(BF16)
            return carry

        lax.fori_loop(0, TILE, step, 0, unroll=8)

    own_head = iota((tile_rows, cols), 0) % heads == iota((tile_rows, cols), 1) // HD
    spread_row = iota((tile_rows, rows), 0) // heads
    first_head = iota((TILE, LANES), 1) < HD

    def spread_of(tile):
        return onehot(rank_row == spread_row + tile * TILE)

    def member_of(tile):
        group8 = jnp.broadcast_to(g_row.astype(F32), (8, rows)).astype(BF16)
        return lax.dot_general(
            spread_of(tile), group8, NT, preferred_element_type=F32
        )[:, 0:1].astype(jnp.int32)

    def group_range(tile):
        low = group_sm[perm_sm[0, tile * TILE]]
        high = group_sm[perm_sm[0, tile * TILE + TILE - 1]]
        return low, high + 1

    def scores(tile, carry):
        build_bias(tile)
        at = pl.ds(pl.multiple_of(tile * tile_rows, tile_rows), tile_rows)
        qrep = jnp.dot(spread_of(tile), q_v[...], preferred_element_type=F32)
        qbd = jnp.where(own_head, qrep, 0.0)
        qbd_v[at, :] = qbd.astype(BF16)
        member = member_of(tile)

        @pl.when(tile == 0)
        def _():
            prompts[0].wait()

        def one_group(g, carry):
            part = jnp.where(member == g, qbd, 0.0).astype(BF16)
            s_p[at, :] += lax.dot_general(part, pk_v[g], NT, preferred_element_type=F32)
            return carry

        low, high = group_range(tile)
        lax.fori_loop(low, high, one_group, 0)
        for copy in tile_in(tile):
            copy.wait()
        insert(tile)
        for copy in tile_out(tile):
            copy.start()
        return carry

    lax.fori_loop(0, tiles, scores, 0)
    prompts[1].wait()

    def gathered(buf, first):
        return jnp.concatenate([buf[perm_sm[0, first + j]] for j in range(per16)], axis=0)

    def values(tile, carry):
        base = pl.multiple_of(tile * tile_rows, tile_rows)
        at = pl.ds(base, tile_rows)
        for i in range(TILE // per16):
            keys = gathered(kbuf, tile * TILE + i * per16)
            here = pl.ds(pl.multiple_of(base + i * 16, 16), 16)
            got = lax.dot_general(qbd_v[here, :], keys, NT, preferred_element_type=F32)
            upper = pl.ds(pl.multiple_of(base + i * 16, 8), 8)
            lower = pl.ds(pl.multiple_of(base + i * 16 + 8, 8), 8)
            s_t[upper, :] += got[:8, :width_t]
            s_t[lower, :] += got[8:, width_t:]
        prompt_s = s_p[at, :]
        tail_s = s_t[at, :]
        top = jnp.maximum(
            jnp.max(prompt_s, axis=1, keepdims=True), jnp.max(tail_s, axis=1, keepdims=True)
        )
        pe = jnp.exp(prompt_s - top)
        te = jnp.exp(tail_s - top)
        total = jnp.sum(pe, axis=1, keepdims=True) + jnp.sum(te, axis=1, keepdims=True)
        part = 1.0 / total
        w_p[...] = (pe * part).astype(BF16)
        tw = te * part
        none = jnp.zeros((8, width_t), F32)
        for i in range(TILE // per16):
            row = i * 16
            upper = jnp.concatenate([tw[row : row + 8], none], axis=1)
            lower = jnp.concatenate([none, tw[row + 8 : row + 16]], axis=1)
            both = jnp.concatenate([upper, lower], axis=0).astype(BF16)
            vals = gathered(vbuf, tile * TILE + i * per16)
            o_t = jnp.dot(both, vals, preferred_element_type=F32)
            for b in range(cols // LANES):
                o_v[b, row : row + 16, :] = o_t[:, b * LANES : (b + 1) * LANES]
        member = member_of(tile)

        def one_group(g, carry):
            w = jnp.where(member == g, w_p[...].astype(F32), 0.0).astype(BF16)
            o_p = jnp.dot(w, pv_v[g], preferred_element_type=F32)
            for b in range(cols // LANES):
                o_v[b] += o_p[:, b * LANES : (b + 1) * LANES]
            return carry

        low, high = group_range(tile)
        lax.fori_loop(low, high, one_group, 0)
        to = pl.ds(pl.multiple_of(tile * TILE, TILE), TILE)
        for b in range(cols // LANES):
            even = o_v[b, pl.ds(2 * b, TILE, stride=heads), :]
            odd = o_v[b, pl.ds(2 * b + 1, TILE, stride=heads), :]
            sorted_v[to, b * LANES : (b + 1) * LANES] = jnp.where(first_head, even, odd).astype(BF16)
        return carry

    lax.fori_loop(0, tiles, values, 0)
    unsort = onehot(rank_col == iota((rows, rows), 1))
    head_ref[...] = jnp.dot(unsort, sorted_v[...], preferred_element_type=F32).astype(BF16)
    for t in range(tiles):
        for copy in tile_out(t):
            copy.wait()


def project_kernel(
    slots_hbm, tlen_hbm, hidden_hbm, gain_hbm, wq_hbm, wk_hbm, wv_hbm, tail_hbm,
    q_ref, knew_ref, vnew_ref, packet_ref,
    slots_sm, tlen_sm, mover_sm, hidden_v, gain_v, wq_v, wk_v, wv_v, sem, slab_sem,
):
    rows = hidden_v.shape[0]
    cols = wq_v.shape[1]
    early = [
        pltpu.make_async_copy(slots_hbm, slots_sm, sem.at[0]),
        pltpu.make_async_copy(tlen_hbm, tlen_sm, sem.at[1]),
    ]
    late = [
        pltpu.make_async_copy(src, dst, sem.at[2 + i])
        for i, (src, dst) in enumerate(
            (
                (hidden_hbm, hidden_v), (gain_hbm, gain_v),
                (wq_hbm, wq_v), (wk_hbm, wk_v), (wv_hbm, wv_v),
            )
        )
    ]
    for copy in early + late:
        copy.start()
    for copy in early:
        copy.wait()
    base = lax.axis_index("req") * rows
    for m in range(MIG + 1):
        mover_sm[m] = 0

    def look(i, count):
        mover_sm[count] = i
        return count + (slots_sm[base + i] != base + i).astype(jnp.int32)

    lax.fori_loop(0, rows, look, 0, unroll=16)
    slabs = [
        pltpu.make_async_copy(
            tail_hbm.at[side, mover_sm[m]], packet_ref.at[2 * m + side], slab_sem.at[2 * m + side]
        )
        for m in range(MIG)
        for side in range(2)
    ]
    for copy in slabs:
        copy.start()
    for copy in late:
        copy.wait()
    v = hidden_v[...].astype(F32)
    normed = (
        v * lax.rsqrt(jnp.mean(v * v, axis=-1, keepdims=True) + EPS) * gain_v[...]
    ).astype(BF16)
    query = jnp.dot(normed, wq_v[...], preferred_element_type=F32).astype(BF16)
    q_ref[...] = query * jnp.asarray(HD ** (-0.5), BF16)
    for new, w in ((knew_ref, wk_v), (vnew_ref, wv_v)):
        new[...] = jnp.dot(normed, w[...], preferred_element_type=F32).astype(BF16).astype(F32)
    for copy in slabs:
        copy.wait()
    at = iota((packet_ref.shape[1], cols), 0)
    for m in range(MIG):
        r = mover_sm[m]
        for side, new in enumerate((knew_ref, vnew_ref)):
            old = packet_ref[2 * m + side].astype(F32)
            packet_ref[2 * m + side] = jnp.where(
                at == tlen_sm[r], new[pl.ds(r, 1), :], old
            ).astype(BF16)


def project(new_slot, tail_len, hidden_in, gain, w_query, w_key, w_value, tail_kv):
    rows, width = hidden_in.shape
    cols = w_query.shape[1]
    tail_rows = tail_kv.shape[2]
    vm = pl.BlockSpec(memory_space=pltpu.VMEM)
    hbm = pl.BlockSpec(memory_space=pl.ANY)
    return pl.pallas_call(
        project_kernel,
        out_shape=(
            jax.ShapeDtypeStruct((rows, cols), BF16),
            jax.ShapeDtypeStruct((rows, cols), F32),
            jax.ShapeDtypeStruct((rows, cols), F32),
            jax.ShapeDtypeStruct((2 * MIG, tail_rows, cols), BF16),
        ),
        in_specs=[hbm] * 8,
        out_specs=(vm,) * 4,
        scratch_shapes=[
            pltpu.SMEM(new_slot.shape, jnp.int32),
            pltpu.SMEM(tail_len.shape, jnp.int32),
            pltpu.SMEM((MIG + 1,), jnp.int32),
            pltpu.VMEM((rows, width), BF16),
            pltpu.VMEM((1, width), F32),
            pltpu.VMEM((width, cols), BF16),
            pltpu.VMEM((width, cols), BF16),
            pltpu.VMEM((width, cols), BF16),
            pltpu.SemaphoreType.DMA((7,)),
            pltpu.SemaphoreType.DMA((2 * MIG,)),
        ],
        compiler_params=pltpu.CompilerParams(vmem_limit_bytes=VMEM_BYTES),
        cost_estimate=pl.CostEstimate(flops=400_000_000, bytes_accessed=3_000_000, transcendentals=0),
        name="project",
    )(new_slot, tail_len, hidden_in, gain[None, :], w_query, w_key, w_value, tail_kv)


def attention(
    query, key_new, value_new, prompt_kv, tail_kv, group_of, prompt_len, tail_len, bucket_of,
    bias_table,
):
    rows, cols = query.shape
    heads = cols // HD
    groups, prompt_rows = prompt_kv.shape[1:3]
    tail_rows = tail_kv.shape[2]
    span = bucket_of.shape[0]
    buckets = bias_table.shape[0]
    table_width = 2 * prompt_rows + LANES
    width_t = 8 // heads * tail_rows
    tiles = rows // TILE
    vm = pl.BlockSpec(memory_space=pltpu.VMEM)
    hbm = pl.BlockSpec(memory_space=pl.ANY)
    return pl.pallas_call(
        attention_kernel,
        out_shape=(
            jax.ShapeDtypeStruct((rows, cols), BF16),
            jax.ShapeDtypeStruct(tail_kv.shape, BF16),
        ),
        in_specs=[hbm] * 11,
        out_specs=(vm, hbm),
        scratch_shapes=[
            pltpu.SMEM((rows,), jnp.int32),
            pltpu.SMEM((groups,), jnp.int32),
            pltpu.SMEM((rows,), jnp.int32),
            pltpu.SMEM((8, rows), jnp.int32),
            pltpu.VMEM((1, rows), jnp.int32),
            pltpu.VMEM((1, span), jnp.int32),
            pltpu.VMEM((heads, buckets), F32),
            pltpu.VMEM((8, rows), jnp.int32),
            pltpu.VMEM((groups, prompt_rows, cols), BF16),
            pltpu.VMEM((groups, prompt_rows, cols), BF16),
            pltpu.VMEM((rows, tail_rows, cols), BF16),
            pltpu.VMEM((rows, tail_rows, cols), BF16),
            pltpu.VMEM((rows, cols), BF16),
            pltpu.VMEM((rows, cols), F32),
            pltpu.VMEM((rows, cols), F32),
            pltpu.VMEM((8, table_width), F32),
            pltpu.VMEM((rows * heads, prompt_rows), F32),
            pltpu.VMEM((rows * heads, width_t), F32),
            pltpu.VMEM((TILE * heads, prompt_rows), BF16),
            pltpu.VMEM((cols // LANES, TILE * heads, LANES), F32),
            pltpu.VMEM((rows, cols), BF16),
            pltpu.VMEM((rows * heads, cols), BF16),
            pltpu.SemaphoreType.DMA((6,)),
            pltpu.SemaphoreType.DMA((3,)),
            pltpu.SemaphoreType.DMA((2,)),
            pltpu.SemaphoreType.DMA((2, tiles)),
            pltpu.SemaphoreType.DMA((2, tiles)),
            pltpu.SemaphoreType.DMA,
        ],
        compiler_params=pltpu.CompilerParams(vmem_limit_bytes=VMEM_BYTES),
        cost_estimate=pl.CostEstimate(flops=8_000_000_000, bytes_accessed=45_000_000, transcendentals=700_000),
        name="attention",
    )(
        group_of, prompt_len, tail_len, group_of[None, :], bucket_of, bias_table.T,
        query, key_new, value_new, prompt_kv, tail_kv,
    )


def block_rows(cap):
    return cap + EXTRA


def low_part(replicas):
    bits = (replicas.bit_length() - 1) // 2
    return bits, 1 << bits


def plan_kernel(cap, slots_ref, ids_ref, *refs):
    place_ref, extra_ref, wide_ref, kron_ref, plan_ref, slot_s = refs[-6:]
    replicas, rows = slots_ref.shape
    experts = slot_s.shape[0]
    size = place_ref.shape[0] // replicas
    me = lax.axis_index("req")
    ns = slots_ref[...]
    at_sub = iota((replicas, rows), 0)
    at_lane = iota((replicas, rows), 1)
    moved = ns != at_sub * rows + at_lane
    tri = (iota((rows, rows), 0) < iota((rows, rows), 1)).astype(BF16)
    rank = jnp.dot(moved.astype(F32).astype(BF16), tri, preferred_element_type=F32).astype(jnp.int32)
    going_to = ns // rows
    mine = at_sub == me

    def own(values):
        return jnp.sum(jnp.where(mine, values, 0), axis=0, keepdims=True)

    moved_me = own(moved.astype(jnp.int32))
    rank_me = own(rank)
    to_me = own(going_to)
    ids_rows = ids_ref[...]
    at_e = iota((experts, rows), 0)
    hit = (ids_rows[0:1] == at_e) | (ids_rows[1:2] == at_e)
    normal = (hit & (moved_me == 0)).astype(F32).astype(BF16)
    slot = jnp.dot(normal, tri, preferred_element_type=F32).astype(jnp.int32)
    slot_s[...] = jnp.where(hit, jnp.where(moved_me > 0, cap + rank_me, slot), -1)
    at_row = iota((size, rows), 0)
    at_extra = iota((EXTRA, rows), 0)
    for k in range(replicas):
        e = me ^ k
        block = pl.ds(k * size, size)
        row = slot_s[pl.ds(e, 1), :]
        leaving = jnp.where((moved_me > 0) & (to_me == e), rank_me, -100)
        place_ref[block, :] = onehot(at_row == row)
        more = pl.ds(k * EXTRA, EXTRA)
        extra_ref[more, 0:rows] = onehot(at_extra == leaving + MIG)
        extra_ref[more, rows:] = onehot(at_extra == leaving + 2 * MIG)
    lane = iota(wide_ref.shape, 1)
    eye = onehot(iota((rows, rows), 0) == iota((rows, rows), 1))
    facts = jnp.concatenate([ids_rows, jnp.zeros((6, rows), jnp.int32)], axis=0)
    columns = lax.dot_general(
        eye, facts.astype(F32).astype(BF16), NT, preferred_element_type=F32
    )
    wide = jnp.where(lane == 0, columns[:, 0:1], jnp.where(lane == 1, columns[:, 1:2], 0.0))
    wide_ref[...] = wide.astype(BF16)
    dest = jnp.max(jnp.where(moved, going_to, -1), axis=1, keepdims=True)
    dest = jnp.where(dest < 0, iota((replicas, 1), 0), dest)
    hot = (dest == iota((replicas, replicas), 1)).astype(F32).astype(BF16)
    span = replicas * EXTRA
    mixed_row = (iota((span, replicas), 0) // EXTRA) ^ me
    a = (mixed_row == iota((span, replicas), 1)).astype(F32).astype(BF16)
    by_source = lax.dot_general(a, hot, NT, preferred_element_type=F32).astype(BF16)
    pairs = lax.dot_general(by_source, a, NT, preferred_element_type=F32)
    same = iota((span, span), 0) % EXTRA == iota((span, span), 1) % EXTRA
    kron_ref[...] = jnp.where(same, pairs, 0.0).astype(BF16)
    sub1 = iota((replicas, 1), 0)

    def source_of(who):
        return jnp.sum(jnp.where(dest == who, sub1, 0), axis=0, keepdims=True)

    low_bits, low = low_part(replicas)
    diff = source_of(me) ^ me
    turn = diff & (low - 1)
    final = jnp.where(turn == 0, diff >> low_bits, (replicas >> low_bits) + turn - 1)
    lane8 = iota((8, LANES), 1)
    plan = jnp.where(lane8 == 0, final, -1)
    for j in range(1, low):
        apart = source_of(me ^ j) ^ me
        plan = jnp.where(lane8 == 24 + j, apart >> low_bits, plan)
    lane1 = iota((1, rows), 1)
    for m in range(MIG):
        is_m = (moved_me > 0) & (rank_me == m)
        mover = jnp.sum(jnp.where(is_m, lane1, 0), axis=1, keepdims=True)
        plan = jnp.where(lane8 == 8 + m, mover, plan)
        come = moved & (going_to == me) & (rank == m)
        to = jnp.sum(jnp.where(come, ns - me * rows + 1, 0), axis=1, keepdims=True)
        to = jnp.sum(to, axis=0, keepdims=True) - 1
        plan = jnp.where(lane8 == 16 + m, to, plan)
    plan_ref[...] = plan


def make_plan(slots, expert_ids, experts, cap, after):
    replicas, rows = slots.shape
    size = block_rows(cap)
    vm = pl.BlockSpec(memory_space=pltpu.VMEM)
    span = replicas * EXTRA
    return pl.pallas_call(
        functools.partial(plan_kernel, cap),
        out_shape=(
            jax.ShapeDtypeStruct((replicas * size, rows), BF16),
            jax.ShapeDtypeStruct((replicas * EXTRA, 2 * rows), BF16),
            jax.ShapeDtypeStruct((rows, LANES), BF16),
            jax.ShapeDtypeStruct((span, span), BF16),
            jax.ShapeDtypeStruct((8, LANES), jnp.int32),
        ),
        in_specs=[vm, vm] + [pl.BlockSpec(memory_space=pl.ANY)] * len(after),
        out_specs=(vm,) * 5,
        scratch_shapes=[pltpu.VMEM((experts, rows), jnp.int32)],
        compiler_params=pltpu.CompilerParams(vmem_limit_bytes=VMEM_BYTES),
        cost_estimate=pl.CostEstimate(flops=0, bytes_accessed=0, transcendentals=0),
        name="plan",
    )(slots, expert_ids.T, *after)


def load(sem, *pairs):
    made = [pltpu.make_async_copy(src, dst, sem.at[i]) for i, (src, dst) in enumerate(pairs)]
    for copy in made:
        copy.start()
    for copy in made:
        copy.wait()


def norm(values, gain):
    v = values.astype(F32)
    return (v * lax.rsqrt(jnp.mean(v * v, axis=-1, keepdims=True) + EPS) * gain).astype(BF16)


def far_part(replicas, pieces):
    return replicas // 2, replicas // pieces


def dispatch_kernel(pieces, replicas, *refs):
    near, each = far_part(replicas, pieces)
    count = near + each
    heads_hbm = refs[:pieces]
    wout_hbm = refs[pieces : 2 * pieces]
    hidden_hbm, gain_ref, place_hbm, extra_hbm, wide_hbm = refs[2 * pieces : 2 * pieces + 5]
    refs = refs[-11 - count :]
    resid_ref = refs[0]
    outs = refs[1 : 1 + count]
    head_v, wout_v, stack, hidden_ref, place_ref, extra_ref, wide_ref, extra_v, sem, more = refs[1 + count :]
    tp = lax.axis_index("tp")
    core = tp & 1
    rows, width = hidden_ref.shape
    cols = width // pieces
    half = width // 2

    def copies():
        made = []
        for k in range(pieces):
            at = pl.ds(pl.multiple_of((tp ^ k) * cols, cols), cols)
            made.append(pltpu.make_async_copy(wout_hbm[k], wout_v.at[at], sem.at[0, k]))
            made.append(pltpu.make_async_copy(heads_hbm[k], head_v.at[:, at], sem.at[1, k]))
        made.append(pltpu.make_async_copy(hidden_hbm, hidden_ref, more.at[0]))
        return made

    late = [
        pltpu.make_async_copy(place_hbm, place_ref, more.at[1]),
        pltpu.make_async_copy(extra_hbm, extra_ref, more.at[2]),
        pltpu.make_async_copy(wide_hbm, wide_ref, more.at[3]),
    ]

    for copy in copies() + late:
        copy.start()
    for copy in copies():
        copy.wait()
    attn = jnp.dot(head_v[...], wout_v[...], preferred_element_type=F32)
    resid = (hidden_ref[...].astype(F32) + attn).astype(BF16)
    resid_ref[...] = resid
    normed = norm(resid, gain_ref[...])
    first = core == 0
    stack[0:rows, :] = jnp.where(first, normed[:, :half], normed[:, half:])
    stack[rows : 2 * rows, :] = jnp.where(first, resid[:, :half], resid[:, half:])
    for copy in late:
        copy.wait()
    size = place_ref.shape[0] // replicas
    extra_v[...] = jnp.dot(extra_ref[:, 0:rows], stack[rows:, :], preferred_element_type=F32)
    extra_v[:, 0:LANES] += jnp.dot(extra_ref[:, rows:], wide_ref[...], preferred_element_type=F32)
    for i in range(count):
        k = i if i < near else near + (tp >> 1) * each + (i - near)
        block = jnp.dot(
            place_ref[pl.ds(k * size, size), :], stack[0:rows, :], preferred_element_type=F32
        )
        outs[i][0 : size - EXTRA, :] = block[: size - EXTRA].astype(BF16)
        outs[i][size - EXTRA :, :] = (
            block[size - EXTRA :] + extra_v[pl.ds(k * EXTRA, EXTRA), :]
        ).astype(BF16)


def dispatch(heads, wouts, hidden, gain, place, extra, wide, after, replicas):
    rows, width = hidden.shape
    pieces = len(heads)
    count = sum(far_part(replicas, pieces))
    half = width // 2
    size = place.shape[0] // replicas
    vm = pl.BlockSpec(memory_space=pltpu.VMEM)
    hbm = pl.BlockSpec(memory_space=pl.ANY)
    return pl.pallas_call(
        functools.partial(dispatch_kernel, pieces, replicas),
        out_shape=(jax.ShapeDtypeStruct((rows, width), BF16),)
        + tuple(jax.ShapeDtypeStruct((size, half), BF16) for _ in range(count)),
        in_specs=[hbm] * (2 * pieces) + [hbm, vm, hbm, hbm, hbm] + [hbm] * len(after),
        out_specs=(vm,) * (1 + count),
        scratch_shapes=[
            pltpu.VMEM((rows, width), BF16),
            pltpu.VMEM((width, width), BF16),
            pltpu.VMEM((2 * rows, half), BF16),
            pltpu.VMEM((rows, width), BF16),
            pltpu.VMEM(place.shape, BF16),
            pltpu.VMEM(extra.shape, BF16),
            pltpu.VMEM(wide.shape, BF16),
            pltpu.VMEM((extra.shape[0], half), F32),
            pltpu.SemaphoreType.DMA((2, pieces)),
            pltpu.SemaphoreType.DMA((5,)),
        ],
        compiler_params=pltpu.CompilerParams(vmem_limit_bytes=VMEM_BYTES),
        cost_estimate=pl.CostEstimate(flops=1_200_000_000, bytes_accessed=6_000_000, transcendentals=0),
        name="dispatch",
    )(*heads, *wouts, hidden, gain[None, :], place, extra, wide, *after)


def pieces_of(total, step):
    return [(at, min(step, total - at)) for at in range(0, total, step)]


def expert_kernel(replicas, pieces, *refs):
    own = refs[:replicas]
    pair = refs[replicas : 2 * replicas]
    wg_hbm, wu_hbm, wd_hbm = refs[2 * replicas : 2 * replicas + 3]
    keep_ref, give_ref, x_own, x_pair, wg, wu, wd, act, sem, xsem = refs[-10:]
    tp = lax.axis_index("tp")
    core = tp & 1
    size, half = own[0].shape
    near, each = far_part(replicas, pieces)
    hidden = wg.shape[0]
    chunks = pieces_of(hidden, 256)
    blocks = []
    for k in range(replicas):
        there = k
        if k >= near:
            turn, f = divmod(k - near, each)
            there = near + ((tp >> 1) ^ turn) * each + f
        at = pl.ds(there * size, size)
        blocks.append(pltpu.make_async_copy(own[k], x_own.at[at], xsem.at[0, k]))
        blocks.append(pltpu.make_async_copy(pair[k], x_pair.at[at], xsem.at[1, k]))
    wide = [
        [
            pltpu.make_async_copy(src.at[0, pl.ds(at, n)], dst.at[pl.ds(at, n)], sem.at[side, c])
            for side, (src, dst) in enumerate(((wg_hbm, wg), (wu_hbm, wu)))
        ]
        for c, (at, n) in enumerate(chunks)
    ]
    down = pltpu.make_async_copy(wd_hbm.at[0], wd, sem.at[2, 0])
    for copy in wide[0] + blocks + sum(wide[1:], []) + [down]:
        copy.start()
    for copy in blocks:
        copy.wait()
    here = pl.ds(pl.multiple_of(core * half, half), half)
    there = pl.ds(pl.multiple_of((1 - core) * half, half), half)
    a, b = x_own[...], x_pair[...]

    def product(w, rows):
        return lax.dot_general(a, w[rows, here], NT, preferred_element_type=F32) + lax.dot_general(
            b, w[rows, there], NT, preferred_element_type=F32
        )

    for c, (at, n) in enumerate(chunks):
        for copy in wide[c]:
            copy.wait()
        rows = pl.ds(at, n)
        gate = product(wg, rows)
        act[:, at : at + n] = (jax.nn.gelu(gate, approximate=True) * product(wu, rows)).astype(BF16)
    down.wait()
    give_ref[...] = jnp.dot(act[...], wd[:, there], preferred_element_type=F32).astype(BF16)
    keep_ref[...] = jnp.dot(act[...], wd[:, here], preferred_element_type=F32).astype(BF16)


def expert(own, pair, w_gate, w_up, w_down, pieces):
    replicas = len(own)
    size, half = own[0].shape
    _, width, hidden = w_gate.shape
    total = replicas * size
    vm = pl.BlockSpec(memory_space=pltpu.VMEM)
    hbm = pl.BlockSpec(memory_space=pl.ANY)
    shape = jax.ShapeDtypeStruct((total, half), BF16)
    return pl.pallas_call(
        functools.partial(expert_kernel, replicas, pieces),
        out_shape=(shape, shape),
        in_specs=[hbm] * (2 * replicas + 3),
        out_specs=(vm, vm),
        scratch_shapes=[
            pltpu.VMEM((total, half), BF16),
            pltpu.VMEM((total, half), BF16),
            pltpu.VMEM((hidden, width), BF16),
            pltpu.VMEM((hidden, width), BF16),
            pltpu.VMEM((hidden, width), BF16),
            pltpu.VMEM((total, hidden), BF16),
            pltpu.SemaphoreType.DMA((3, len(pieces_of(hidden, 256)))),
            pltpu.SemaphoreType.DMA((2, replicas)),
        ],
        compiler_params=pltpu.CompilerParams(vmem_limit_bytes=VMEM_BYTES),
        cost_estimate=pl.CostEstimate(flops=3_400_000_000, bytes_accessed=8_000_000, transcendentals=600_000),
        name="expert",
    )(*own, *pair, jnp.swapaxes(w_gate, 1, 2), jnp.swapaxes(w_up, 1, 2), w_down)


def give_back_kernel(cap, keep_hbm, got_hbm, kron_hbm, *refs):
    replicas = len(refs) - 5
    outs = refs[:replicas]
    rows_v, keep_ref, got_ref, kron_ref, sem = refs[replicas:]
    load(sem, (keep_hbm, keep_ref), (got_hbm, got_ref), (kron_hbm, kron_ref))
    size = outs[0].shape[0]
    for k in range(replicas):
        at = slice(k * size, (k + 1) * size)
        both = keep_ref[at, :].astype(F32) + got_ref[at, :].astype(F32)
        outs[k][...] = both.astype(BF16)
        rows_v[k * EXTRA : (k + 1) * EXTRA, :] = both[size - EXTRA :].astype(BF16)
    moved = jnp.dot(kron_ref[...], rows_v[...], preferred_element_type=F32)
    first = iota((EXTRA, 1), 0) >= cap - (size - EXTRA)
    for k in range(replicas):
        at = slice(k * EXTRA, (k + 1) * EXTRA)
        outs[k][size - EXTRA :, :] = jnp.where(
            first, moved[at], rows_v[at, :].astype(F32)
        ).astype(BF16)


def give_back(keep, got, kron, cap, replicas):
    total, half = keep.shape
    size = total // replicas
    vm = pl.BlockSpec(memory_space=pltpu.VMEM)
    hbm = pl.BlockSpec(memory_space=pl.ANY)
    return pl.pallas_call(
        functools.partial(give_back_kernel, cap),
        out_shape=tuple(jax.ShapeDtypeStruct((size, half), BF16) for _ in range(replicas)),
        in_specs=[hbm] * 3,
        out_specs=(vm,) * replicas,
        scratch_shapes=[
            pltpu.VMEM((replicas * EXTRA, half), BF16),
            pltpu.VMEM((total, half), BF16),
            pltpu.VMEM((total, half), BF16),
            pltpu.VMEM(kron.shape, BF16),
            pltpu.SemaphoreType.DMA((3,)),
        ],
        compiler_params=pltpu.CompilerParams(vmem_limit_bytes=VMEM_BYTES),
        cost_estimate=pl.CostEstimate(flops=30_000_000, bytes_accessed=2_500_000, transcendentals=0),
        name="give_back",
    )(keep, got, kron)


def gates_kernel(cap, replicas, *refs):
    own = refs[:replicas]
    pair = refs[replicas : 2 * replicas]
    (after_hbm, resid_hbm, slots_ref, ids_ref, gain_ref, router_ref) = refs[
        2 * replicas : 2 * replicas + 6
    ]
    (first_ref, second_ref, gate_ref, new_ref, resid_ref, own_v, pair_v, sem) = refs[2 * replicas + 6 :]
    me = lax.axis_index("req")
    core = lax.axis_index("tp") & 1
    rows, width = resid_ref.shape
    half = width // 2
    size = own[0].shape[0]
    low = pl.ds(size - EXTRA, EXTRA)
    skip = 0
    load(
        sem,
        (resid_hbm, resid_ref),
        *[(own[k].at[low], own_v.at[k]) for k in range(replicas)],
        *[(pair[k].at[low], pair_v.at[k]) for k in range(replicas)],
    )
    ns = slots_ref[...]
    count = ns.shape[0]
    at_sub = iota((count, rows), 0)
    moved = ns != at_sub * rows + iota((count, rows), 1)
    before = (iota((rows, rows), 0) < iota((rows, rows), 1)).astype(BF16)
    movedf = moved.astype(F32)
    rank = jnp.dot(movedf.astype(BF16), before, preferred_element_type=F32)
    coming = moved & (ns // rows == me)
    slot_to = jnp.sum(jnp.where(coming, ns - me * rows + 1, 0), axis=0, keepdims=True) - 1
    rank_in = jnp.sum(jnp.where(coming, rank, 0.0), axis=0, keepdims=True).astype(jnp.int32)
    landing = (iota((rows, rows), 0) == slot_to).astype(F32).astype(BF16)
    at16 = iota((EXTRA, rows), 0)

    def taken(offset):
        hot = (at16 == rank_in + (skip + offset)) & (slot_to >= 0)
        return lax.dot_general(landing, hot.astype(F32).astype(BF16), NT, preferred_element_type=F32)

    take_resid = taken(MIG)
    take_ids = taken(2 * MIG)
    vacated = jnp.sum(take_resid, axis=1, keepdims=True) > 0.5
    in_own = own_v[0].astype(F32)
    in_pair = pair_v[0].astype(F32)
    for k in range(1, replicas):
        in_own = in_own + own_v[k].astype(F32)
        in_pair = in_pair + pair_v[k].astype(F32)
    in_own, in_pair = in_own.astype(BF16), in_pair.astype(BF16)
    first_core = core == 0
    in_low = jnp.where(first_core, in_own, in_pair)
    in_high = jnp.where(first_core, in_pair, in_own)
    picked = take_resid.astype(BF16)
    resid = resid_ref[...]
    new_low = jnp.where(
        vacated, jnp.dot(picked, in_low, preferred_element_type=F32), resid[:, :half].astype(F32)
    ).astype(BF16)
    new_high = jnp.where(
        vacated, jnp.dot(picked, in_high, preferred_element_type=F32), resid[:, half:].astype(F32)
    ).astype(BF16)
    new_ref[...] = jnp.where(first_core, new_low, new_high)
    normed = norm(jnp.concatenate([new_low, new_high], axis=1), gain_ref[...])
    logits = lax.dot_general(normed, router_ref[...], NT, preferred_element_type=F32)
    experts = logits.shape[1]
    ids_in = jnp.dot(take_ids.astype(BF16), in_low[:, :LANES], preferred_element_type=F32)
    eye = onehot(iota((rows, rows), 0) == iota((rows, rows), 1))
    mine = at_sub == me
    moved_me = jnp.sum(jnp.where(mine, movedf, 0.0), axis=0, keepdims=True)
    facts = jnp.concatenate(
        [ids_ref[...].astype(F32), moved_me, jnp.zeros((5, rows), F32)], axis=0
    ).astype(BF16)
    ids = lax.dot_general(eye, facts, NT, preferred_element_type=F32)
    moved_col = ids[:, 2:3]
    id1 = jnp.where(vacated, ids_in[:, 0:1], ids[:, 0:1]).astype(jnp.int32)
    id2 = jnp.where(vacated, ids_in[:, 1:2], ids[:, 1:2]).astype(jnp.int32)
    at_e = iota((rows, experts), 1)
    hit1, hit2 = id1 == at_e, id2 == at_e
    picked1 = jnp.sum(jnp.where(hit1, logits, 0.0), axis=1, keepdims=True)
    picked2 = jnp.sum(jnp.where(hit2, logits, 0.0), axis=1, keepdims=True)
    gate = jax.nn.sigmoid(picked1 - picked2)
    gate_ref[...] = jnp.broadcast_to(gate, gate_ref.shape)
    old1 = ids[:, 0:1].astype(jnp.int32) == at_e
    old2 = ids[:, 1:2].astype(jnp.int32) == at_e
    normal = ((old1 | old2) & (moved_col < 0.5)).astype(F32).astype(BF16)
    after = (iota((rows, rows), 0) > iota((rows, rows), 1)).astype(BF16)
    slot = jnp.dot(after, normal, preferred_element_type=F32)
    slot1 = jnp.sum(jnp.where(hit1, slot, 0.0), axis=1, keepdims=True)
    slot2 = jnp.sum(jnp.where(hit2, slot, 0.0), axis=1, keepdims=True)
    in_rank = jnp.sum(
        jnp.where(take_resid > 0.5, iota((rows, EXTRA), 1), 0), axis=1, keepdims=True
    ) - (skip + MIG)
    slot1 = jnp.where(vacated, cap + in_rank, slot1.astype(jnp.int32))
    slot2 = jnp.where(vacated, cap + in_rank, slot2.astype(jnp.int32))
    lane = iota((rows, replicas * size), 1)
    first_ref[...] = (lane == (id1 ^ me) * size + slot1).astype(F32).astype(BF16)
    second_ref[...] = (lane == (id2 ^ me) * size + slot2).astype(F32).astype(BF16)


def make_gates(own, pair, after, resid, slots, ids, gain, router, cap):
    replicas = len(own)
    size, half = own[0].shape
    rows, width = resid.shape
    vm = pl.BlockSpec(memory_space=pltpu.VMEM)
    hbm = pl.BlockSpec(memory_space=pl.ANY)
    hot = jax.ShapeDtypeStruct((rows, replicas * size), BF16)
    return pl.pallas_call(
        functools.partial(gates_kernel, cap, replicas),
        out_shape=(
            hot,
            hot,
            jax.ShapeDtypeStruct((rows, LANES), F32),
            jax.ShapeDtypeStruct((rows, half), BF16),
        ),
        in_specs=[hbm] * (2 * replicas + 2) + [vm] * 4,
        out_specs=(vm,) * 4,
        scratch_shapes=[
            pltpu.VMEM((rows, width), BF16),
            pltpu.VMEM((replicas, EXTRA, half), BF16),
            pltpu.VMEM((replicas, EXTRA, half), BF16),
            pltpu.SemaphoreType.DMA((2 * replicas + 1,)),
        ],
        compiler_params=pltpu.CompilerParams(vmem_limit_bytes=VMEM_BYTES),
        cost_estimate=pl.CostEstimate(flops=200_000_000, bytes_accessed=6_000_000, transcendentals=0),
        name="gates",
    )(*own, *pair, after, resid, slots, ids.T, gain[None, :], router.T)


def combine_kernel(replicas, *refs):
    blocks = refs[:replicas]
    first_hbm, second_hbm, gate_hbm, after_hbm, out_ref, all_v, first_ref, second_ref, gate_ref, sem = refs[
        replicas:
    ]
    size = blocks[0].shape[0]
    load(
        sem,
        (first_hbm, first_ref),
        (second_hbm, second_ref),
        (gate_hbm, gate_ref),
        *[(blocks[k], all_v.at[pl.ds(k * size, size)]) for k in range(replicas)],
    )
    gate = gate_ref[:, 0:1]
    one = jnp.dot(first_ref[...], all_v[...], preferred_element_type=F32)
    two = jnp.dot(second_ref[...], all_v[...], preferred_element_type=F32)
    out_ref[...] = (gate * one + (1.0 - gate) * two).astype(BF16)


def combine(blocks, first, second, gate, after):
    replicas = len(blocks)
    size, half = blocks[0].shape
    rows = first.shape[0]
    vm = pl.BlockSpec(memory_space=pltpu.VMEM)
    hbm = pl.BlockSpec(memory_space=pl.ANY)
    return pl.pallas_call(
        functools.partial(combine_kernel, replicas),
        out_shape=jax.ShapeDtypeStruct((rows, half), BF16),
        in_specs=[hbm] * (replicas + 4),
        out_specs=vm,
        scratch_shapes=[
            pltpu.VMEM((replicas * size, half), BF16),
            pltpu.VMEM(first.shape, BF16),
            pltpu.VMEM(second.shape, BF16),
            pltpu.VMEM(gate.shape, F32),
            pltpu.SemaphoreType.DMA((replicas + 3,)),
        ],
        compiler_params=pltpu.CompilerParams(vmem_limit_bytes=VMEM_BYTES),
        cost_estimate=pl.CostEstimate(flops=400_000_000, bytes_accessed=2_500_000, transcendentals=0),
        name="combine",
    )(*blocks, first, second, gate, after)


def choose_kernel(turn, plan_hbm, *refs):
    choices = refs[:-4]
    out_ref, plan_sm, sem, plan_sem = refs[-4:]
    load(plan_sem, (plan_hbm, plan_sm))
    index = plan_sm[0, 24 + turn]
    for i, choice in enumerate(choices):
        @pl.when(index == i)
        def _():
            load(sem, (choice, out_ref))


def choose(plan, held, turn):
    hbm = pl.BlockSpec(memory_space=pl.ANY)
    return pl.pallas_call(
        functools.partial(choose_kernel, turn),
        out_shape=jax.ShapeDtypeStruct(held[0].shape, BF16),
        in_specs=[hbm] * (1 + len(held)),
        out_specs=pl.BlockSpec(memory_space=pltpu.VMEM),
        scratch_shapes=[
            pltpu.SMEM(plan.shape, jnp.int32),
            pltpu.SemaphoreType.DMA((1,)),
            pltpu.SemaphoreType.DMA((1,)),
        ],
        compiler_params=pltpu.CompilerParams(vmem_limit_bytes=VMEM_BYTES),
        cost_estimate=pl.CostEstimate(flops=0, bytes_accessed=0, transcendentals=0),
        name="choose",
    )(plan, *held)


def patch_kernel(count, plan_hbm, *refs):
    choices = refs[:count]
    tail_hbm, out_hbm, token_ref, plan_sm, slabs, sem, slab_sem, out_sem = refs[count:]
    load(sem, (plan_hbm, plan_sm))
    index = plan_sm[0, 0]
    for i, choice in enumerate(choices):
        @pl.when(index == i)
        def _():
            load(slab_sem, (choice, slabs))
    def moves(m):
        to = plan_sm[0, 16 + m]
        return to, [
            pltpu.make_async_copy(
                slabs.at[2 * m + side], out_hbm.at[side, to], out_sem.at[2 * m + side]
            )
            for side in range(2)
        ]

    for m in range(MIG):
        to, copies = moves(m)

        @pl.when(to >= 0)
        def _():
            for copy in copies:
                copy.start()
    for m in range(MIG):
        to, copies = moves(m)

        @pl.when(to >= 0)
        def _():
            for copy in copies:
                copy.wait()
    token_ref[...] = jnp.zeros(token_ref.shape, F32)


def patch(plan, held, tail_new):
    hbm = pl.BlockSpec(memory_space=pl.ANY)
    count = len(held)
    return pl.pallas_call(
        functools.partial(patch_kernel, count),
        out_shape=(
            jax.ShapeDtypeStruct(tail_new.shape, BF16),
            jax.ShapeDtypeStruct((8, LANES), F32),
        ),
        in_specs=[hbm] * (2 + count),
        out_specs=(hbm, pl.BlockSpec(memory_space=pltpu.VMEM)),
        scratch_shapes=[
            pltpu.SMEM(plan.shape, jnp.int32),
            pltpu.VMEM(held[0].shape, BF16),
            pltpu.SemaphoreType.DMA((1,)),
            pltpu.SemaphoreType.DMA((1,)),
            pltpu.SemaphoreType.DMA((2 * MIG,)),
        ],
        input_output_aliases={1 + count: 0},
        compiler_params=pltpu.CompilerParams(vmem_limit_bytes=VMEM_BYTES),
        cost_estimate=pl.CostEstimate(flops=0, bytes_accessed=0, transcendentals=0),
        name="patch",
    )(plan, *held, tail_new)


def body(
    hidden_in, prompt_kv, tail_kv, group_of, prompt_len, tail_len, bucket_of, bias_table,
    attn_gain, w_query, w_key, w_value, w_out, ffn_gain, router_weight, expert_ids,
    w_gate, w_up, w_down, new_slot,
):
    rows, width = hidden_in.shape
    replicas = lax.axis_size("req")
    pieces = lax.axis_size("tp")
    experts = router_weight.shape[1]
    cap = -(-(5 * rows * TOP // (4 * experts)) // 16) * 16
    half = width // 2

    def across(axis, size, k):
        return lambda v: lax.ppermute(v, axis, [(i, i ^ k) for i in range(size)])

    def over_req(k):
        return across("req", replicas, k)

    def over_tp(k):
        return across("tp", pieces, k)

    low_bits, low = low_part(replicas)
    query, key_new, value_new, packet = project(
        new_slot, tail_len, hidden_in, attn_gain, w_query, w_key, w_value, tail_kv
    )
    held = [packet] + [
        over_req(h << low_bits)(packet) for h in range(1, replicas >> low_bits)
    ]
    wouts = [w_out, over_tp(1)(w_out)]
    for k in range(2, pieces, 2):
        wouts += [over_tp(k)(w) for w in wouts[:2]]
    head_out, tail_new = attention(
        query, key_new, value_new, prompt_kv, tail_kv, group_of, prompt_len, tail_len, bucket_of,
        bias_table,
    )
    heads = [head_out] + [over_tp(k)(head_out) for k in range(1, pieces)]
    slots = new_slot.reshape(replicas, rows)
    place, extra, wide, kron, plan = make_plan(
        slots, expert_ids, experts, cap, [head_out] + held[1:] + wouts[2:]
    )
    chosen = [choose(plan, held, j) for j in range(1, low)]
    resid, *blocks = dispatch(
        heads, wouts, hidden_in, ffn_gain, place, extra, wide, chosen, replicas
    )
    near, each = far_part(replicas, pieces)

    def far(f):
        pairs = []
        for r in range(replicas):
            for t in range(pieces):
                to = r ^ (near + (t >> 1) * each + f)
                pairs.append((r * pieces + t, to * pieces + t))
        return lax.ppermute(blocks[near + f], ("req", "tp"), pairs)

    distant = [far(f) for f in range(each)]
    own = [blocks[0]] + [over_req(k)(blocks[k]) for k in range(1, near)] + distant
    for turn in range(1, pieces // 2):
        own += [over_tp(2 * turn)(b) for b in distant]
    pair = [over_tp(1)(b) for b in own]
    keep, give = expert(own, pair, w_gate, w_up, w_down, pieces)
    held = held + [over_req(j + 1)(p) for j, p in enumerate(chosen)]
    back = give_back(keep, over_tp(1)(give), kron, cap, replicas)
    first, second, gate, resid_new = make_gates(
        own, pair, plan, resid, slots, expert_ids, ffn_gain, router_weight, cap
    )
    result = [back[0]] + [over_req(k)(back[k]) for k in range(1, replicas)]
    new_tail_kv, token = patch(plan, held, tail_new)
    mixed = combine(result, first, second, gate, token)
    k = 2
    while k < pieces:
        other = over_tp(k)(mixed)
        mixed = mixed.astype(F32) + other.astype(F32)
        k *= 2
        if k < pieces:
            mixed = mixed.astype(BF16)
    out_half = (resid_new.astype(F32) + mixed.astype(F32)).astype(BF16)
    out_other = over_tp(1)(out_half)
    core = lax.axis_index("tp") & 1
    out_hidden = jnp.where(
        core == 0,
        jnp.concatenate([out_half, out_other], axis=1),
        jnp.concatenate([out_other, out_half], axis=1),
    )
    return (out_hidden, new_tail_kv)


def solution(mesh):
    return jax.shard_map(
        body,
        mesh=mesh,
        in_specs=(
            P("req", None), P(None, "req", None, "tp"), P(None, "req", None, "tp"),
            P("req"), P("req"), P("req"), P(), P(None, "tp"), P(),
            P(None, "tp"), P(None, "tp"), P(None, "tp"), P("tp", None), P(), P(),
            P("req", None), P("req", None, "tp"), P("req", None, "tp"), P("req", "tp", None), P(),
        ),
        out_specs=(P("req", None), P(None, "req", None, "tp")),
        check_vma=False,
    )
```

```python
import functools
import jax
import jax.numpy as jnp
from jax import lax
from jax.experimental import pallas as pl
from jax.experimental.pallas import tpu as pltpu
from jax.sharding import PartitionSpec as P

HD = 64
EPS = 1e-06
F32 = jnp.float32
BF16 = jnp.bfloat16
NT = (((1,), (1,)), ((), ()))
LANES = 128
TILE = 128
TOP = 2
MIG = 4
EXTRA = 16
VMEM_BYTES = 64 * 1024 * 1024


def iota(shape, dim):
    return lax.broadcasted_iota(jnp.int32, shape, dim)


def onehot(hit):
    return hit.astype(F32).astype(BF16)


def attention_kernel(
    group_hbm, plen_hbm, tlen_hbm, group_row_hbm, bucket_hbm, bias_hbm,
    q_hbm, knew_hbm, vnew_hbm, prompt_hbm, tail_hbm,
    head_ref, tail_out,
    group_sm, plen_sm, tlen_sm, perm_sm, group_row, bucket_row, bias_rows, perm_v,
    pk_v, pv_v, kbuf, vbuf,
    q_v, knew_v, vnew_v, table, s_p, s_t, w_p, o_v, sorted_v, qbd_v,
    small_sem, w_sem, p_sem, in_sem, out_sem, perm_sem,
):
    rows = q_v.shape[0]
    groups, prompt_rows, cols = pv_v.shape
    tail_rows = kbuf.shape[1]
    heads = cols // HD
    per8 = 8 // heads
    per16 = 16 // heads
    width_t = per8 * tail_rows
    span_end = prompt_rows + tail_rows
    tile_rows = TILE * heads
    tiles = rows // TILE

    small = [
        pltpu.make_async_copy(src, dst, small_sem.at[i])
        for i, (src, dst) in enumerate(
            (
                (group_hbm, group_sm), (plen_hbm, plen_sm), (tlen_hbm, tlen_sm),
                (group_row_hbm, group_row), (bucket_hbm, bucket_row.at[0]),
                (bias_hbm, bias_rows),
            )
        )
    ]
    weights = [
        pltpu.make_async_copy(src, dst, w_sem.at[i])
        for i, (src, dst) in enumerate(
            ((q_hbm, q_v), (knew_hbm, knew_v), (vnew_hbm, vnew_v))
        )
    ]
    prompts = [
        pltpu.make_async_copy(prompt_hbm.at[0], pk_v, p_sem.at[0]),
        pltpu.make_async_copy(prompt_hbm.at[1], pv_v, p_sem.at[1]),
    ]

    def tile_in(t):
        at = pl.ds(t * TILE, TILE)
        return [
            pltpu.make_async_copy(tail_hbm.at[0, at], kbuf.at[at], in_sem.at[0, t]),
            pltpu.make_async_copy(tail_hbm.at[1, at], vbuf.at[at], in_sem.at[1, t]),
        ]

    def tile_out(t):
        at = pl.ds(t * TILE, TILE)
        return [
            pltpu.make_async_copy(kbuf.at[at], tail_out.at[0, at], out_sem.at[0, t]),
            pltpu.make_async_copy(vbuf.at[at], tail_out.at[1, at], out_sem.at[1, t]),
        ]

    for copy in small + weights + prompts[:1]:
        copy.start()
    for copy in small:
        copy.wait()

    for t in range(tiles):
        for copy in tile_in(t):
            copy.start()
    prompts[1].start()

    eye = onehot(iota((rows, rows), 0) == iota((rows, rows), 1))
    g_row = group_row[...]
    g_col = lax.dot_general(
        eye, jnp.broadcast_to(g_row.astype(F32), (8, rows)).astype(BF16), NT,
        preferred_element_type=F32,
    )[:, 0:1].astype(jnp.int32)
    key_row = g_row * rows + iota((1, rows), 1)
    key_col = g_col * rows + iota((rows, 1), 0)
    rank_row = jnp.sum((key_col < key_row).astype(jnp.int32), axis=0, keepdims=True)
    rank_col = jnp.sum((key_row < key_col).astype(jnp.int32), axis=1, keepdims=True)
    perm_row = jnp.sum(
        jnp.where(rank_col == iota((rows, rows), 1), iota((rows, rows), 0), 0), axis=0, keepdims=True
    )
    perm_v[...] = jnp.broadcast_to(perm_row, perm_v.shape)
    perm_copy = pltpu.make_async_copy(perm_v, perm_sm, perm_sem)
    perm_copy.start()

    span = bucket_row.shape[1]
    buckets = bias_rows.shape[1]
    below = (bucket_row[...] < iota((buckets, span), 0)).astype(jnp.int32)
    starts = jnp.sum(below, axis=1, keepdims=True)
    bias = jnp.concatenate([bias_rows[...]] * per8, axis=0)
    distance = span_end - iota(table.shape, 1)
    found = jnp.broadcast_to(bias[:, 0:1], table.shape)
    for k in range(1, buckets):
        found = jnp.where(distance >= starts[k : k + 1, 0:1], bias[:, k : k + 1], found)
    table[...] = found

    for copy in weights:
        copy.wait()
    perm_copy.wait()

    lane = iota((8, LANES), 1)
    sub = iota((8, LANES), 0)
    row16 = iota((16, cols), 0)
    minus = jnp.float32(-jnp.inf)
    pieces = prompt_rows // LANES

    def build_bias(tile):
        def step(i, carry):
            base = tile * TILE + i * per8
            out_p = [jnp.full((8, LANES), minus) for _ in range(pieces)]
            out_t = [jnp.full((8, LANES), minus) for _ in range(width_t // LANES)]
            for j in range(per8):
                r = perm_sm[0, base + j]
                length = tlen_sm[r]
                plen = plen_sm[group_sm[r]]
                start = span_end - plen - length
                block = lax.shift_right_logical(start, 7)
                off = start & (LANES - 1)
                mine = (sub >= j * heads) & (sub < (j + 1) * heads)
                window = table[:, pl.ds(pl.multiple_of(block * LANES, LANES), prompt_rows + LANES)]
                turn = (LANES - off) & (LANES - 1)
                turned = [
                    pltpu.roll(window[:, k * LANES : (k + 1) * LANES], turn, 1)
                    for k in range(pieces + 1)
                ]
                for k in range(pieces):
                    here = jnp.where(lane < LANES - off, turned[k], turned[k + 1])
                    out_p[k] = jnp.where(mine & (lane < plen - k * LANES), here, out_p[k])
                place = j * tail_rows
                k = place // LANES
                place = place - k * LANES
                own = table[:, prompt_rows : prompt_rows + LANES]
                shift = (place - tail_rows + length) & (LANES - 1)
                own = pltpu.roll(own, shift, 1)
                live = mine & (lane >= place) & (lane <= place + length)
                out_t[k] = jnp.where(live, own, out_t[k])
            at = pl.ds(pl.multiple_of(tile * tile_rows + i * 8, 8), 8)
            for k in range(pieces):
                s_p[at, k * LANES : (k + 1) * LANES] = out_p[k]
            for k in range(width_t // LANES):
                s_t[at, k * LANES : (k + 1) * LANES] = out_t[k]
            return carry

        lax.fori_loop(0, TILE // per8, step, 0, unroll=16)

    def insert(t):
        def step(i, carry):
            r = t * TILE + i
            length = tlen_sm[r]
            first = pl.multiple_of(length & 0x30, 16)
            hit = row16 == (length & 15)
            for new, buf in ((knew_v, kbuf), (vnew_v, vbuf)):
                fresh = jnp.broadcast_to(new[pl.ds(r, 1), :], (16, cols)).astype(BF16)
                old = buf[r, pl.ds(first, 16), :]
                buf[r, pl.ds(first, 16), :] = jnp.where(hit, fresh, old)
            return carry

        lax.fori_loop(0, TILE, step, 0, unroll=8)

    own_head = iota((tile_rows, cols), 0) % heads == iota((tile_rows, cols), 1) // HD
    spread_row = iota((tile_rows, rows), 0) // heads
    first_head = iota((TILE, LANES), 1) < HD

    def spread_of(tile):
        return onehot(rank_row == spread_row + tile * TILE)

    def member_of(tile):
        group8 = jnp.broadcast_to(g_row.astype(F32), (8, rows)).astype(BF16)
        return lax.dot_general(
            spread_of(tile), group8, NT, preferred_element_type=F32
        )[:, 0:1].astype(jnp.int32)

    def group_range(tile):
        low = group_sm[perm_sm[0, tile * TILE]]
        high = group_sm[perm_sm[0, tile * TILE + TILE - 1]]
        return low, high + 1

    def scores(tile, carry):
        build_bias(tile)
        at = pl.ds(pl.multiple_of(tile * tile_rows, tile_rows), tile_rows)
        qrep = jnp.dot(spread_of(tile), q_v[...], preferred_element_type=F32)
        qbd = jnp.where(own_head, qrep, 0.0)
        qbd_v[at, :] = qbd.astype(BF16)
        member = member_of(tile)

        @pl.when(tile == 0)
        def _():
            prompts[0].wait()

        def one_group(g, carry):
            part = jnp.where(member == g, qbd, 0.0).astype(BF16)
            s_p[at, :] += lax.dot_general(part, pk_v[g], NT, preferred_element_type=F32)
            return carry

        low, high = group_range(tile)
        lax.fori_loop(low, high, one_group, 0)
        for copy in tile_in(tile):
            copy.wait()

        @pl.when(tile > 0)
        def _():
            for copy in tile_out(tile - 1):
                copy.start()

        insert(tile)
        return carry

    lax.fori_loop(0, tiles, scores, 0)
    for copy in tile_out(tiles - 1):
        copy.start()
    prompts[1].wait()

    def gathered(buf, first):
        return jnp.concatenate([buf[perm_sm[0, first + j]] for j in range(per16)], axis=0)

    def values(tile, carry):
        base = pl.multiple_of(tile * tile_rows, tile_rows)
        at = pl.ds(base, tile_rows)
        for i in range(TILE // per16):
            keys = gathered(kbuf, tile * TILE + i * per16)
            here = pl.ds(pl.multiple_of(base + i * 16, 16), 16)
            got = lax.dot_general(qbd_v[here, :], keys, NT, preferred_element_type=F32)
            upper = pl.ds(pl.multiple_of(base + i * 16, 8), 8)
            lower = pl.ds(pl.multiple_of(base + i * 16 + 8, 8), 8)
            s_t[upper, :] += got[:8, :width_t]
            s_t[lower, :] += got[8:, width_t:]
        prompt_s = s_p[at, :]
        tail_s = s_t[at, :]
        top = jnp.maximum(
            jnp.max(prompt_s, axis=1, keepdims=True), jnp.max(tail_s, axis=1, keepdims=True)
        )
        pe = jnp.exp(prompt_s - top)
        te = jnp.exp(tail_s - top)
        total = jnp.sum(pe, axis=1, keepdims=True) + jnp.sum(te, axis=1, keepdims=True)
        part = 1.0 / total
        w_p[...] = (pe * part).astype(BF16)
        tw = te * part
        none = jnp.zeros((8, width_t), F32)
        for i in range(TILE // per16):
            row = i * 16
            upper = jnp.concatenate([tw[row : row + 8], none], axis=1)
            lower = jnp.concatenate([none, tw[row + 8 : row + 16]], axis=1)
            both = jnp.concatenate([upper, lower], axis=0).astype(BF16)
            vals = gathered(vbuf, tile * TILE + i * per16)
            o_t = jnp.dot(both, vals, preferred_element_type=F32)
            for b in range(cols // LANES):
                o_v[b, row : row + 16, :] = o_t[:, b * LANES : (b + 1) * LANES]
        member = member_of(tile)

        def one_group(g, carry):
            w = jnp.where(member == g, w_p[...].astype(F32), 0.0).astype(BF16)
            o_p = jnp.dot(w, pv_v[g], preferred_element_type=F32)
            for b in range(cols // LANES):
                o_v[b] += o_p[:, b * LANES : (b + 1) * LANES]
            return carry

        low, high = group_range(tile)
        lax.fori_loop(low, high, one_group, 0)
        to = pl.ds(pl.multiple_of(tile * TILE, TILE), TILE)
        for b in range(cols // LANES):
            even = o_v[b, pl.ds(2 * b, TILE, stride=heads), :]
            odd = o_v[b, pl.ds(2 * b + 1, TILE, stride=heads), :]
            sorted_v[to, b * LANES : (b + 1) * LANES] = jnp.where(first_head, even, odd).astype(BF16)
        return carry

    lax.fori_loop(0, tiles, values, 0)
    unsort = onehot(rank_col == iota((rows, rows), 1))
    head_ref[...] = jnp.dot(unsort, sorted_v[...], preferred_element_type=F32).astype(BF16)
    for t in range(tiles):
        for copy in tile_out(t):
            copy.wait()


def project_kernel(
    slots_hbm, tlen_hbm, hidden_hbm, gain_hbm, wq_hbm, wk_hbm, wv_hbm, tail_hbm,
    q_ref, knew_ref, vnew_ref, packet_ref,
    slots_sm, tlen_sm, mover_sm, hidden_v, gain_v, wq_v, wk_v, wv_v, sem, slab_sem,
):
    rows = hidden_v.shape[0]
    cols = wq_v.shape[1]
    early = [
        pltpu.make_async_copy(slots_hbm, slots_sm, sem.at[0]),
        pltpu.make_async_copy(tlen_hbm, tlen_sm, sem.at[1]),
    ]
    late = [
        pltpu.make_async_copy(src, dst, sem.at[2 + i])
        for i, (src, dst) in enumerate(
            (
                (hidden_hbm, hidden_v), (gain_hbm, gain_v),
                (wq_hbm, wq_v), (wk_hbm, wk_v), (wv_hbm, wv_v),
            )
        )
    ]
    for copy in early + late:
        copy.start()
    for copy in early:
        copy.wait()
    base = lax.axis_index("req") * rows
    for m in range(MIG + 1):
        mover_sm[m] = 0

    def look(i, count):
        mover_sm[count] = i
        return count + (slots_sm[base + i] != base + i).astype(jnp.int32)

    lax.fori_loop(0, rows, look, 0, unroll=16)
    slabs = [
        pltpu.make_async_copy(
            tail_hbm.at[side, mover_sm[m]], packet_ref.at[2 * m + side], slab_sem.at[2 * m + side]
        )
        for m in range(MIG)
        for side in range(2)
    ]
    for copy in slabs:
        copy.start()
    for copy in late:
        copy.wait()
    v = hidden_v[...].astype(F32)
    normed = (
        v * lax.rsqrt(jnp.mean(v * v, axis=-1, keepdims=True) + EPS) * gain_v[...]
    ).astype(BF16)
    query = jnp.dot(normed, wq_v[...], preferred_element_type=F32).astype(BF16)
    q_ref[...] = query * jnp.asarray(HD ** (-0.5), BF16)
    for new, w in ((knew_ref, wk_v), (vnew_ref, wv_v)):
        new[...] = jnp.dot(normed, w[...], preferred_element_type=F32).astype(BF16).astype(F32)
    for copy in slabs:
        copy.wait()
    at = iota((packet_ref.shape[1], cols), 0)
    for m in range(MIG):
        r = mover_sm[m]
        for side, new in enumerate((knew_ref, vnew_ref)):
            old = packet_ref[2 * m + side].astype(F32)
            packet_ref[2 * m + side] = jnp.where(
                at == tlen_sm[r], new[pl.ds(r, 1), :], old
            ).astype(BF16)


def project(new_slot, tail_len, hidden_in, gain, w_query, w_key, w_value, tail_kv):
    rows, width = hidden_in.shape
    cols = w_query.shape[1]
    tail_rows = tail_kv.shape[2]
    vm = pl.BlockSpec(memory_space=pltpu.VMEM)
    hbm = pl.BlockSpec(memory_space=pl.ANY)
    return pl.pallas_call(
        project_kernel,
        out_shape=(
            jax.ShapeDtypeStruct((rows, cols), BF16),
            jax.ShapeDtypeStruct((rows, cols), F32),
            jax.ShapeDtypeStruct((rows, cols), F32),
            jax.ShapeDtypeStruct((2 * MIG, tail_rows, cols), BF16),
        ),
        in_specs=[hbm] * 8,
        out_specs=(vm,) * 4,
        scratch_shapes=[
            pltpu.SMEM(new_slot.shape, jnp.int32),
            pltpu.SMEM(tail_len.shape, jnp.int32),
            pltpu.SMEM((MIG + 1,), jnp.int32),
            pltpu.VMEM((rows, width), BF16),
            pltpu.VMEM((1, width), F32),
            pltpu.VMEM((width, cols), BF16),
            pltpu.VMEM((width, cols), BF16),
            pltpu.VMEM((width, cols), BF16),
            pltpu.SemaphoreType.DMA((7,)),
            pltpu.SemaphoreType.DMA((2 * MIG,)),
        ],
        compiler_params=pltpu.CompilerParams(vmem_limit_bytes=VMEM_BYTES),
        cost_estimate=pl.CostEstimate(flops=400_000_000, bytes_accessed=3_000_000, transcendentals=0),
        name="project",
    )(new_slot, tail_len, hidden_in, gain[None, :], w_query, w_key, w_value, tail_kv)


def attention(
    query, key_new, value_new, prompt_kv, tail_kv, group_of, prompt_len, tail_len, bucket_of,
    bias_table,
):
    rows, cols = query.shape
    heads = cols // HD
    groups, prompt_rows = prompt_kv.shape[1:3]
    tail_rows = tail_kv.shape[2]
    span = bucket_of.shape[0]
    buckets = bias_table.shape[0]
    table_width = 2 * prompt_rows + LANES
    width_t = 8 // heads * tail_rows
    tiles = rows // TILE
    vm = pl.BlockSpec(memory_space=pltpu.VMEM)
    hbm = pl.BlockSpec(memory_space=pl.ANY)
    return pl.pallas_call(
        attention_kernel,
        out_shape=(
            jax.ShapeDtypeStruct((rows, cols), BF16),
            jax.ShapeDtypeStruct(tail_kv.shape, BF16),
        ),
        in_specs=[hbm] * 11,
        out_specs=(vm, hbm),
        scratch_shapes=[
            pltpu.SMEM((rows,), jnp.int32),
            pltpu.SMEM((groups,), jnp.int32),
            pltpu.SMEM((rows,), jnp.int32),
            pltpu.SMEM((8, rows), jnp.int32),
            pltpu.VMEM((1, rows), jnp.int32),
            pltpu.VMEM((1, span), jnp.int32),
            pltpu.VMEM((heads, buckets), F32),
            pltpu.VMEM((8, rows), jnp.int32),
            pltpu.VMEM((groups, prompt_rows, cols), BF16),
            pltpu.VMEM((groups, prompt_rows, cols), BF16),
            pltpu.VMEM((rows, tail_rows, cols), BF16),
            pltpu.VMEM((rows, tail_rows, cols), BF16),
            pltpu.VMEM((rows, cols), BF16),
            pltpu.VMEM((rows, cols), F32),
            pltpu.VMEM((rows, cols), F32),
            pltpu.VMEM((8, table_width), F32),
            pltpu.VMEM((rows * heads, prompt_rows), F32),
            pltpu.VMEM((rows * heads, width_t), F32),
            pltpu.VMEM((TILE * heads, prompt_rows), BF16),
            pltpu.VMEM((cols // LANES, TILE * heads, LANES), F32),
            pltpu.VMEM((rows, cols), BF16),
            pltpu.VMEM((rows * heads, cols), BF16),
            pltpu.SemaphoreType.DMA((6,)),
            pltpu.SemaphoreType.DMA((3,)),
            pltpu.SemaphoreType.DMA((2,)),
            pltpu.SemaphoreType.DMA((2, tiles)),
            pltpu.SemaphoreType.DMA((2, tiles)),
            pltpu.SemaphoreType.DMA,
        ],
        compiler_params=pltpu.CompilerParams(vmem_limit_bytes=VMEM_BYTES),
        cost_estimate=pl.CostEstimate(flops=8_000_000_000, bytes_accessed=45_000_000, transcendentals=700_000),
        name="attention",
    )(
        group_of, prompt_len, tail_len, group_of[None, :], bucket_of, bias_table.T,
        query, key_new, value_new, prompt_kv, tail_kv,
    )


def block_rows(cap):
    return cap + EXTRA


def low_part(replicas):
    bits = (replicas.bit_length() - 1) // 2
    return bits, 1 << bits


def plan_kernel(cap, slots_ref, ids_ref, *refs):
    place_ref, extra_ref, wide_ref, kron_ref, plan_ref, slot_s = refs[-6:]
    replicas, rows = slots_ref.shape
    experts = slot_s.shape[0]
    size = place_ref.shape[0] // replicas
    me = lax.axis_index("req")
    ns = slots_ref[...]
    at_sub = iota((replicas, rows), 0)
    at_lane = iota((replicas, rows), 1)
    moved = ns != at_sub * rows + at_lane
    tri = (iota((rows, rows), 0) < iota((rows, rows), 1)).astype(BF16)
    rank = jnp.dot(moved.astype(F32).astype(BF16), tri, preferred_element_type=F32).astype(jnp.int32)
    going_to = ns // rows
    mine = at_sub == me

    def own(values):
        return jnp.sum(jnp.where(mine, values, 0), axis=0, keepdims=True)

    moved_me = own(moved.astype(jnp.int32))
    rank_me = own(rank)
    to_me = own(going_to)
    ids_rows = ids_ref[...]
    at_e = iota((experts, rows), 0)
    hit = (ids_rows[0:1] == at_e) | (ids_rows[1:2] == at_e)
    normal = (hit & (moved_me == 0)).astype(F32).astype(BF16)
    slot = jnp.dot(normal, tri, preferred_element_type=F32).astype(jnp.int32)
    slot_s[...] = jnp.where(hit, jnp.where(moved_me > 0, cap + rank_me, slot), -1)
    at_row = iota((size, rows), 0)
    at_extra = iota((EXTRA, rows), 0)
    for k in range(replicas):
        e = me ^ k
        block = pl.ds(k * size, size)
        row = slot_s[pl.ds(e, 1), :]
        leaving = jnp.where((moved_me > 0) & (to_me == e), rank_me, -100)
        place_ref[block, :] = onehot(at_row == row)
        more = pl.ds(k * EXTRA, EXTRA)
        extra_ref[more, 0:rows] = onehot(at_extra == leaving + MIG)
        extra_ref[more, rows:] = onehot(at_extra == leaving + 2 * MIG)
    lane = iota(wide_ref.shape, 1)
    eye = onehot(iota((rows, rows), 0) == iota((rows, rows), 1))
    facts = jnp.concatenate([ids_rows, jnp.zeros((6, rows), jnp.int32)], axis=0)
    columns = lax.dot_general(
        eye, facts.astype(F32).astype(BF16), NT, preferred_element_type=F32
    )
    wide = jnp.where(lane == 0, columns[:, 0:1], jnp.where(lane == 1, columns[:, 1:2], 0.0))
    wide_ref[...] = wide.astype(BF16)
    dest = jnp.max(jnp.where(moved, going_to, -1), axis=1, keepdims=True)
    dest = jnp.where(dest < 0, iota((replicas, 1), 0), dest)
    hot = (dest == iota((replicas, replicas), 1)).astype(F32).astype(BF16)
    span = replicas * EXTRA
    mixed_row = (iota((span, replicas), 0) // EXTRA) ^ me
    a = (mixed_row == iota((span, replicas), 1)).astype(F32).astype(BF16)
    by_source = lax.dot_general(a, hot, NT, preferred_element_type=F32).astype(BF16)
    pairs = lax.dot_general(by_source, a, NT, preferred_element_type=F32)
    same = iota((span, span), 0) % EXTRA == iota((span, span), 1) % EXTRA
    kron_ref[...] = jnp.where(same, pairs, 0.0).astype(BF16)
    sub1 = iota((replicas, 1), 0)

    def source_of(who):
        return jnp.sum(jnp.where(dest == who, sub1, 0), axis=0, keepdims=True)

    low_bits, low = low_part(replicas)
    diff = source_of(me) ^ me
    turn = diff & (low - 1)
    final = jnp.where(turn == 0, diff >> low_bits, (replicas >> low_bits) + turn - 1)
    lane8 = iota((8, LANES), 1)
    plan = jnp.where(lane8 == 0, final, -1)
    for j in range(1, low):
        apart = source_of(me ^ j) ^ me
        plan = jnp.where(lane8 == 24 + j, apart >> low_bits, plan)
    lane1 = iota((1, rows), 1)
    for m in range(MIG):
        is_m = (moved_me > 0) & (rank_me == m)
        mover = jnp.sum(jnp.where(is_m, lane1, 0), axis=1, keepdims=True)
        plan = jnp.where(lane8 == 8 + m, mover, plan)
        come = moved & (going_to == me) & (rank == m)
        to = jnp.sum(jnp.where(come, ns - me * rows + 1, 0), axis=1, keepdims=True)
        to = jnp.sum(to, axis=0, keepdims=True) - 1
        plan = jnp.where(lane8 == 16 + m, to, plan)
    plan_ref[...] = plan


def make_plan(slots, expert_ids, experts, cap, after):
    replicas, rows = slots.shape
    size = block_rows(cap)
    vm = pl.BlockSpec(memory_space=pltpu.VMEM)
    span = replicas * EXTRA
    return pl.pallas_call(
        functools.partial(plan_kernel, cap),
        out_shape=(
            jax.ShapeDtypeStruct((replicas * size, rows), BF16),
            jax.ShapeDtypeStruct((replicas * EXTRA, 2 * rows), BF16),
            jax.ShapeDtypeStruct((rows, LANES), BF16),
            jax.ShapeDtypeStruct((span, span), BF16),
            jax.ShapeDtypeStruct((8, LANES), jnp.int32),
        ),
        in_specs=[vm, vm] + [pl.BlockSpec(memory_space=pl.ANY)] * len(after),
        out_specs=(vm,) * 5,
        scratch_shapes=[pltpu.VMEM((experts, rows), jnp.int32)],
        compiler_params=pltpu.CompilerParams(vmem_limit_bytes=VMEM_BYTES),
        cost_estimate=pl.CostEstimate(flops=0, bytes_accessed=0, transcendentals=0),
        name="plan",
    )(slots, expert_ids.T, *after)


def load(sem, *pairs):
    made = [pltpu.make_async_copy(src, dst, sem.at[i]) for i, (src, dst) in enumerate(pairs)]
    for copy in made:
        copy.start()
    for copy in made:
        copy.wait()


def norm(values, gain):
    v = values.astype(F32)
    return (v * lax.rsqrt(jnp.mean(v * v, axis=-1, keepdims=True) + EPS) * gain).astype(BF16)


def far_part(replicas, pieces):
    return replicas // 2, replicas // pieces


def dispatch_kernel(pieces, replicas, *refs):
    near, each = far_part(replicas, pieces)
    count = near + each
    heads_hbm = refs[:pieces]
    wout_hbm = refs[pieces : 2 * pieces]
    hidden_hbm, gain_ref, place_hbm, extra_hbm, wide_hbm = refs[2 * pieces : 2 * pieces + 5]
    refs = refs[-11 - count :]
    resid_ref = refs[0]
    outs = refs[1 : 1 + count]
    head_v, wout_v, stack, hidden_ref, place_ref, extra_ref, wide_ref, extra_v, sem, more = refs[1 + count :]
    tp = lax.axis_index("tp")
    core = tp & 1
    rows, width = hidden_ref.shape
    cols = width // pieces
    half = width // 2

    def copies():
        made = []
        for k in range(pieces):
            at = pl.ds(pl.multiple_of((tp ^ k) * cols, cols), cols)
            made.append(pltpu.make_async_copy(wout_hbm[k], wout_v.at[at], sem.at[0, k]))
            made.append(pltpu.make_async_copy(heads_hbm[k], head_v.at[:, at], sem.at[1, k]))
        made.append(pltpu.make_async_copy(hidden_hbm, hidden_ref, more.at[0]))
        return made

    late = [
        pltpu.make_async_copy(place_hbm, place_ref, more.at[1]),
        pltpu.make_async_copy(extra_hbm, extra_ref, more.at[2]),
        pltpu.make_async_copy(wide_hbm, wide_ref, more.at[3]),
    ]

    for copy in copies() + late:
        copy.start()
    for copy in copies():
        copy.wait()
    attn = jnp.dot(head_v[...], wout_v[...], preferred_element_type=F32)
    resid = (hidden_ref[...].astype(F32) + attn).astype(BF16)
    resid_ref[...] = resid
    normed = norm(resid, gain_ref[...])
    first = core == 0
    stack[0:rows, :] = jnp.where(first, normed[:, :half], normed[:, half:])
    stack[rows : 2 * rows, :] = jnp.where(first, resid[:, :half], resid[:, half:])
    for copy in late:
        copy.wait()
    size = place_ref.shape[0] // replicas
    extra_v[...] = jnp.dot(extra_ref[:, 0:rows], stack[rows:, :], preferred_element_type=F32)
    extra_v[:, 0:LANES] += jnp.dot(extra_ref[:, rows:], wide_ref[...], preferred_element_type=F32)
    for i in range(count):
        k = i if i < near else near + (tp >> 1) * each + (i - near)
        block = jnp.dot(
            place_ref[pl.ds(k * size, size), :], stack[0:rows, :], preferred_element_type=F32
        )
        outs[i][0 : size - EXTRA, :] = block[: size - EXTRA].astype(BF16)
        outs[i][size - EXTRA :, :] = (
            block[size - EXTRA :] + extra_v[pl.ds(k * EXTRA, EXTRA), :]
        ).astype(BF16)


def dispatch(heads, wouts, hidden, gain, place, extra, wide, after, replicas):
    rows, width = hidden.shape
    pieces = len(heads)
    count = sum(far_part(replicas, pieces))
    half = width // 2
    size = place.shape[0] // replicas
    vm = pl.BlockSpec(memory_space=pltpu.VMEM)
    hbm = pl.BlockSpec(memory_space=pl.ANY)
    return pl.pallas_call(
        functools.partial(dispatch_kernel, pieces, replicas),
        out_shape=(jax.ShapeDtypeStruct((rows, width), BF16),)
        + tuple(jax.ShapeDtypeStruct((size, half), BF16) for _ in range(count)),
        in_specs=[hbm] * (2 * pieces) + [hbm, vm, hbm, hbm, hbm] + [hbm] * len(after),
        out_specs=(vm,) * (1 + count),
        scratch_shapes=[
            pltpu.VMEM((rows, width), BF16),
            pltpu.VMEM((width, width), BF16),
            pltpu.VMEM((2 * rows, half), BF16),
            pltpu.VMEM((rows, width), BF16),
            pltpu.VMEM(place.shape, BF16),
            pltpu.VMEM(extra.shape, BF16),
            pltpu.VMEM(wide.shape, BF16),
            pltpu.VMEM((extra.shape[0], half), F32),
            pltpu.SemaphoreType.DMA((2, pieces)),
            pltpu.SemaphoreType.DMA((5,)),
        ],
        compiler_params=pltpu.CompilerParams(vmem_limit_bytes=VMEM_BYTES),
        cost_estimate=pl.CostEstimate(flops=1_200_000_000, bytes_accessed=6_000_000, transcendentals=0),
        name="dispatch",
    )(*heads, *wouts, hidden, gain[None, :], place, extra, wide, *after)


def pieces_of(total, step):
    return [(at, min(step, total - at)) for at in range(0, total, step)]


def expert_kernel(replicas, pieces, *refs):
    own = refs[:replicas]
    pair = refs[replicas : 2 * replicas]
    wg_hbm, wu_hbm, wd_hbm = refs[2 * replicas : 2 * replicas + 3]
    keep_ref, give_ref, x_own, x_pair, wg, wu, wd, act, sem, xsem = refs[-10:]
    tp = lax.axis_index("tp")
    core = tp & 1
    size, half = own[0].shape
    near, each = far_part(replicas, pieces)
    hidden = wg.shape[0]
    chunks = pieces_of(hidden, 256)
    blocks = []
    for k in range(replicas):
        there = k
        if k >= near:
            turn, f = divmod(k - near, each)
            there = near + ((tp >> 1) ^ turn) * each + f
        at = pl.ds(there * size, size)
        blocks.append(pltpu.make_async_copy(own[k], x_own.at[at], xsem.at[0, k]))
        blocks.append(pltpu.make_async_copy(pair[k], x_pair.at[at], xsem.at[1, k]))
    wide = [
        [
            pltpu.make_async_copy(src.at[0, pl.ds(at, n)], dst.at[pl.ds(at, n)], sem.at[side, c])
            for side, (src, dst) in enumerate(((wg_hbm, wg), (wu_hbm, wu)))
        ]
        for c, (at, n) in enumerate(chunks)
    ]
    down = pltpu.make_async_copy(wd_hbm.at[0], wd, sem.at[2, 0])
    for copy in wide[0] + blocks + sum(wide[1:], []) + [down]:
        copy.start()
    for copy in blocks:
        copy.wait()
    here = pl.ds(pl.multiple_of(core * half, half), half)
    there = pl.ds(pl.multiple_of((1 - core) * half, half), half)
    a, b = x_own[...], x_pair[...]

    def product(w, rows):
        return lax.dot_general(a, w[rows, here], NT, preferred_element_type=F32) + lax.dot_general(
            b, w[rows, there], NT, preferred_element_type=F32
        )

    for c, (at, n) in enumerate(chunks):
        for copy in wide[c]:
            copy.wait()
        rows = pl.ds(at, n)
        gate = product(wg, rows)
        act[:, at : at + n] = (jax.nn.gelu(gate, approximate=True) * product(wu, rows)).astype(BF16)
    down.wait()
    give_ref[...] = jnp.dot(act[...], wd[:, there], preferred_element_type=F32).astype(BF16)
    keep_ref[...] = jnp.dot(act[...], wd[:, here], preferred_element_type=F32).astype(BF16)


def expert(own, pair, w_gate, w_up, w_down, pieces):
    replicas = len(own)
    size, half = own[0].shape
    _, width, hidden = w_gate.shape
    total = replicas * size
    vm = pl.BlockSpec(memory_space=pltpu.VMEM)
    hbm = pl.BlockSpec(memory_space=pl.ANY)
    shape = jax.ShapeDtypeStruct((total, half), BF16)
    return pl.pallas_call(
        functools.partial(expert_kernel, replicas, pieces),
        out_shape=(shape, shape),
        in_specs=[hbm] * (2 * replicas + 3),
        out_specs=(vm, vm),
        scratch_shapes=[
            pltpu.VMEM((total, half), BF16),
            pltpu.VMEM((total, half), BF16),
            pltpu.VMEM((hidden, width), BF16),
            pltpu.VMEM((hidden, width), BF16),
            pltpu.VMEM((hidden, width), BF16),
            pltpu.VMEM((total, hidden), BF16),
            pltpu.SemaphoreType.DMA((3, len(pieces_of(hidden, 256)))),
            pltpu.SemaphoreType.DMA((2, replicas)),
        ],
        compiler_params=pltpu.CompilerParams(vmem_limit_bytes=VMEM_BYTES),
        cost_estimate=pl.CostEstimate(flops=3_400_000_000, bytes_accessed=8_000_000, transcendentals=600_000),
        name="expert",
    )(*own, *pair, jnp.swapaxes(w_gate, 1, 2), jnp.swapaxes(w_up, 1, 2), w_down)


def give_back_kernel(cap, keep_hbm, got_hbm, kron_hbm, *refs):
    replicas = len(refs) - 5
    outs = refs[:replicas]
    rows_v, keep_ref, got_ref, kron_ref, sem = refs[replicas:]
    load(sem, (keep_hbm, keep_ref), (got_hbm, got_ref), (kron_hbm, kron_ref))
    size = outs[0].shape[0]
    for k in range(replicas):
        at = slice(k * size, (k + 1) * size)
        both = keep_ref[at, :].astype(F32) + got_ref[at, :].astype(F32)
        outs[k][...] = both.astype(BF16)
        rows_v[k * EXTRA : (k + 1) * EXTRA, :] = both[size - EXTRA :].astype(BF16)
    moved = jnp.dot(kron_ref[...], rows_v[...], preferred_element_type=F32)
    first = iota((EXTRA, 1), 0) >= cap - (size - EXTRA)
    for k in range(replicas):
        at = slice(k * EXTRA, (k + 1) * EXTRA)
        outs[k][size - EXTRA :, :] = jnp.where(
            first, moved[at], rows_v[at, :].astype(F32)
        ).astype(BF16)


def give_back(keep, got, kron, cap, replicas):
    total, half = keep.shape
    size = total // replicas
    vm = pl.BlockSpec(memory_space=pltpu.VMEM)
    hbm = pl.BlockSpec(memory_space=pl.ANY)
    return pl.pallas_call(
        functools.partial(give_back_kernel, cap),
        out_shape=tuple(jax.ShapeDtypeStruct((size, half), BF16) for _ in range(replicas)),
        in_specs=[hbm] * 3,
        out_specs=(vm,) * replicas,
        scratch_shapes=[
            pltpu.VMEM((replicas * EXTRA, half), BF16),
            pltpu.VMEM((total, half), BF16),
            pltpu.VMEM((total, half), BF16),
            pltpu.VMEM(kron.shape, BF16),
            pltpu.SemaphoreType.DMA((3,)),
        ],
        compiler_params=pltpu.CompilerParams(vmem_limit_bytes=VMEM_BYTES),
        cost_estimate=pl.CostEstimate(flops=30_000_000, bytes_accessed=2_500_000, transcendentals=0),
        name="give_back",
    )(keep, got, kron)


def gates_kernel(cap, replicas, *refs):
    own = refs[:replicas]
    pair = refs[replicas : 2 * replicas]
    (after_hbm, resid_hbm, slots_ref, ids_ref, gain_ref, router_ref) = refs[
        2 * replicas : 2 * replicas + 6
    ]
    (first_ref, second_ref, gate_ref, new_ref, resid_ref, own_v, pair_v, sem) = refs[2 * replicas + 6 :]
    me = lax.axis_index("req")
    core = lax.axis_index("tp") & 1
    rows, width = resid_ref.shape
    half = width // 2
    size = own[0].shape[0]
    low = pl.ds(size - EXTRA, EXTRA)
    skip = 0
    load(
        sem,
        (resid_hbm, resid_ref),
        *[(own[k].at[low], own_v.at[k]) for k in range(replicas)],
        *[(pair[k].at[low], pair_v.at[k]) for k in range(replicas)],
    )
    ns = slots_ref[...]
    count = ns.shape[0]
    at_sub = iota((count, rows), 0)
    moved = ns != at_sub * rows + iota((count, rows), 1)
    before = (iota((rows, rows), 0) < iota((rows, rows), 1)).astype(BF16)
    movedf = moved.astype(F32)
    rank = jnp.dot(movedf.astype(BF16), before, preferred_element_type=F32)
    coming = moved & (ns // rows == me)
    slot_to = jnp.sum(jnp.where(coming, ns - me * rows + 1, 0), axis=0, keepdims=True) - 1
    rank_in = jnp.sum(jnp.where(coming, rank, 0.0), axis=0, keepdims=True).astype(jnp.int32)
    landing = (iota((rows, rows), 0) == slot_to).astype(F32).astype(BF16)
    at16 = iota((EXTRA, rows), 0)

    def taken(offset):
        hot = (at16 == rank_in + (skip + offset)) & (slot_to >= 0)
        return lax.dot_general(landing, hot.astype(F32).astype(BF16), NT, preferred_element_type=F32)

    take_resid = taken(MIG)
    take_ids = taken(2 * MIG)
    vacated = jnp.sum(take_resid, axis=1, keepdims=True) > 0.5
    in_own = own_v[0].astype(F32)
    in_pair = pair_v[0].astype(F32)
    for k in range(1, replicas):
        in_own = in_own + own_v[k].astype(F32)
        in_pair = in_pair + pair_v[k].astype(F32)
    in_own, in_pair = in_own.astype(BF16), in_pair.astype(BF16)
    first_core = core == 0
    in_low = jnp.where(first_core, in_own, in_pair)
    in_high = jnp.where(first_core, in_pair, in_own)
    picked = take_resid.astype(BF16)
    resid = resid_ref[...]
    new_low = jnp.where(
        vacated, jnp.dot(picked, in_low, preferred_element_type=F32), resid[:, :half].astype(F32)
    ).astype(BF16)
    new_high = jnp.where(
        vacated, jnp.dot(picked, in_high, preferred_element_type=F32), resid[:, half:].astype(F32)
    ).astype(BF16)
    new_ref[...] = jnp.where(first_core, new_low, new_high)
    normed = norm(jnp.concatenate([new_low, new_high], axis=1), gain_ref[...])
    logits = lax.dot_general(normed, router_ref[...], NT, preferred_element_type=F32)
    experts = logits.shape[1]
    ids_in = jnp.dot(take_ids.astype(BF16), in_low[:, :LANES], preferred_element_type=F32)
    eye = onehot(iota((rows, rows), 0) == iota((rows, rows), 1))
    mine = at_sub == me
    moved_me = jnp.sum(jnp.where(mine, movedf, 0.0), axis=0, keepdims=True)
    facts = jnp.concatenate(
        [ids_ref[...].astype(F32), moved_me, jnp.zeros((5, rows), F32)], axis=0
    ).astype(BF16)
    ids = lax.dot_general(eye, facts, NT, preferred_element_type=F32)
    moved_col = ids[:, 2:3]
    id1 = jnp.where(vacated, ids_in[:, 0:1], ids[:, 0:1]).astype(jnp.int32)
    id2 = jnp.where(vacated, ids_in[:, 1:2], ids[:, 1:2]).astype(jnp.int32)
    at_e = iota((rows, experts), 1)
    hit1, hit2 = id1 == at_e, id2 == at_e
    picked1 = jnp.sum(jnp.where(hit1, logits, 0.0), axis=1, keepdims=True)
    picked2 = jnp.sum(jnp.where(hit2, logits, 0.0), axis=1, keepdims=True)
    gate = jax.nn.sigmoid(picked1 - picked2)
    gate_ref[...] = jnp.broadcast_to(gate, gate_ref.shape)
    old1 = ids[:, 0:1].astype(jnp.int32) == at_e
    old2 = ids[:, 1:2].astype(jnp.int32) == at_e
    normal = ((old1 | old2) & (moved_col < 0.5)).astype(F32).astype(BF16)
    after = (iota((rows, rows), 0) > iota((rows, rows), 1)).astype(BF16)
    slot = jnp.dot(after, normal, preferred_element_type=F32)
    slot1 = jnp.sum(jnp.where(hit1, slot, 0.0), axis=1, keepdims=True)
    slot2 = jnp.sum(jnp.where(hit2, slot, 0.0), axis=1, keepdims=True)
    in_rank = jnp.sum(
        jnp.where(take_resid > 0.5, iota((rows, EXTRA), 1), 0), axis=1, keepdims=True
    ) - (skip + MIG)
    slot1 = jnp.where(vacated, cap + in_rank, slot1.astype(jnp.int32))
    slot2 = jnp.where(vacated, cap + in_rank, slot2.astype(jnp.int32))
    lane = iota((rows, replicas * size), 1)
    first_ref[...] = (lane == (id1 ^ me) * size + slot1).astype(F32).astype(BF16)
    second_ref[...] = (lane == (id2 ^ me) * size + slot2).astype(F32).astype(BF16)


def make_gates(own, pair, after, resid, slots, ids, gain, router, cap):
    replicas = len(own)
    size, half = own[0].shape
    rows, width = resid.shape
    vm = pl.BlockSpec(memory_space=pltpu.VMEM)
    hbm = pl.BlockSpec(memory_space=pl.ANY)
    hot = jax.ShapeDtypeStruct((rows, replicas * size), BF16)
    return pl.pallas_call(
        functools.partial(gates_kernel, cap, replicas),
        out_shape=(
            hot,
            hot,
            jax.ShapeDtypeStruct((rows, LANES), F32),
            jax.ShapeDtypeStruct((rows, half), BF16),
        ),
        in_specs=[hbm] * (2 * replicas + 2) + [vm] * 4,
        out_specs=(vm,) * 4,
        scratch_shapes=[
            pltpu.VMEM((rows, width), BF16),
            pltpu.VMEM((replicas, EXTRA, half), BF16),
            pltpu.VMEM((replicas, EXTRA, half), BF16),
            pltpu.SemaphoreType.DMA((2 * replicas + 1,)),
        ],
        compiler_params=pltpu.CompilerParams(vmem_limit_bytes=VMEM_BYTES),
        cost_estimate=pl.CostEstimate(flops=200_000_000, bytes_accessed=6_000_000, transcendentals=0),
        name="gates",
    )(*own, *pair, after, resid, slots, ids.T, gain[None, :], router.T)


def combine_kernel(replicas, *refs):
    blocks = refs[:replicas]
    first_hbm, second_hbm, gate_hbm, after_hbm, out_ref, all_v, first_ref, second_ref, gate_ref, sem = refs[
        replicas:
    ]
    size = blocks[0].shape[0]
    load(
        sem,
        (first_hbm, first_ref),
        (second_hbm, second_ref),
        (gate_hbm, gate_ref),
        *[(blocks[k], all_v.at[pl.ds(k * size, size)]) for k in range(replicas)],
    )
    gate = gate_ref[:, 0:1]
    one = jnp.dot(first_ref[...], all_v[...], preferred_element_type=F32)
    two = jnp.dot(second_ref[...], all_v[...], preferred_element_type=F32)
    out_ref[...] = (gate * one + (1.0 - gate) * two).astype(BF16)


def combine(blocks, first, second, gate, after):
    replicas = len(blocks)
    size, half = blocks[0].shape
    rows = first.shape[0]
    vm = pl.BlockSpec(memory_space=pltpu.VMEM)
    hbm = pl.BlockSpec(memory_space=pl.ANY)
    return pl.pallas_call(
        functools.partial(combine_kernel, replicas),
        out_shape=jax.ShapeDtypeStruct((rows, half), BF16),
        in_specs=[hbm] * (replicas + 4),
        out_specs=vm,
        scratch_shapes=[
            pltpu.VMEM((replicas * size, half), BF16),
            pltpu.VMEM(first.shape, BF16),
            pltpu.VMEM(second.shape, BF16),
            pltpu.VMEM(gate.shape, F32),
            pltpu.SemaphoreType.DMA((replicas + 3,)),
        ],
        compiler_params=pltpu.CompilerParams(vmem_limit_bytes=VMEM_BYTES),
        cost_estimate=pl.CostEstimate(flops=400_000_000, bytes_accessed=2_500_000, transcendentals=0),
        name="combine",
    )(*blocks, first, second, gate, after)


def choose_kernel(turn, plan_hbm, *refs):
    choices = refs[:-4]
    out_ref, plan_sm, sem, plan_sem = refs[-4:]
    load(plan_sem, (plan_hbm, plan_sm))
    index = plan_sm[0, 24 + turn]
    for i, choice in enumerate(choices):
        @pl.when(index == i)
        def _():
            load(sem, (choice, out_ref))


def choose(plan, held, turn):
    hbm = pl.BlockSpec(memory_space=pl.ANY)
    return pl.pallas_call(
        functools.partial(choose_kernel, turn),
        out_shape=jax.ShapeDtypeStruct(held[0].shape, BF16),
        in_specs=[hbm] * (1 + len(held)),
        out_specs=pl.BlockSpec(memory_space=pltpu.VMEM),
        scratch_shapes=[
            pltpu.SMEM(plan.shape, jnp.int32),
            pltpu.SemaphoreType.DMA((1,)),
            pltpu.SemaphoreType.DMA((1,)),
        ],
        compiler_params=pltpu.CompilerParams(vmem_limit_bytes=VMEM_BYTES),
        cost_estimate=pl.CostEstimate(flops=0, bytes_accessed=0, transcendentals=0),
        name="choose",
    )(plan, *held)


def patch_kernel(count, plan_hbm, *refs):
    choices = refs[:count]
    tail_hbm, out_hbm, token_ref, plan_sm, slabs, sem, slab_sem, out_sem = refs[count:]
    load(sem, (plan_hbm, plan_sm))
    index = plan_sm[0, 0]
    for i, choice in enumerate(choices):
        @pl.when(index == i)
        def _():
            load(slab_sem, (choice, slabs))
    def moves(m):
        to = plan_sm[0, 16 + m]
        return to, [
            pltpu.make_async_copy(
                slabs.at[2 * m + side], out_hbm.at[side, to], out_sem.at[2 * m + side]
            )
            for side in range(2)
        ]

    for m in range(MIG):
        to, copies = moves(m)

        @pl.when(to >= 0)
        def _():
            for copy in copies:
                copy.start()
    for m in range(MIG):
        to, copies = moves(m)

        @pl.when(to >= 0)
        def _():
            for copy in copies:
                copy.wait()
    token_ref[...] = jnp.zeros(token_ref.shape, F32)


def patch(plan, held, tail_new):
    hbm = pl.BlockSpec(memory_space=pl.ANY)
    count = len(held)
    return pl.pallas_call(
        functools.partial(patch_kernel, count),
        out_shape=(
            jax.ShapeDtypeStruct(tail_new.shape, BF16),
            jax.ShapeDtypeStruct((8, LANES), F32),
        ),
        in_specs=[hbm] * (2 + count),
        out_specs=(hbm, pl.BlockSpec(memory_space=pltpu.VMEM)),
        scratch_shapes=[
            pltpu.SMEM(plan.shape, jnp.int32),
            pltpu.VMEM(held[0].shape, BF16),
            pltpu.SemaphoreType.DMA((1,)),
            pltpu.SemaphoreType.DMA((1,)),
            pltpu.SemaphoreType.DMA((2 * MIG,)),
        ],
        input_output_aliases={1 + count: 0},
        compiler_params=pltpu.CompilerParams(vmem_limit_bytes=VMEM_BYTES),
        cost_estimate=pl.CostEstimate(flops=0, bytes_accessed=0, transcendentals=0),
        name="patch",
    )(plan, *held, tail_new)


def body(
    hidden_in, prompt_kv, tail_kv, group_of, prompt_len, tail_len, bucket_of, bias_table,
    attn_gain, w_query, w_key, w_value, w_out, ffn_gain, router_weight, expert_ids,
    w_gate, w_up, w_down, new_slot,
):
    rows, width = hidden_in.shape
    replicas = lax.axis_size("req")
    pieces = lax.axis_size("tp")
    experts = router_weight.shape[1]
    cap = -(-(5 * rows * TOP // (4 * experts)) // 16) * 16
    half = width // 2

    def across(axis, size, k):
        return lambda v: lax.ppermute(v, axis, [(i, i ^ k) for i in range(size)])

    def over_req(k):
        return across("req", replicas, k)

    def over_tp(k):
        return across("tp", pieces, k)

    low_bits, low = low_part(replicas)
    query, key_new, value_new, packet = project(
        new_slot, tail_len, hidden_in, attn_gain, w_query, w_key, w_value, tail_kv
    )
    held = [packet] + [
        over_req(h << low_bits)(packet) for h in range(1, replicas >> low_bits)
    ]
    wouts = [w_out, over_tp(1)(w_out)]
    for k in range(2, pieces, 2):
        wouts += [over_tp(k)(w) for w in wouts[:2]]
    head_out, tail_new = attention(
        query, key_new, value_new, prompt_kv, tail_kv, group_of, prompt_len, tail_len, bucket_of,
        bias_table,
    )
    heads = [head_out] + [over_tp(k)(head_out) for k in range(1, pieces)]
    slots = new_slot.reshape(replicas, rows)
    place, extra, wide, kron, plan = make_plan(
        slots, expert_ids, experts, cap, [head_out] + held[1:] + wouts[2:]
    )
    chosen = [choose(plan, held, j) for j in range(1, low)]
    resid, *blocks = dispatch(
        heads, wouts, hidden_in, ffn_gain, place, extra, wide, chosen, replicas
    )
    near, each = far_part(replicas, pieces)

    def far(f):
        pairs = []
        for r in range(replicas):
            for t in range(pieces):
                to = r ^ (near + (t >> 1) * each + f)
                pairs.append((r * pieces + t, to * pieces + t))
        return lax.ppermute(blocks[near + f], ("req", "tp"), pairs)

    distant = [far(f) for f in range(each)]
    own = [blocks[0]] + [over_req(k)(blocks[k]) for k in range(1, near)] + distant
    for turn in range(1, pieces // 2):
        own += [over_tp(2 * turn)(b) for b in distant]
    pair = [over_tp(1)(b) for b in own]
    keep, give = expert(own, pair, w_gate, w_up, w_down, pieces)
    held = held + [over_req(j + 1)(p) for j, p in enumerate(chosen)]
    back = give_back(keep, over_tp(1)(give), kron, cap, replicas)
    first, second, gate, resid_new = make_gates(
        own, pair, plan, resid, slots, expert_ids, ffn_gain, router_weight, cap
    )
    result = [back[0]] + [over_req(k)(back[k]) for k in range(1, replicas)]
    new_tail_kv, token = patch(plan, held, tail_new)
    mixed = combine(result, first, second, gate, token)
    k = 2
    while k < pieces:
        other = over_tp(k)(mixed)
        mixed = mixed.astype(F32) + other.astype(F32)
        k *= 2
        if k < pieces:
            mixed = mixed.astype(BF16)
    out_half = (resid_new.astype(F32) + mixed.astype(F32)).astype(BF16)
    out_other = over_tp(1)(out_half)
    core = lax.axis_index("tp") & 1
    out_hidden = jnp.where(
        core == 0,
        jnp.concatenate([out_half, out_other], axis=1),
        jnp.concatenate([out_other, out_half], axis=1),
    )
    return (out_hidden, new_tail_kv)


def solution(mesh):
    return jax.shard_map(
        body,
        mesh=mesh,
        in_specs=(
            P("req", None), P(None, "req", None, "tp"), P(None, "req", None, "tp"),
            P("req"), P("req"), P("req"), P(), P(None, "tp"), P(),
            P(None, "tp"), P(None, "tp"), P(None, "tp"), P("tp", None), P(), P(),
            P("req", None), P("req", None, "tp"), P("req", None, "tp"), P("req", "tp", None), P(),
        ),
        out_specs=(P("req", None), P(None, "req", None, "tp")),
        check_vma=False,
    )
```

```python
import functools
import jax
import jax.numpy as jnp
from jax import lax
from jax.experimental import pallas as pl
from jax.experimental.pallas import tpu as pltpu
from jax.sharding import PartitionSpec as P

HD = 64
EPS = 1e-06
F32 = jnp.float32
BF16 = jnp.bfloat16
NT = (((1,), (1,)), ((), ()))
LANES = 128
TILE = 128
TOP = 2
MIG = 4
EXTRA = 16
VMEM_BYTES = 64 * 1024 * 1024


def iota(shape, dim):
    return lax.broadcasted_iota(jnp.int32, shape, dim)


def onehot(hit):
    return hit.astype(F32).astype(BF16)


def attention_kernel(
    group_hbm, plen_hbm, tlen_hbm, group_row_hbm, bucket_hbm, bias_hbm,
    q_hbm, knew_hbm, vnew_hbm, prompt_hbm, tail_hbm,
    head_ref, tail_out,
    group_sm, plen_sm, tlen_sm, perm_sm, group_row, bucket_row, bias_rows, perm_v,
    pk_v, pv_v, kbuf, vbuf,
    q_v, knew_v, vnew_v, table, s_p, s_t, w_p, o_v, sorted_v, qbd_v,
    small_sem, w_sem, p_sem, in_sem, out_sem, perm_sem,
):
    rows = q_v.shape[0]
    groups, prompt_rows, cols = pv_v.shape
    tail_rows = kbuf.shape[1]
    heads = cols // HD
    per8 = 8 // heads
    per16 = 16 // heads
    width_t = per8 * tail_rows
    span_end = prompt_rows + tail_rows
    tile_rows = TILE * heads
    tiles = rows // TILE

    small = [
        pltpu.make_async_copy(src, dst, small_sem.at[i])
        for i, (src, dst) in enumerate(
            (
                (group_hbm, group_sm), (plen_hbm, plen_sm), (tlen_hbm, tlen_sm),
                (group_row_hbm, group_row), (bucket_hbm, bucket_row.at[0]),
                (bias_hbm, bias_rows),
            )
        )
    ]
    weights = [
        pltpu.make_async_copy(src, dst, w_sem.at[i])
        for i, (src, dst) in enumerate(
            ((q_hbm, q_v), (knew_hbm, knew_v), (vnew_hbm, vnew_v))
        )
    ]
    prompts = [
        pltpu.make_async_copy(prompt_hbm.at[0], pk_v, p_sem.at[0]),
        pltpu.make_async_copy(prompt_hbm.at[1], pv_v, p_sem.at[1]),
    ]

    def tile_in(t):
        at = pl.ds(t * TILE, TILE)
        return [
            pltpu.make_async_copy(tail_hbm.at[0, at], kbuf.at[at], in_sem.at[0, t]),
            pltpu.make_async_copy(tail_hbm.at[1, at], vbuf.at[at], in_sem.at[1, t]),
        ]

    def tile_out(t):
        at = pl.ds(t * TILE, TILE)
        return [
            pltpu.make_async_copy(kbuf.at[at], tail_out.at[0, at], out_sem.at[0, t]),
            pltpu.make_async_copy(vbuf.at[at], tail_out.at[1, at], out_sem.at[1, t]),
        ]

    for copy in small + weights + prompts[:1]:
        copy.start()
    for copy in small:
        copy.wait()

    for t in range(tiles):
        for copy in tile_in(t):
            copy.start()
    prompts[1].start()

    eye = onehot(iota((rows, rows), 0) == iota((rows, rows), 1))
    g_row = group_row[...]
    g_col = lax.dot_general(
        eye, jnp.broadcast_to(g_row.astype(F32), (8, rows)).astype(BF16), NT,
        preferred_element_type=F32,
    )[:, 0:1].astype(jnp.int32)
    key_row = g_row * rows + iota((1, rows), 1)
    key_col = g_col * rows + iota((rows, 1), 0)
    rank_row = jnp.sum((key_col < key_row).astype(jnp.int32), axis=0, keepdims=True)
    rank_col = jnp.sum((key_row < key_col).astype(jnp.int32), axis=1, keepdims=True)
    perm_row = jnp.sum(
        jnp.where(rank_col == iota((rows, rows), 1), iota((rows, rows), 0), 0), axis=0, keepdims=True
    )
    perm_v[...] = jnp.broadcast_to(perm_row, perm_v.shape)
    perm_copy = pltpu.make_async_copy(perm_v, perm_sm, perm_sem)
    perm_copy.start()

    span = bucket_row.shape[1]
    buckets = bias_rows.shape[1]
    below = (bucket_row[...] < iota((buckets, span), 0)).astype(jnp.int32)
    starts = jnp.sum(below, axis=1, keepdims=True)
    bias = jnp.concatenate([bias_rows[...]] * per8, axis=0)
    distance = span_end - iota(table.shape, 1)
    found = jnp.broadcast_to(bias[:, 0:1], table.shape)
    for k in range(1, buckets):
        found = jnp.where(distance >= starts[k : k + 1, 0:1], bias[:, k : k + 1], found)
    table[...] = found

    for copy in weights:
        copy.wait()
    perm_copy.wait()

    lane = iota((8, LANES), 1)
    sub = iota((8, LANES), 0)
    row16 = iota((16, cols), 0)
    minus = jnp.float32(-jnp.inf)
    pieces = prompt_rows // LANES

    def build_bias(tile):
        def step(i, carry):
            base = tile * TILE + i * per8
            out_p = [jnp.full((8, LANES), minus) for _ in range(pieces)]
            out_t = [jnp.full((8, LANES), minus) for _ in range(width_t // LANES)]
            for j in range(per8):
                r = perm_sm[0, base + j]
                length = tlen_sm[r]
                plen = plen_sm[group_sm[r]]
                start = span_end - plen - length
                block = lax.shift_right_logical(start, 7)
                off = start & (LANES - 1)
                mine = (sub >= j * heads) & (sub < (j + 1) * heads)
                window = table[:, pl.ds(pl.multiple_of(block * LANES, LANES), prompt_rows + LANES)]
                turn = (LANES - off) & (LANES - 1)
                turned = [
                    pltpu.roll(window[:, k * LANES : (k + 1) * LANES], turn, 1)
                    for k in range(pieces + 1)
                ]
                for k in range(pieces):
                    here = jnp.where(lane < LANES - off, turned[k], turned[k + 1])
                    out_p[k] = jnp.where(mine & (lane < plen - k * LANES), here, out_p[k])
                place = j * tail_rows
                k = place // LANES
                place = place - k * LANES
                own = table[:, prompt_rows : prompt_rows + LANES]
                shift = (place - tail_rows + length) & (LANES - 1)
                own = pltpu.roll(own, shift, 1)
                live = mine & (lane >= place) & (lane <= place + length)
                out_t[k] = jnp.where(live, own, out_t[k])
            at = pl.ds(pl.multiple_of(tile * tile_rows + i * 8, 8), 8)
            for k in range(pieces):
                s_p[at, k * LANES : (k + 1) * LANES] = out_p[k]
            for k in range(width_t // LANES):
                s_t[at, k * LANES : (k + 1) * LANES] = out_t[k]
            return carry

        lax.fori_loop(0, TILE // per8, step, 0, unroll=16)

    def insert(t):
        def step(i, carry):
            r = t * TILE + i
            length = tlen_sm[r]
            first = pl.multiple_of(length & 0x30, 16)
            hit = row16 == (length & 15)
            for new, buf in ((knew_v, kbuf), (vnew_v, vbuf)):
                fresh = jnp.broadcast_to(new[pl.ds(r, 1), :], (16, cols)).astype(BF16)
                old = buf[r, pl.ds(first, 16), :]
                buf[r, pl.ds(first, 16), :] = jnp.where(hit, fresh, old)
            return carry

        lax.fori_loop(0, TILE, step, 0, unroll=8)

    own_head = iota((tile_rows, cols), 0) % heads == iota((tile_rows, cols), 1) // HD
    spread_row = iota((tile_rows, rows), 0) // heads
    first_head = iota((TILE, LANES), 1) < HD

    def spread_of(tile):
        return onehot(rank_row == spread_row + tile * TILE)

    def member_of(tile):
        group8 = jnp.broadcast_to(g_row.astype(F32), (8, rows)).astype(BF16)
        return lax.dot_general(
            spread_of(tile), group8, NT, preferred_element_type=F32
        )[:, 0:1].astype(jnp.int32)

    def group_range(tile):
        low = group_sm[perm_sm[0, tile * TILE]]
        high = group_sm[perm_sm[0, tile * TILE + TILE - 1]]
        return low, high + 1

    def scores(tile, carry):
        build_bias(tile)
        at = pl.ds(pl.multiple_of(tile * tile_rows, tile_rows), tile_rows)
        qrep = jnp.dot(spread_of(tile), q_v[...], preferred_element_type=F32)
        qbd = jnp.where(own_head, qrep, 0.0)
        qbd_v[at, :] = qbd.astype(BF16)
        member = member_of(tile)

        @pl.when(tile == 0)
        def _():
            prompts[0].wait()

        def one_group(g, carry):
            part = jnp.where(member == g, qbd, 0.0).astype(BF16)
            s_p[at, :] += lax.dot_general(part, pk_v[g], NT, preferred_element_type=F32)
            return carry

        low, high = group_range(tile)
        lax.fori_loop(low, high, one_group, 0)
        for copy in tile_in(tile):
            copy.wait()

        @pl.when(tile > 0)
        def _():
            for copy in tile_out(tile - 1):
                copy.start()

        insert(tile)
        return carry

    lax.fori_loop(0, tiles, scores, 0)
    for copy in tile_out(tiles - 1):
        copy.start()
    prompts[1].wait()

    def gathered(buf, first):
        return jnp.concatenate([buf[perm_sm[0, first + j]] for j in range(per16)], axis=0)

    def values(tile, carry):
        base = pl.multiple_of(tile * tile_rows, tile_rows)
        at = pl.ds(base, tile_rows)
        for i in range(TILE // per16):
            keys = gathered(kbuf, tile * TILE + i * per16)
            here = pl.ds(pl.multiple_of(base + i * 16, 16), 16)
            got = lax.dot_general(qbd_v[here, :], keys, NT, preferred_element_type=F32)
            upper = pl.ds(pl.multiple_of(base + i * 16, 8), 8)
            lower = pl.ds(pl.multiple_of(base + i * 16 + 8, 8), 8)
            s_t[upper, :] += got[:8, :width_t]
            s_t[lower, :] += got[8:, width_t:]
        prompt_s = s_p[at, :]
        tail_s = s_t[at, :]
        top = jnp.maximum(
            jnp.max(prompt_s, axis=1, keepdims=True), jnp.max(tail_s, axis=1, keepdims=True)
        )
        pe = jnp.exp(prompt_s - top)
        te = jnp.exp(tail_s - top)
        total = jnp.sum(pe, axis=1, keepdims=True) + jnp.sum(te, axis=1, keepdims=True)
        part = 1.0 / total
        w_p[...] = (pe * part).astype(BF16)
        tw = te * part
        none = jnp.zeros((8, width_t), F32)
        for i in range(TILE // per16):
            row = i * 16
            upper = jnp.concatenate([tw[row : row + 8], none], axis=1)
            lower = jnp.concatenate([none, tw[row + 8 : row + 16]], axis=1)
            both = jnp.concatenate([upper, lower], axis=0).astype(BF16)
            vals = gathered(vbuf, tile * TILE + i * per16)
            o_t = jnp.dot(both, vals, preferred_element_type=F32)
            for b in range(cols // LANES):
                o_v[b, row : row + 16, :] = o_t[:, b * LANES : (b + 1) * LANES]
        member = member_of(tile)

        def one_group(g, carry):
            w = jnp.where(member == g, w_p[...].astype(F32), 0.0).astype(BF16)
            o_p = jnp.dot(w, pv_v[g], preferred_element_type=F32)
            for b in range(cols // LANES):
                o_v[b, 0:tile_rows, :] += o_p[:, b * LANES : (b + 1) * LANES]
            return carry

        low, high = group_range(tile)
        lax.fori_loop(low, high, one_group, 0)
        to = pl.ds(pl.multiple_of(tile * TILE, TILE), TILE)
        for b in range(cols // LANES):
            even = o_v[b, pl.ds(2 * b, TILE, stride=heads), :]
            odd = o_v[b, pl.ds(2 * b + 1, TILE, stride=heads), :]
            sorted_v[to, b * LANES : (b + 1) * LANES] = jnp.where(first_head, even, odd).astype(BF16)
        return carry

    lax.fori_loop(0, tiles, values, 0)
    unsort = onehot(rank_col == iota((rows, rows), 1))
    head_ref[...] = jnp.dot(unsort, sorted_v[...], preferred_element_type=F32).astype(BF16)
    for t in range(tiles):
        for copy in tile_out(t):
            copy.wait()


def project_kernel(
    slots_hbm, tlen_hbm, hidden_hbm, gain_hbm, wq_hbm, wk_hbm, wv_hbm, tail_hbm,
    q_ref, knew_ref, vnew_ref, packet_ref,
    slots_sm, tlen_sm, mover_sm, hidden_v, gain_v, wq_v, wk_v, wv_v, sem, slab_sem,
):
    rows = hidden_v.shape[0]
    cols = wq_v.shape[1]
    early = [
        pltpu.make_async_copy(slots_hbm, slots_sm, sem.at[0]),
        pltpu.make_async_copy(tlen_hbm, tlen_sm, sem.at[1]),
    ]
    late = [
        pltpu.make_async_copy(src, dst, sem.at[2 + i])
        for i, (src, dst) in enumerate(
            (
                (hidden_hbm, hidden_v), (gain_hbm, gain_v),
                (wq_hbm, wq_v), (wk_hbm, wk_v), (wv_hbm, wv_v),
            )
        )
    ]
    for copy in early + late:
        copy.start()
    for copy in early:
        copy.wait()
    base = lax.axis_index("req") * rows
    for m in range(MIG + 1):
        mover_sm[m] = 0

    def look(i, count):
        mover_sm[count] = i
        return count + (slots_sm[base + i] != base + i).astype(jnp.int32)

    lax.fori_loop(0, rows, look, 0, unroll=16)
    slabs = [
        pltpu.make_async_copy(
            tail_hbm.at[side, mover_sm[m]], packet_ref.at[2 * m + side], slab_sem.at[2 * m + side]
        )
        for m in range(MIG)
        for side in range(2)
    ]
    for copy in slabs:
        copy.start()
    for copy in late:
        copy.wait()
    v = hidden_v[...].astype(F32)
    normed = (
        v * lax.rsqrt(jnp.mean(v * v, axis=-1, keepdims=True) + EPS) * gain_v[...]
    ).astype(BF16)
    query = jnp.dot(normed, wq_v[...], preferred_element_type=F32).astype(BF16)
    q_ref[...] = query * jnp.asarray(HD ** (-0.5), BF16)
    for new, w in ((knew_ref, wk_v), (vnew_ref, wv_v)):
        new[...] = jnp.dot(normed, w[...], preferred_element_type=F32).astype(BF16).astype(F32)
    for copy in slabs:
        copy.wait()
    at = iota((packet_ref.shape[1], cols), 0)
    for m in range(MIG):
        r = mover_sm[m]
        for side, new in enumerate((knew_ref, vnew_ref)):
            old = packet_ref[2 * m + side].astype(F32)
            packet_ref[2 * m + side] = jnp.where(
                at == tlen_sm[r], new[pl.ds(r, 1), :], old
            ).astype(BF16)


def project(new_slot, tail_len, hidden_in, gain, w_query, w_key, w_value, tail_kv):
    rows, width = hidden_in.shape
    cols = w_query.shape[1]
    tail_rows = tail_kv.shape[2]
    vm = pl.BlockSpec(memory_space=pltpu.VMEM)
    hbm = pl.BlockSpec(memory_space=pl.ANY)
    return pl.pallas_call(
        project_kernel,
        out_shape=(
            jax.ShapeDtypeStruct((rows, cols), BF16),
            jax.ShapeDtypeStruct((rows, cols), F32),
            jax.ShapeDtypeStruct((rows, cols), F32),
            jax.ShapeDtypeStruct((2 * MIG, tail_rows, cols), BF16),
        ),
        in_specs=[hbm] * 8,
        out_specs=(vm,) * 4,
        scratch_shapes=[
            pltpu.SMEM(new_slot.shape, jnp.int32),
            pltpu.SMEM(tail_len.shape, jnp.int32),
            pltpu.SMEM((MIG + 1,), jnp.int32),
            pltpu.VMEM((rows, width), BF16),
            pltpu.VMEM((1, width), F32),
            pltpu.VMEM((width, cols), BF16),
            pltpu.VMEM((width, cols), BF16),
            pltpu.VMEM((width, cols), BF16),
            pltpu.SemaphoreType.DMA((7,)),
            pltpu.SemaphoreType.DMA((2 * MIG,)),
        ],
        compiler_params=pltpu.CompilerParams(vmem_limit_bytes=VMEM_BYTES),
        cost_estimate=pl.CostEstimate(flops=400_000_000, bytes_accessed=3_000_000, transcendentals=0),
        name="project",
    )(new_slot, tail_len, hidden_in, gain[None, :], w_query, w_key, w_value, tail_kv)


def attention(
    query, key_new, value_new, prompt_kv, tail_kv, group_of, prompt_len, tail_len, bucket_of,
    bias_table,
):
    rows, cols = query.shape
    heads = cols // HD
    groups, prompt_rows = prompt_kv.shape[1:3]
    tail_rows = tail_kv.shape[2]
    span = bucket_of.shape[0]
    buckets = bias_table.shape[0]
    table_width = 2 * prompt_rows + LANES
    width_t = 8 // heads * tail_rows
    tiles = rows // TILE
    vm = pl.BlockSpec(memory_space=pltpu.VMEM)
    hbm = pl.BlockSpec(memory_space=pl.ANY)
    return pl.pallas_call(
        attention_kernel,
        out_shape=(
            jax.ShapeDtypeStruct((rows, cols), BF16),
            jax.ShapeDtypeStruct(tail_kv.shape, BF16),
        ),
        in_specs=[hbm] * 11,
        out_specs=(vm, hbm),
        scratch_shapes=[
            pltpu.SMEM((rows,), jnp.int32),
            pltpu.SMEM((groups,), jnp.int32),
            pltpu.SMEM((rows,), jnp.int32),
            pltpu.SMEM((8, rows), jnp.int32),
            pltpu.VMEM((1, rows), jnp.int32),
            pltpu.VMEM((1, span), jnp.int32),
            pltpu.VMEM((heads, buckets), F32),
            pltpu.VMEM((8, rows), jnp.int32),
            pltpu.VMEM((groups, prompt_rows, cols), BF16),
            pltpu.VMEM((groups, prompt_rows, cols), BF16),
            pltpu.VMEM((rows, tail_rows, cols), BF16),
            pltpu.VMEM((rows, tail_rows, cols), BF16),
            pltpu.VMEM((rows, cols), BF16),
            pltpu.VMEM((rows, cols), F32),
            pltpu.VMEM((rows, cols), F32),
            pltpu.VMEM((8, table_width), F32),
            pltpu.VMEM((rows * heads, prompt_rows), F32),
            pltpu.VMEM((rows * heads, width_t), F32),
            pltpu.VMEM((TILE * heads, prompt_rows), BF16),
            pltpu.VMEM((cols // LANES, TILE * heads + 8, LANES), F32),
            pltpu.VMEM((rows, cols), BF16),
            pltpu.VMEM((rows * heads, cols), BF16),
            pltpu.SemaphoreType.DMA((6,)),
            pltpu.SemaphoreType.DMA((3,)),
            pltpu.SemaphoreType.DMA((2,)),
            pltpu.SemaphoreType.DMA((2, tiles)),
            pltpu.SemaphoreType.DMA((2, tiles)),
            pltpu.SemaphoreType.DMA,
        ],
        compiler_params=pltpu.CompilerParams(vmem_limit_bytes=VMEM_BYTES),
        cost_estimate=pl.CostEstimate(flops=8_000_000_000, bytes_accessed=45_000_000, transcendentals=700_000),
        name="attention",
    )(
        group_of, prompt_len, tail_len, group_of[None, :], bucket_of, bias_table.T,
        query, key_new, value_new, prompt_kv, tail_kv,
    )


def block_rows(cap):
    return cap + EXTRA


def low_part(replicas):
    bits = (replicas.bit_length() - 1) // 2
    return bits, 1 << bits


def plan_kernel(cap, slots_ref, ids_ref, *refs):
    place_ref, extra_ref, wide_ref, kron_ref, plan_ref, slot_s = refs[-6:]
    replicas, rows = slots_ref.shape
    experts = slot_s.shape[0]
    size = place_ref.shape[0] // replicas
    me = lax.axis_index("req")
    ns = slots_ref[...]
    at_sub = iota((replicas, rows), 0)
    at_lane = iota((replicas, rows), 1)
    moved = ns != at_sub * rows + at_lane
    tri = (iota((rows, rows), 0) < iota((rows, rows), 1)).astype(BF16)
    rank = jnp.dot(moved.astype(F32).astype(BF16), tri, preferred_element_type=F32).astype(jnp.int32)
    going_to = ns // rows
    mine = at_sub == me

    def own(values):
        return jnp.sum(jnp.where(mine, values, 0), axis=0, keepdims=True)

    moved_me = own(moved.astype(jnp.int32))
    rank_me = own(rank)
    to_me = own(going_to)
    ids_rows = ids_ref[...]
    at_e = iota((experts, rows), 0)
    hit = (ids_rows[0:1] == at_e) | (ids_rows[1:2] == at_e)
    normal = (hit & (moved_me == 0)).astype(F32).astype(BF16)
    slot = jnp.dot(normal, tri, preferred_element_type=F32).astype(jnp.int32)
    slot_s[...] = jnp.where(hit, jnp.where(moved_me > 0, cap + rank_me, slot), -1)
    at_row = iota((size, rows), 0)
    at_extra = iota((EXTRA, rows), 0)
    for k in range(replicas):
        e = me ^ k
        block = pl.ds(k * size, size)
        row = slot_s[pl.ds(e, 1), :]
        leaving = jnp.where((moved_me > 0) & (to_me == e), rank_me, -100)
        place_ref[block, :] = onehot(at_row == row)
        more = pl.ds(k * EXTRA, EXTRA)
        extra_ref[more, 0:rows] = onehot(at_extra == leaving + MIG)
        extra_ref[more, rows:] = onehot(at_extra == leaving + 2 * MIG)
    lane = iota(wide_ref.shape, 1)
    eye = onehot(iota((rows, rows), 0) == iota((rows, rows), 1))
    facts = jnp.concatenate([ids_rows, jnp.zeros((6, rows), jnp.int32)], axis=0)
    columns = lax.dot_general(
        eye, facts.astype(F32).astype(BF16), NT, preferred_element_type=F32
    )
    wide = jnp.where(lane == 0, columns[:, 0:1], jnp.where(lane == 1, columns[:, 1:2], 0.0))
    wide_ref[...] = wide.astype(BF16)
    dest = jnp.max(jnp.where(moved, going_to, -1), axis=1, keepdims=True)
    dest = jnp.where(dest < 0, iota((replicas, 1), 0), dest)
    hot = (dest == iota((replicas, replicas), 1)).astype(F32).astype(BF16)
    span = replicas * EXTRA
    mixed_row = (iota((span, replicas), 0) // EXTRA) ^ me
    a = (mixed_row == iota((span, replicas), 1)).astype(F32).astype(BF16)
    by_source = lax.dot_general(a, hot, NT, preferred_element_type=F32).astype(BF16)
    pairs = lax.dot_general(by_source, a, NT, preferred_element_type=F32)
    same = iota((span, span), 0) % EXTRA == iota((span, span), 1) % EXTRA
    kron_ref[...] = jnp.where(same, pairs, 0.0).astype(BF16)
    sub1 = iota((replicas, 1), 0)

    def source_of(who):
        return jnp.sum(jnp.where(dest == who, sub1, 0), axis=0, keepdims=True)

    low_bits, low = low_part(replicas)
    diff = source_of(me) ^ me
    turn = diff & (low - 1)
    final = jnp.where(turn == 0, diff >> low_bits, (replicas >> low_bits) + turn - 1)
    lane8 = iota((8, LANES), 1)
    plan = jnp.where(lane8 == 0, final, -1)
    for j in range(1, low):
        apart = source_of(me ^ j) ^ me
        plan = jnp.where(lane8 == 24 + j, apart >> low_bits, plan)
    lane1 = iota((1, rows), 1)
    for m in range(MIG):
        is_m = (moved_me > 0) & (rank_me == m)
        mover = jnp.sum(jnp.where(is_m, lane1, 0), axis=1, keepdims=True)
        plan = jnp.where(lane8 == 8 + m, mover, plan)
        come = moved & (going_to == me) & (rank == m)
        to = jnp.sum(jnp.where(come, ns - me * rows + 1, 0), axis=1, keepdims=True)
        to = jnp.sum(to, axis=0, keepdims=True) - 1
        plan = jnp.where(lane8 == 16 + m, to, plan)
    plan_ref[...] = plan


def make_plan(slots, expert_ids, experts, cap, after):
    replicas, rows = slots.shape
    size = block_rows(cap)
    vm = pl.BlockSpec(memory_space=pltpu.VMEM)
    span = replicas * EXTRA
    return pl.pallas_call(
        functools.partial(plan_kernel, cap),
        out_shape=(
            jax.ShapeDtypeStruct((replicas * size, rows), BF16),
            jax.ShapeDtypeStruct((replicas * EXTRA, 2 * rows), BF16),
            jax.ShapeDtypeStruct((rows, LANES), BF16),
            jax.ShapeDtypeStruct((span, span), BF16),
            jax.ShapeDtypeStruct((8, LANES), jnp.int32),
        ),
        in_specs=[vm, vm] + [pl.BlockSpec(memory_space=pl.ANY)] * len(after),
        out_specs=(vm,) * 5,
        scratch_shapes=[pltpu.VMEM((experts, rows), jnp.int32)],
        compiler_params=pltpu.CompilerParams(vmem_limit_bytes=VMEM_BYTES),
        cost_estimate=pl.CostEstimate(flops=0, bytes_accessed=0, transcendentals=0),
        name="plan",
    )(slots, expert_ids.T, *after)


def load(sem, *pairs):
    made = [pltpu.make_async_copy(src, dst, sem.at[i]) for i, (src, dst) in enumerate(pairs)]
    for copy in made:
        copy.start()
    for copy in made:
        copy.wait()


def norm(values, gain):
    v = values.astype(F32)
    return (v * lax.rsqrt(jnp.mean(v * v, axis=-1, keepdims=True) + EPS) * gain).astype(BF16)


def far_part(replicas, pieces):
    return replicas // 2, replicas // pieces


def dispatch_kernel(pieces, replicas, *refs):
    near, each = far_part(replicas, pieces)
    count = near + each
    heads_hbm = refs[:pieces]
    wout_hbm = refs[pieces : 2 * pieces]
    hidden_hbm, gain_ref, place_hbm, extra_hbm, wide_hbm = refs[2 * pieces : 2 * pieces + 5]
    refs = refs[-11 - count :]
    resid_ref = refs[0]
    outs = refs[1 : 1 + count]
    head_v, wout_v, stack, hidden_ref, place_ref, extra_ref, wide_ref, extra_v, sem, more = refs[1 + count :]
    tp = lax.axis_index("tp")
    core = tp & 1
    rows, width = hidden_ref.shape
    cols = width // pieces
    half = width // 2

    def copies():
        made = []
        for k in range(pieces):
            at = pl.ds(pl.multiple_of((tp ^ k) * cols, cols), cols)
            made.append(pltpu.make_async_copy(wout_hbm[k], wout_v.at[at], sem.at[0, k]))
            made.append(pltpu.make_async_copy(heads_hbm[k], head_v.at[:, at], sem.at[1, k]))
        made.append(pltpu.make_async_copy(hidden_hbm, hidden_ref, more.at[0]))
        return made

    late = [
        pltpu.make_async_copy(place_hbm, place_ref, more.at[1]),
        pltpu.make_async_copy(extra_hbm, extra_ref, more.at[2]),
        pltpu.make_async_copy(wide_hbm, wide_ref, more.at[3]),
    ]

    for copy in copies() + late:
        copy.start()
    for copy in copies():
        copy.wait()
    attn = jnp.dot(head_v[...], wout_v[...], preferred_element_type=F32)
    resid = (hidden_ref[...].astype(F32) + attn).astype(BF16)
    resid_ref[...] = resid
    normed = norm(resid, gain_ref[...])
    first = core == 0
    stack[0:rows, :] = jnp.where(first, normed[:, :half], normed[:, half:])
    stack[rows : 2 * rows, :] = jnp.where(first, resid[:, :half], resid[:, half:])
    for copy in late:
        copy.wait()
    size = place_ref.shape[0] // replicas
    extra_v[...] = jnp.dot(extra_ref[:, 0:rows], stack[rows:, :], preferred_element_type=F32)
    extra_v[:, 0:LANES] += jnp.dot(extra_ref[:, rows:], wide_ref[...], preferred_element_type=F32)
    for i in range(count):
        k = i if i < near else near + (tp >> 1) * each + (i - near)
        block = jnp.dot(
            place_ref[pl.ds(k * size, size), :], stack[0:rows, :], preferred_element_type=F32
        )
        outs[i][0 : size - EXTRA, :] = block[: size - EXTRA].astype(BF16)
        outs[i][size - EXTRA :, :] = (
            block[size - EXTRA :] + extra_v[pl.ds(k * EXTRA, EXTRA), :]
        ).astype(BF16)


def dispatch(heads, wouts, hidden, gain, place, extra, wide, after, replicas):
    rows, width = hidden.shape
    pieces = len(heads)
    count = sum(far_part(replicas, pieces))
    half = width // 2
    size = place.shape[0] // replicas
    vm = pl.BlockSpec(memory_space=pltpu.VMEM)
    hbm = pl.BlockSpec(memory_space=pl.ANY)
    return pl.pallas_call(
        functools.partial(dispatch_kernel, pieces, replicas),
        out_shape=(jax.ShapeDtypeStruct((rows, width), BF16),)
        + tuple(jax.ShapeDtypeStruct((size, half), BF16) for _ in range(count)),
        in_specs=[hbm] * (2 * pieces) + [hbm, vm, hbm, hbm, hbm] + [hbm] * len(after),
        out_specs=(vm,) * (1 + count),
        scratch_shapes=[
            pltpu.VMEM((rows, width), BF16),
            pltpu.VMEM((width, width), BF16),
            pltpu.VMEM((2 * rows, half), BF16),
            pltpu.VMEM((rows, width), BF16),
            pltpu.VMEM(place.shape, BF16),
            pltpu.VMEM(extra.shape, BF16),
            pltpu.VMEM(wide.shape, BF16),
            pltpu.VMEM((extra.shape[0], half), F32),
            pltpu.SemaphoreType.DMA((2, pieces)),
            pltpu.SemaphoreType.DMA((5,)),
        ],
        compiler_params=pltpu.CompilerParams(vmem_limit_bytes=VMEM_BYTES),
        cost_estimate=pl.CostEstimate(flops=1_200_000_000, bytes_accessed=6_000_000, transcendentals=0),
        name="dispatch",
    )(*heads, *wouts, hidden, gain[None, :], place, extra, wide, *after)


def pieces_of(total, step):
    return [(at, min(step, total - at)) for at in range(0, total, step)]


def expert_kernel(replicas, pieces, *refs):
    own = refs[:replicas]
    pair = refs[replicas : 2 * replicas]
    wg_hbm, wu_hbm, wd_hbm = refs[2 * replicas : 2 * replicas + 3]
    keep_hbm, give_hbm, keep_ref, give_ref, x_own, x_pair, wg, wu, wd, act, sem, xsem, osem = refs[-13:]
    tp = lax.axis_index("tp")
    core = tp & 1
    size, half = own[0].shape
    near, each = far_part(replicas, pieces)
    hidden = wg.shape[0]
    chunks = pieces_of(hidden, 256)
    blocks = []
    for k in range(replicas):
        there = k
        if k >= near:
            turn, f = divmod(k - near, each)
            there = near + ((tp >> 1) ^ turn) * each + f
        at = pl.ds(there * size, size)
        blocks.append(pltpu.make_async_copy(own[k], x_own.at[at], xsem.at[0, k]))
        blocks.append(pltpu.make_async_copy(pair[k], x_pair.at[at], xsem.at[1, k]))
    wide = [
        [
            pltpu.make_async_copy(src.at[0, pl.ds(at, n)], dst.at[pl.ds(at, n)], sem.at[side, c])
            for side, (src, dst) in enumerate(((wg_hbm, wg), (wu_hbm, wu)))
        ]
        for c, (at, n) in enumerate(chunks)
    ]
    down = pltpu.make_async_copy(wd_hbm.at[0], wd, sem.at[2, 0])
    for copy in wide[0] + blocks + sum(wide[1:], []) + [down]:
        copy.start()
    for copy in blocks:
        copy.wait()
    here = pl.ds(pl.multiple_of(core * half, half), half)
    there = pl.ds(pl.multiple_of((1 - core) * half, half), half)
    a, b = x_own[...], x_pair[...]

    def product(w, rows):
        return lax.dot_general(a, w[rows, here], NT, preferred_element_type=F32) + lax.dot_general(
            b, w[rows, there], NT, preferred_element_type=F32
        )

    for c, (at, n) in enumerate(chunks):
        for copy in wide[c]:
            copy.wait()
        rows = pl.ds(at, n)
        gate = product(wg, rows)
        act[:, at : at + n] = (jax.nn.gelu(gate, approximate=True) * product(wu, rows)).astype(BF16)
    down.wait()
    leave = [
        pltpu.make_async_copy(give_ref, give_hbm, osem.at[0]),
        pltpu.make_async_copy(keep_ref, keep_hbm, osem.at[1]),
    ]
    give_ref[...] = jnp.dot(act[...], wd[:, there], preferred_element_type=F32).astype(BF16)
    leave[0].start()
    keep_ref[...] = jnp.dot(act[...], wd[:, here], preferred_element_type=F32).astype(BF16)
    leave[1].start()
    for copy in leave:
        copy.wait()


def expert(own, pair, w_gate, w_up, w_down, pieces):
    replicas = len(own)
    size, half = own[0].shape
    _, width, hidden = w_gate.shape
    total = replicas * size
    hbm = pl.BlockSpec(memory_space=pl.ANY)
    shape = jax.ShapeDtypeStruct((total, half), BF16)
    return pl.pallas_call(
        functools.partial(expert_kernel, replicas, pieces),
        out_shape=(shape, shape),
        in_specs=[hbm] * (2 * replicas + 3),
        out_specs=(hbm, hbm),
        scratch_shapes=[
            pltpu.VMEM((total, half), BF16),
            pltpu.VMEM((total, half), BF16),
            pltpu.VMEM((total, half), BF16),
            pltpu.VMEM((total, half), BF16),
            pltpu.VMEM((hidden, width), BF16),
            pltpu.VMEM((hidden, width), BF16),
            pltpu.VMEM((hidden, width), BF16),
            pltpu.VMEM((total, hidden), BF16),
            pltpu.SemaphoreType.DMA((3, len(pieces_of(hidden, 256)))),
            pltpu.SemaphoreType.DMA((2, replicas)),
            pltpu.SemaphoreType.DMA((2,)),
        ],
        compiler_params=pltpu.CompilerParams(vmem_limit_bytes=VMEM_BYTES),
        cost_estimate=pl.CostEstimate(flops=3_400_000_000, bytes_accessed=8_000_000, transcendentals=600_000),
        name="expert",
    )(*own, *pair, jnp.swapaxes(w_gate, 1, 2), jnp.swapaxes(w_up, 1, 2), w_down)


def give_back_kernel(cap, keep_hbm, got_hbm, kron_hbm, *refs):
    replicas = len(refs) - 5
    outs = refs[:replicas]
    rows_v, keep_ref, got_ref, kron_ref, sem = refs[replicas:]
    load(sem, (keep_hbm, keep_ref), (got_hbm, got_ref), (kron_hbm, kron_ref))
    size = outs[0].shape[0]
    for k in range(replicas):
        at = slice(k * size, (k + 1) * size)
        both = keep_ref[at, :].astype(F32) + got_ref[at, :].astype(F32)
        outs[k][...] = both.astype(BF16)
        rows_v[k * EXTRA : (k + 1) * EXTRA, :] = both[size - EXTRA :].astype(BF16)
    moved = jnp.dot(kron_ref[...], rows_v[...], preferred_element_type=F32)
    first = iota((EXTRA, 1), 0) >= cap - (size - EXTRA)
    for k in range(replicas):
        at = slice(k * EXTRA, (k + 1) * EXTRA)
        outs[k][size - EXTRA :, :] = jnp.where(
            first, moved[at], rows_v[at, :].astype(F32)
        ).astype(BF16)


def give_back(keep, got, kron, cap, replicas):
    total, half = keep.shape
    size = total // replicas
    vm = pl.BlockSpec(memory_space=pltpu.VMEM)
    hbm = pl.BlockSpec(memory_space=pl.ANY)
    return pl.pallas_call(
        functools.partial(give_back_kernel, cap),
        out_shape=tuple(jax.ShapeDtypeStruct((size, half), BF16) for _ in range(replicas)),
        in_specs=[hbm] * 3,
        out_specs=(vm,) * replicas,
        scratch_shapes=[
            pltpu.VMEM((replicas * EXTRA, half), BF16),
            pltpu.VMEM((total, half), BF16),
            pltpu.VMEM((total, half), BF16),
            pltpu.VMEM(kron.shape, BF16),
            pltpu.SemaphoreType.DMA((3,)),
        ],
        compiler_params=pltpu.CompilerParams(vmem_limit_bytes=VMEM_BYTES),
        cost_estimate=pl.CostEstimate(flops=30_000_000, bytes_accessed=2_500_000, transcendentals=0),
        name="give_back",
    )(keep, got, kron)


def gates_kernel(cap, replicas, *refs):
    own = refs[:replicas]
    pair = refs[replicas : 2 * replicas]
    (after_hbm, resid_hbm, slots_ref, ids_ref, gain_ref, router_ref) = refs[
        2 * replicas : 2 * replicas + 6
    ]
    (first_ref, second_ref, gate_ref, new_ref, resid_ref, own_v, pair_v, sem) = refs[2 * replicas + 6 :]
    me = lax.axis_index("req")
    core = lax.axis_index("tp") & 1
    rows, width = resid_ref.shape
    half = width // 2
    size = own[0].shape[0]
    low = pl.ds(size - EXTRA, EXTRA)
    skip = 0
    load(
        sem,
        (resid_hbm, resid_ref),
        *[(own[k].at[low], own_v.at[k]) for k in range(replicas)],
        *[(pair[k].at[low], pair_v.at[k]) for k in range(replicas)],
    )
    ns = slots_ref[...]
    count = ns.shape[0]
    at_sub = iota((count, rows), 0)
    moved = ns != at_sub * rows + iota((count, rows), 1)
    before = (iota((rows, rows), 0) < iota((rows, rows), 1)).astype(BF16)
    movedf = moved.astype(F32)
    rank = jnp.dot(movedf.astype(BF16), before, preferred_element_type=F32)
    coming = moved & (ns // rows == me)
    slot_to = jnp.sum(jnp.where(coming, ns - me * rows + 1, 0), axis=0, keepdims=True) - 1
    rank_in = jnp.sum(jnp.where(coming, rank, 0.0), axis=0, keepdims=True).astype(jnp.int32)
    landing = (iota((rows, rows), 0) == slot_to).astype(F32).astype(BF16)
    at16 = iota((EXTRA, rows), 0)

    def taken(offset):
        hot = (at16 == rank_in + (skip + offset)) & (slot_to >= 0)
        return lax.dot_general(landing, hot.astype(F32).astype(BF16), NT, preferred_element_type=F32)

    take_resid = taken(MIG)
    take_ids = taken(2 * MIG)
    vacated = jnp.sum(take_resid, axis=1, keepdims=True) > 0.5
    in_own = own_v[0].astype(F32)
    in_pair = pair_v[0].astype(F32)
    for k in range(1, replicas):
        in_own = in_own + own_v[k].astype(F32)
        in_pair = in_pair + pair_v[k].astype(F32)
    in_own, in_pair = in_own.astype(BF16), in_pair.astype(BF16)
    first_core = core == 0
    in_low = jnp.where(first_core, in_own, in_pair)
    in_high = jnp.where(first_core, in_pair, in_own)
    picked = take_resid.astype(BF16)
    resid = resid_ref[...]
    new_low = jnp.where(
        vacated, jnp.dot(picked, in_low, preferred_element_type=F32), resid[:, :half].astype(F32)
    ).astype(BF16)
    new_high = jnp.where(
        vacated, jnp.dot(picked, in_high, preferred_element_type=F32), resid[:, half:].astype(F32)
    ).astype(BF16)
    new_ref[...] = jnp.where(first_core, new_low, new_high)
    normed = norm(jnp.concatenate([new_low, new_high], axis=1), gain_ref[...])
    logits = lax.dot_general(normed, router_ref[...], NT, preferred_element_type=F32)
    experts = logits.shape[1]
    ids_in = jnp.dot(take_ids.astype(BF16), in_low[:, :LANES], preferred_element_type=F32)
    eye = onehot(iota((rows, rows), 0) == iota((rows, rows), 1))
    mine = at_sub == me
    moved_me = jnp.sum(jnp.where(mine, movedf, 0.0), axis=0, keepdims=True)
    facts = jnp.concatenate(
        [ids_ref[...].astype(F32), moved_me, jnp.zeros((5, rows), F32)], axis=0
    ).astype(BF16)
    ids = lax.dot_general(eye, facts, NT, preferred_element_type=F32)
    moved_col = ids[:, 2:3]
    id1 = jnp.where(vacated, ids_in[:, 0:1], ids[:, 0:1]).astype(jnp.int32)
    id2 = jnp.where(vacated, ids_in[:, 1:2], ids[:, 1:2]).astype(jnp.int32)
    at_e = iota((rows, experts), 1)
    hit1, hit2 = id1 == at_e, id2 == at_e
    picked1 = jnp.sum(jnp.where(hit1, logits, 0.0), axis=1, keepdims=True)
    picked2 = jnp.sum(jnp.where(hit2, logits, 0.0), axis=1, keepdims=True)
    gate = jax.nn.sigmoid(picked1 - picked2)
    gate_ref[...] = jnp.broadcast_to(gate, gate_ref.shape)
    old1 = ids[:, 0:1].astype(jnp.int32) == at_e
    old2 = ids[:, 1:2].astype(jnp.int32) == at_e
    normal = ((old1 | old2) & (moved_col < 0.5)).astype(F32).astype(BF16)
    after = (iota((rows, rows), 0) > iota((rows, rows), 1)).astype(BF16)
    slot = jnp.dot(after, normal, preferred_element_type=F32)
    slot1 = jnp.sum(jnp.where(hit1, slot, 0.0), axis=1, keepdims=True)
    slot2 = jnp.sum(jnp.where(hit2, slot, 0.0), axis=1, keepdims=True)
    in_rank = jnp.sum(
        jnp.where(take_resid > 0.5, iota((rows, EXTRA), 1), 0), axis=1, keepdims=True
    ) - (skip + MIG)
    slot1 = jnp.where(vacated, cap + in_rank, slot1.astype(jnp.int32))
    slot2 = jnp.where(vacated, cap + in_rank, slot2.astype(jnp.int32))
    lane = iota((rows, replicas * size), 1)
    first_ref[...] = (lane == (id1 ^ me) * size + slot1).astype(F32).astype(BF16)
    second_ref[...] = (lane == (id2 ^ me) * size + slot2).astype(F32).astype(BF16)


def make_gates(own, pair, after, resid, slots, ids, gain, router, cap):
    replicas = len(own)
    size, half = own[0].shape
    rows, width = resid.shape
    vm = pl.BlockSpec(memory_space=pltpu.VMEM)
    hbm = pl.BlockSpec(memory_space=pl.ANY)
    hot = jax.ShapeDtypeStruct((rows, replicas * size), BF16)
    return pl.pallas_call(
        functools.partial(gates_kernel, cap, replicas),
        out_shape=(
            hot,
            hot,
            jax.ShapeDtypeStruct((rows, LANES), F32),
            jax.ShapeDtypeStruct((rows, half), BF16),
        ),
        in_specs=[hbm] * (2 * replicas + 2) + [vm] * 4,
        out_specs=(vm,) * 4,
        scratch_shapes=[
            pltpu.VMEM((rows, width), BF16),
            pltpu.VMEM((replicas, EXTRA, half), BF16),
            pltpu.VMEM((replicas, EXTRA, half), BF16),
            pltpu.SemaphoreType.DMA((2 * replicas + 1,)),
        ],
        compiler_params=pltpu.CompilerParams(vmem_limit_bytes=VMEM_BYTES),
        cost_estimate=pl.CostEstimate(flops=200_000_000, bytes_accessed=6_000_000, transcendentals=0),
        name="gates",
    )(*own, *pair, after, resid, slots, ids.T, gain[None, :], router.T)


def combine_kernel(replicas, *refs):
    blocks = refs[:replicas]
    first_hbm, second_hbm, gate_hbm, after_hbm, out_ref, all_v, first_ref, second_ref, gate_ref, sem = refs[
        replicas:
    ]
    size = blocks[0].shape[0]
    load(
        sem,
        (first_hbm, first_ref),
        (second_hbm, second_ref),
        (gate_hbm, gate_ref),
        *[(blocks[k], all_v.at[pl.ds(k * size, size)]) for k in range(replicas)],
    )
    gate = gate_ref[:, 0:1]
    one = jnp.dot(first_ref[...], all_v[...], preferred_element_type=F32)
    two = jnp.dot(second_ref[...], all_v[...], preferred_element_type=F32)
    out_ref[...] = (gate * one + (1.0 - gate) * two).astype(BF16)


def combine(blocks, first, second, gate, after):
    replicas = len(blocks)
    size, half = blocks[0].shape
    rows = first.shape[0]
    vm = pl.BlockSpec(memory_space=pltpu.VMEM)
    hbm = pl.BlockSpec(memory_space=pl.ANY)
    return pl.pallas_call(
        functools.partial(combine_kernel, replicas),
        out_shape=jax.ShapeDtypeStruct((rows, half), BF16),
        in_specs=[hbm] * (replicas + 4),
        out_specs=vm,
        scratch_shapes=[
            pltpu.VMEM((replicas * size, half), BF16),
            pltpu.VMEM(first.shape, BF16),
            pltpu.VMEM(second.shape, BF16),
            pltpu.VMEM(gate.shape, F32),
            pltpu.SemaphoreType.DMA((replicas + 3,)),
        ],
        compiler_params=pltpu.CompilerParams(vmem_limit_bytes=VMEM_BYTES),
        cost_estimate=pl.CostEstimate(flops=400_000_000, bytes_accessed=2_500_000, transcendentals=0),
        name="combine",
    )(*blocks, first, second, gate, after)


def choose_kernel(turn, plan_hbm, *refs):
    choices = refs[:-4]
    out_ref, plan_sm, sem, plan_sem = refs[-4:]
    load(plan_sem, (plan_hbm, plan_sm))
    index = plan_sm[0, 24 + turn]
    for i, choice in enumerate(choices):
        @pl.when(index == i)
        def _():
            load(sem, (choice, out_ref))


def choose(plan, held, turn):
    hbm = pl.BlockSpec(memory_space=pl.ANY)
    return pl.pallas_call(
        functools.partial(choose_kernel, turn),
        out_shape=jax.ShapeDtypeStruct(held[0].shape, BF16),
        in_specs=[hbm] * (1 + len(held)),
        out_specs=pl.BlockSpec(memory_space=pltpu.VMEM),
        scratch_shapes=[
            pltpu.SMEM(plan.shape, jnp.int32),
            pltpu.SemaphoreType.DMA((1,)),
            pltpu.SemaphoreType.DMA((1,)),
        ],
        compiler_params=pltpu.CompilerParams(vmem_limit_bytes=VMEM_BYTES),
        cost_estimate=pl.CostEstimate(flops=0, bytes_accessed=0, transcendentals=0),
        name="choose",
    )(plan, *held)


def patch_kernel(count, plan_hbm, *refs):
    choices = refs[:count]
    tail_hbm, out_hbm, token_ref, plan_sm, slabs, sem, slab_sem, out_sem = refs[count:]
    load(sem, (plan_hbm, plan_sm))
    index = plan_sm[0, 0]
    for i, choice in enumerate(choices):
        @pl.when(index == i)
        def _():
            load(slab_sem, (choice, slabs))
    def moves(m):
        to = plan_sm[0, 16 + m]
        return to, [
            pltpu.make_async_copy(
                slabs.at[2 * m + side],
                out_hbm.at[side, jnp.maximum(to, 0)],
                out_sem.at[2 * m + side],
            )
            for side in range(2)
        ]

    for m in range(MIG):
        to, copies = moves(m)

        @pl.when(to >= 0)
        def _():
            for copy in copies:
                copy.start()
    for m in range(MIG):
        to, copies = moves(m)

        @pl.when(to >= 0)
        def _():
            for copy in copies:
                copy.wait()
    token_ref[...] = jnp.zeros(token_ref.shape, F32)


def patch(plan, held, tail_new):
    hbm = pl.BlockSpec(memory_space=pl.ANY)
    count = len(held)
    return pl.pallas_call(
        functools.partial(patch_kernel, count),
        out_shape=(
            jax.ShapeDtypeStruct(tail_new.shape, BF16),
            jax.ShapeDtypeStruct((8, LANES), F32),
        ),
        in_specs=[hbm] * (2 + count),
        out_specs=(hbm, pl.BlockSpec(memory_space=pltpu.VMEM)),
        scratch_shapes=[
            pltpu.SMEM(plan.shape, jnp.int32),
            pltpu.VMEM(held[0].shape, BF16),
            pltpu.SemaphoreType.DMA((1,)),
            pltpu.SemaphoreType.DMA((1,)),
            pltpu.SemaphoreType.DMA((2 * MIG,)),
        ],
        input_output_aliases={1 + count: 0},
        compiler_params=pltpu.CompilerParams(vmem_limit_bytes=VMEM_BYTES),
        cost_estimate=pl.CostEstimate(flops=0, bytes_accessed=0, transcendentals=0),
        name="patch",
    )(plan, *held, tail_new)


def body(
    hidden_in, prompt_kv, tail_kv, group_of, prompt_len, tail_len, bucket_of, bias_table,
    attn_gain, w_query, w_key, w_value, w_out, ffn_gain, router_weight, expert_ids,
    w_gate, w_up, w_down, new_slot,
):
    rows, width = hidden_in.shape
    replicas = lax.axis_size("req")
    pieces = lax.axis_size("tp")
    experts = router_weight.shape[1]
    cap = -(-(5 * rows * TOP // (4 * experts)) // 16) * 16
    half = width // 2

    def across(axis, size, k):
        return lambda v: lax.ppermute(v, axis, [(i, i ^ k) for i in range(size)])

    def over_req(k):
        return across("req", replicas, k)

    def over_tp(k):
        return across("tp", pieces, k)

    low_bits, low = low_part(replicas)
    query, key_new, value_new, packet = project(
        new_slot, tail_len, hidden_in, attn_gain, w_query, w_key, w_value, tail_kv
    )
    held = [packet] + [
        over_req(h << low_bits)(packet) for h in range(1, replicas >> low_bits)
    ]
    wouts = [w_out, over_tp(1)(w_out)]
    for k in range(2, pieces, 2):
        wouts += [over_tp(k)(w) for w in wouts[:2]]
    head_out, tail_new = attention(
        query, key_new, value_new, prompt_kv, tail_kv, group_of, prompt_len, tail_len, bucket_of,
        bias_table,
    )
    heads = [head_out] + [over_tp(k)(head_out) for k in range(1, pieces)]
    slots = new_slot.reshape(replicas, rows)
    place, extra, wide, kron, plan = make_plan(
        slots, expert_ids, experts, cap, [head_out] + held[1:] + wouts[2:]
    )
    chosen = [choose(plan, held, j) for j in range(1, low)]
    resid, *blocks = dispatch(
        heads, wouts, hidden_in, ffn_gain, place, extra, wide, chosen, replicas
    )
    near, each = far_part(replicas, pieces)

    def far(f):
        pairs = []
        for r in range(replicas):
            for t in range(pieces):
                to = r ^ (near + (t >> 1) * each + f)
                pairs.append((r * pieces + t, to * pieces + t))
        return lax.ppermute(blocks[near + f], ("req", "tp"), pairs)

    distant = [far(f) for f in range(each)]
    own = [blocks[0]] + [over_req(k)(blocks[k]) for k in range(1, near)] + distant
    for turn in range(1, pieces // 2):
        own += [over_tp(2 * turn)(b) for b in distant]
    pair = [over_tp(1)(b) for b in own]
    keep, give = expert(own, pair, w_gate, w_up, w_down, pieces)
    held = held + [over_req(j + 1)(p) for j, p in enumerate(chosen)]
    back = give_back(keep, over_tp(1)(give), kron, cap, replicas)
    first, second, gate, resid_new = make_gates(
        own, pair, plan, resid, slots, expert_ids, ffn_gain, router_weight, cap
    )
    result = [back[0]] + [over_req(k)(back[k]) for k in range(1, replicas)]
    new_tail_kv, token = patch(plan, held, tail_new)
    mixed = combine(result, first, second, gate, token)
    k = 2
    while k < pieces:
        other = over_tp(k)(mixed)
        mixed = mixed.astype(F32) + other.astype(F32)
        k *= 2
        if k < pieces:
            mixed = mixed.astype(BF16)
    out_half = (resid_new.astype(F32) + mixed.astype(F32)).astype(BF16)
    out_other = over_tp(1)(out_half)
    core = lax.axis_index("tp") & 1
    out_hidden = jnp.where(
        core == 0,
        jnp.concatenate([out_half, out_other], axis=1),
        jnp.concatenate([out_other, out_half], axis=1),
    )
    return (out_hidden, new_tail_kv)


def solution(mesh):
    return jax.shard_map(
        body,
        mesh=mesh,
        in_specs=(
            P("req", None), P(None, "req", None, "tp"), P(None, "req", None, "tp"),
            P("req"), P("req"), P("req"), P(), P(None, "tp"), P(),
            P(None, "tp"), P(None, "tp"), P(None, "tp"), P("tp", None), P(), P(),
            P("req", None), P("req", None, "tp"), P("req", None, "tp"), P("req", "tp", None), P(),
        ),
        out_specs=(P("req", None), P(None, "req", None, "tp")),
        check_vma=False,
    )
```

```python
import functools
import jax
import jax.numpy as jnp
from jax import lax
from jax.experimental import pallas as pl
from jax.experimental.pallas import tpu as pltpu
from jax.sharding import PartitionSpec as P

HD = 64
EPS = 1e-06
F32 = jnp.float32
BF16 = jnp.bfloat16
NT = (((1,), (1,)), ((), ()))
LANES = 128
TILE = 128
TOP = 2
MIG = 4
EXTRA = 16
VMEM_BYTES = 64 * 1024 * 1024


def iota(shape, dim):
    return lax.broadcasted_iota(jnp.int32, shape, dim)


def onehot(hit):
    return hit.astype(F32).astype(BF16)


def attention_kernel(
    group_hbm, plen_hbm, tlen_hbm, group_row_hbm, bucket_hbm, bias_hbm,
    q_hbm, knew_hbm, vnew_hbm, prompt_hbm, tail_hbm,
    head_ref, tail_out,
    group_sm, plen_sm, tlen_sm, perm_sm, group_row, bucket_row, bias_rows, perm_v,
    pk_v, pv_v, kbuf, vbuf,
    q_v, knew_v, vnew_v, table, s_p, s_t, w_p, o_v, sorted_v, qbd_v,
    small_sem, w_sem, p_sem, in_sem, out_sem, perm_sem,
):
    rows = q_v.shape[0]
    groups, prompt_rows, cols = pv_v.shape
    tail_rows = kbuf.shape[1]
    heads = cols // HD
    per8 = 8 // heads
    per16 = 16 // heads
    width_t = per8 * tail_rows
    span_end = prompt_rows + tail_rows
    tile_rows = TILE * heads
    tiles = rows // TILE

    small = [
        pltpu.make_async_copy(src, dst, small_sem.at[i])
        for i, (src, dst) in enumerate(
            (
                (group_hbm, group_sm), (plen_hbm, plen_sm), (tlen_hbm, tlen_sm),
                (group_row_hbm, group_row), (bucket_hbm, bucket_row.at[0]),
                (bias_hbm, bias_rows),
            )
        )
    ]
    weights = [
        pltpu.make_async_copy(src, dst, w_sem.at[i])
        for i, (src, dst) in enumerate(
            ((q_hbm, q_v), (knew_hbm, knew_v), (vnew_hbm, vnew_v))
        )
    ]
    prompts = [
        pltpu.make_async_copy(prompt_hbm.at[0], pk_v, p_sem.at[0]),
        pltpu.make_async_copy(prompt_hbm.at[1], pv_v, p_sem.at[1]),
    ]

    def tile_in(t):
        at = pl.ds(t * TILE, TILE)
        return [
            pltpu.make_async_copy(tail_hbm.at[0, at], kbuf.at[at], in_sem.at[0, t]),
            pltpu.make_async_copy(tail_hbm.at[1, at], vbuf.at[at], in_sem.at[1, t]),
        ]

    def tile_out(t):
        at = pl.ds(t * TILE, TILE)
        return [
            pltpu.make_async_copy(kbuf.at[at], tail_out.at[0, at], out_sem.at[0, t]),
            pltpu.make_async_copy(vbuf.at[at], tail_out.at[1, at], out_sem.at[1, t]),
        ]

    for copy in small + weights + prompts[:1]:
        copy.start()
    for copy in small:
        copy.wait()

    for t in range(tiles):
        for copy in tile_in(t):
            copy.start()
    prompts[1].start()

    eye = onehot(iota((rows, rows), 0) == iota((rows, rows), 1))
    g_row = group_row[...]
    g_col = lax.dot_general(
        eye, jnp.broadcast_to(g_row.astype(F32), (8, rows)).astype(BF16), NT,
        preferred_element_type=F32,
    )[:, 0:1].astype(jnp.int32)
    key_row = g_row * rows + iota((1, rows), 1)
    key_col = g_col * rows + iota((rows, 1), 0)
    rank_row = jnp.sum((key_col < key_row).astype(jnp.int32), axis=0, keepdims=True)
    rank_col = jnp.sum((key_row < key_col).astype(jnp.int32), axis=1, keepdims=True)
    perm_row = jnp.sum(
        jnp.where(rank_col == iota((rows, rows), 1), iota((rows, rows), 0), 0), axis=0, keepdims=True
    )
    perm_v[...] = jnp.broadcast_to(perm_row, perm_v.shape)
    perm_copy = pltpu.make_async_copy(perm_v, perm_sm, perm_sem)
    perm_copy.start()

    span = bucket_row.shape[1]
    buckets = bias_rows.shape[1]
    below = (bucket_row[...] < iota((buckets, span), 0)).astype(jnp.int32)
    starts = jnp.sum(below, axis=1, keepdims=True)
    bias = jnp.concatenate([bias_rows[...]] * per8, axis=0)
    distance = span_end - iota(table.shape, 1)
    found = jnp.broadcast_to(bias[:, 0:1], table.shape)
    for k in range(1, buckets):
        found = jnp.where(distance >= starts[k : k + 1, 0:1], bias[:, k : k + 1], found)
    table[...] = found

    for copy in weights:
        copy.wait()
    perm_copy.wait()

    lane = iota((8, LANES), 1)
    sub = iota((8, LANES), 0)
    row16 = iota((16, cols), 0)
    minus = jnp.float32(-jnp.inf)
    pieces = prompt_rows // LANES

    def build_bias(tile):
        def step(i, carry):
            base = tile * TILE + i * per8
            out_p = [jnp.full((8, LANES), minus) for _ in range(pieces)]
            out_t = [jnp.full((8, LANES), minus) for _ in range(width_t // LANES)]
            for j in range(per8):
                r = perm_sm[0, base + j]
                length = tlen_sm[r]
                plen = plen_sm[group_sm[r]]
                start = span_end - plen - length
                block = lax.shift_right_logical(start, 7)
                off = start & (LANES - 1)
                mine = (sub >= j * heads) & (sub < (j + 1) * heads)
                window = table[:, pl.ds(pl.multiple_of(block * LANES, LANES), prompt_rows + LANES)]
                turn = (LANES - off) & (LANES - 1)
                turned = [
                    pltpu.roll(window[:, k * LANES : (k + 1) * LANES], turn, 1)
                    for k in range(pieces + 1)
                ]
                for k in range(pieces):
                    here = jnp.where(lane < LANES - off, turned[k], turned[k + 1])
                    out_p[k] = jnp.where(mine & (lane < plen - k * LANES), here, out_p[k])
                place = j * tail_rows
                k = place // LANES
                place = place - k * LANES
                own = table[:, prompt_rows : prompt_rows + LANES]
                shift = (place - tail_rows + length) & (LANES - 1)
                own = pltpu.roll(own, shift, 1)
                live = mine & (lane >= place) & (lane <= place + length)
                out_t[k] = jnp.where(live, own, out_t[k])
            at = pl.ds(pl.multiple_of(tile * tile_rows + i * 8, 8), 8)
            for k in range(pieces):
                s_p[at, k * LANES : (k + 1) * LANES] = out_p[k]
            for k in range(width_t // LANES):
                s_t[at, k * LANES : (k + 1) * LANES] = out_t[k]
            return carry

        lax.fori_loop(0, TILE // per8, step, 0, unroll=16)

    def insert(t):
        def step(i, carry):
            r = t * TILE + i
            length = tlen_sm[r]
            first = pl.multiple_of(length & 0x30, 16)
            hit = row16 == (length & 15)
            for new, buf in ((knew_v, kbuf), (vnew_v, vbuf)):
                fresh = jnp.broadcast_to(new[pl.ds(r, 1), :], (16, cols)).astype(BF16)
                old = buf[r, pl.ds(first, 16), :]
                buf[r, pl.ds(first, 16), :] = jnp.where(hit, fresh, old)
            return carry

        lax.fori_loop(0, TILE, step, 0, unroll=8)

    own_head = iota((tile_rows, cols), 0) % heads == iota((tile_rows, cols), 1) // HD
    spread_row = iota((tile_rows, rows), 0) // heads
    first_head = iota((TILE, LANES), 1) < HD

    def spread_of(tile):
        return onehot(rank_row == spread_row + tile * TILE)

    def member_of(tile):
        group8 = jnp.broadcast_to(g_row.astype(F32), (8, rows)).astype(BF16)
        return lax.dot_general(
            spread_of(tile), group8, NT, preferred_element_type=F32
        )[:, 0:1].astype(jnp.int32)

    def group_range(tile):
        low = group_sm[perm_sm[0, tile * TILE]]
        high = group_sm[perm_sm[0, tile * TILE + TILE - 1]]
        return low, high + 1

    def scores(tile, carry):
        build_bias(tile)
        at = pl.ds(pl.multiple_of(tile * tile_rows, tile_rows), tile_rows)
        qrep = jnp.dot(spread_of(tile), q_v[...], preferred_element_type=F32)
        qbd = jnp.where(own_head, qrep, 0.0)
        qbd_v[at, :] = qbd.astype(BF16)
        member = member_of(tile)

        @pl.when(tile == 0)
        def _():
            prompts[0].wait()

        def one_group(g, carry):
            part = jnp.where(member == g, qbd, 0.0).astype(BF16)
            s_p[at, :] += lax.dot_general(part, pk_v[g], NT, preferred_element_type=F32)
            return carry

        low, high = group_range(tile)
        lax.fori_loop(low, high, one_group, 0)
        for copy in tile_in(tile):
            copy.wait()

        @pl.when(tile > 0)
        def _():
            for copy in tile_out(tile - 1):
                copy.start()

        insert(tile)
        return carry

    lax.fori_loop(0, tiles, scores, 0)
    for copy in tile_out(tiles - 1):
        copy.start()
    prompts[1].wait()

    def gathered(buf, first):
        return jnp.concatenate([buf[perm_sm[0, first + j]] for j in range(per16)], axis=0)

    def values(tile, carry):
        base = pl.multiple_of(tile * tile_rows, tile_rows)
        at = pl.ds(base, tile_rows)
        for i in range(TILE // per16):
            keys = gathered(kbuf, tile * TILE + i * per16)
            here = pl.ds(pl.multiple_of(base + i * 16, 16), 16)
            got = lax.dot_general(qbd_v[here, :], keys, NT, preferred_element_type=F32)
            upper = pl.ds(pl.multiple_of(base + i * 16, 8), 8)
            lower = pl.ds(pl.multiple_of(base + i * 16 + 8, 8), 8)
            s_t[upper, :] += got[:8, :width_t]
            s_t[lower, :] += got[8:, width_t:]
        prompt_s = s_p[at, :]
        tail_s = s_t[at, :]
        top = jnp.maximum(
            jnp.max(prompt_s, axis=1, keepdims=True), jnp.max(tail_s, axis=1, keepdims=True)
        )
        pe = jnp.exp(prompt_s - top)
        te = jnp.exp(tail_s - top)
        total = jnp.sum(pe, axis=1, keepdims=True) + jnp.sum(te, axis=1, keepdims=True)
        part = 1.0 / total
        w_p[...] = (pe * part).astype(BF16)
        tw = te * part
        none = jnp.zeros((8, width_t), F32)
        for i in range(TILE // per16):
            row = i * 16
            upper = jnp.concatenate([tw[row : row + 8], none], axis=1)
            lower = jnp.concatenate([none, tw[row + 8 : row + 16]], axis=1)
            both = jnp.concatenate([upper, lower], axis=0).astype(BF16)
            vals = gathered(vbuf, tile * TILE + i * per16)
            o_t = jnp.dot(both, vals, preferred_element_type=F32)
            for b in range(cols // LANES):
                o_v[b, row : row + 16, :] = o_t[:, b * LANES : (b + 1) * LANES]
        member = member_of(tile)

        def one_group(g, carry):
            w = jnp.where(member == g, w_p[...].astype(F32), 0.0).astype(BF16)
            o_p = jnp.dot(w, pv_v[g], preferred_element_type=F32)
            for b in range(cols // LANES):
                o_v[b, 0:tile_rows, :] += o_p[:, b * LANES : (b + 1) * LANES]
            return carry

        low, high = group_range(tile)
        lax.fori_loop(low, high, one_group, 0)
        to = pl.ds(pl.multiple_of(tile * TILE, TILE), TILE)
        for b in range(cols // LANES):
            even = o_v[b, pl.ds(2 * b, TILE, stride=heads), :]
            odd = o_v[b, pl.ds(2 * b + 1, TILE, stride=heads), :]
            sorted_v[to, b * LANES : (b + 1) * LANES] = jnp.where(first_head, even, odd).astype(BF16)
        return carry

    lax.fori_loop(0, tiles, values, 0)
    unsort = onehot(rank_col == iota((rows, rows), 1))
    head_ref[...] = jnp.dot(unsort, sorted_v[...], preferred_element_type=F32).astype(BF16)
    for t in range(tiles):
        for copy in tile_out(t):
            copy.wait()


def project_kernel(
    slots_hbm, tlen_hbm, hidden_hbm, gain_hbm, wq_hbm, wk_hbm, wv_hbm, tail_hbm,
    q_ref, knew_ref, vnew_ref, packet_ref,
    slots_sm, tlen_sm, mover_sm, hidden_v, gain_v, wq_v, wk_v, wv_v, sem, slab_sem,
):
    rows = hidden_v.shape[0]
    cols = wq_v.shape[1]
    early = [
        pltpu.make_async_copy(slots_hbm, slots_sm, sem.at[0]),
        pltpu.make_async_copy(tlen_hbm, tlen_sm, sem.at[1]),
    ]
    late = [
        pltpu.make_async_copy(src, dst, sem.at[2 + i])
        for i, (src, dst) in enumerate(
            (
                (hidden_hbm, hidden_v), (gain_hbm, gain_v),
                (wq_hbm, wq_v), (wk_hbm, wk_v), (wv_hbm, wv_v),
            )
        )
    ]
    for copy in early + late:
        copy.start()
    for copy in early:
        copy.wait()
    base = lax.axis_index("req") * rows
    for m in range(MIG + 1):
        mover_sm[m] = 0

    def look(i, count):
        mover_sm[count] = i
        return count + (slots_sm[base + i] != base + i).astype(jnp.int32)

    lax.fori_loop(0, rows, look, 0, unroll=16)
    slabs = [
        pltpu.make_async_copy(
            tail_hbm.at[side, mover_sm[m]], packet_ref.at[2 * m + side], slab_sem.at[2 * m + side]
        )
        for m in range(MIG)
        for side in range(2)
    ]
    for copy in slabs:
        copy.start()
    for copy in late:
        copy.wait()
    v = hidden_v[...].astype(F32)
    normed = (
        v * lax.rsqrt(jnp.mean(v * v, axis=-1, keepdims=True) + EPS) * gain_v[...]
    ).astype(BF16)
    query = jnp.dot(normed, wq_v[...], preferred_element_type=F32).astype(BF16)
    q_ref[...] = query * jnp.asarray(HD ** (-0.5), BF16)
    for new, w in ((knew_ref, wk_v), (vnew_ref, wv_v)):
        new[...] = jnp.dot(normed, w[...], preferred_element_type=F32).astype(BF16).astype(F32)
    for copy in slabs:
        copy.wait()
    at = iota((packet_ref.shape[1], cols), 0)
    for m in range(MIG):
        r = mover_sm[m]
        for side, new in enumerate((knew_ref, vnew_ref)):
            old = packet_ref[2 * m + side].astype(F32)
            packet_ref[2 * m + side] = jnp.where(
                at == tlen_sm[r], new[pl.ds(r, 1), :], old
            ).astype(BF16)


def project(new_slot, tail_len, hidden_in, gain, w_query, w_key, w_value, tail_kv):
    rows, width = hidden_in.shape
    cols = w_query.shape[1]
    tail_rows = tail_kv.shape[2]
    vm = pl.BlockSpec(memory_space=pltpu.VMEM)
    hbm = pl.BlockSpec(memory_space=pl.ANY)
    return pl.pallas_call(
        project_kernel,
        out_shape=(
            jax.ShapeDtypeStruct((rows, cols), BF16),
            jax.ShapeDtypeStruct((rows, cols), F32),
            jax.ShapeDtypeStruct((rows, cols), F32),
            jax.ShapeDtypeStruct((2 * MIG, tail_rows, cols), BF16),
        ),
        in_specs=[hbm] * 8,
        out_specs=(vm,) * 4,
        scratch_shapes=[
            pltpu.SMEM(new_slot.shape, jnp.int32),
            pltpu.SMEM(tail_len.shape, jnp.int32),
            pltpu.SMEM((MIG + 1,), jnp.int32),
            pltpu.VMEM((rows, width), BF16),
            pltpu.VMEM((1, width), F32),
            pltpu.VMEM((width, cols), BF16),
            pltpu.VMEM((width, cols), BF16),
            pltpu.VMEM((width, cols), BF16),
            pltpu.SemaphoreType.DMA((7,)),
            pltpu.SemaphoreType.DMA((2 * MIG,)),
        ],
        compiler_params=pltpu.CompilerParams(vmem_limit_bytes=VMEM_BYTES),
        cost_estimate=pl.CostEstimate(flops=400_000_000, bytes_accessed=3_000_000, transcendentals=0),
        name="project",
    )(new_slot, tail_len, hidden_in, gain[None, :], w_query, w_key, w_value, tail_kv)


def attention(
    query, key_new, value_new, prompt_kv, tail_kv, group_of, prompt_len, tail_len, bucket_of,
    bias_table,
):
    rows, cols = query.shape
    heads = cols // HD
    groups, prompt_rows = prompt_kv.shape[1:3]
    tail_rows = tail_kv.shape[2]
    span = bucket_of.shape[0]
    buckets = bias_table.shape[0]
    table_width = 2 * prompt_rows + LANES
    width_t = 8 // heads * tail_rows
    tiles = rows // TILE
    vm = pl.BlockSpec(memory_space=pltpu.VMEM)
    hbm = pl.BlockSpec(memory_space=pl.ANY)
    return pl.pallas_call(
        attention_kernel,
        out_shape=(
            jax.ShapeDtypeStruct((rows, cols), BF16),
            jax.ShapeDtypeStruct(tail_kv.shape, BF16),
        ),
        in_specs=[hbm] * 11,
        out_specs=(vm, hbm),
        scratch_shapes=[
            pltpu.SMEM((rows,), jnp.int32),
            pltpu.SMEM((groups,), jnp.int32),
            pltpu.SMEM((rows,), jnp.int32),
            pltpu.SMEM((8, rows), jnp.int32),
            pltpu.VMEM((1, rows), jnp.int32),
            pltpu.VMEM((1, span), jnp.int32),
            pltpu.VMEM((heads, buckets), F32),
            pltpu.VMEM((8, rows), jnp.int32),
            pltpu.VMEM((groups, prompt_rows, cols), BF16),
            pltpu.VMEM((groups, prompt_rows, cols), BF16),
            pltpu.VMEM((rows, tail_rows, cols), BF16),
            pltpu.VMEM((rows, tail_rows, cols), BF16),
            pltpu.VMEM((rows, cols), BF16),
            pltpu.VMEM((rows, cols), F32),
            pltpu.VMEM((rows, cols), F32),
            pltpu.VMEM((8, table_width), F32),
            pltpu.VMEM((rows * heads, prompt_rows), F32),
            pltpu.VMEM((rows * heads, width_t), F32),
            pltpu.VMEM((TILE * heads, prompt_rows), BF16),
            pltpu.VMEM((cols // LANES, TILE * heads + 8, LANES), F32),
            pltpu.VMEM((rows, cols), BF16),
            pltpu.VMEM((rows * heads, cols), BF16),
            pltpu.SemaphoreType.DMA((6,)),
            pltpu.SemaphoreType.DMA((3,)),
            pltpu.SemaphoreType.DMA((2,)),
            pltpu.SemaphoreType.DMA((2, tiles)),
            pltpu.SemaphoreType.DMA((2, tiles)),
            pltpu.SemaphoreType.DMA,
        ],
        compiler_params=pltpu.CompilerParams(vmem_limit_bytes=VMEM_BYTES),
        cost_estimate=pl.CostEstimate(flops=8_000_000_000, bytes_accessed=45_000_000, transcendentals=700_000),
        name="attention",
    )(
        group_of, prompt_len, tail_len, group_of[None, :], bucket_of, bias_table.T,
        query, key_new, value_new, prompt_kv, tail_kv,
    )


def block_rows(cap):
    return cap + EXTRA


def low_part(replicas):
    bits = (replicas.bit_length() - 1) // 2
    return bits, 1 << bits


def plan_kernel(cap, slots_ref, ids_ref, *refs):
    place_ref, extra_ref, wide_ref, kron_ref, plan_ref, slot_s = refs[-6:]
    replicas, rows = slots_ref.shape
    experts = slot_s.shape[0]
    size = place_ref.shape[0] // replicas
    me = lax.axis_index("req")
    ns = slots_ref[...]
    at_sub = iota((replicas, rows), 0)
    at_lane = iota((replicas, rows), 1)
    moved = ns != at_sub * rows + at_lane
    tri = (iota((rows, rows), 0) < iota((rows, rows), 1)).astype(BF16)
    rank = jnp.dot(moved.astype(F32).astype(BF16), tri, preferred_element_type=F32).astype(jnp.int32)
    going_to = ns // rows
    mine = at_sub == me

    def own(values):
        return jnp.sum(jnp.where(mine, values, 0), axis=0, keepdims=True)

    moved_me = own(moved.astype(jnp.int32))
    rank_me = own(rank)
    to_me = own(going_to)
    ids_rows = ids_ref[...]
    at_e = iota((experts, rows), 0)
    hit = (ids_rows[0:1] == at_e) | (ids_rows[1:2] == at_e)
    normal = (hit & (moved_me == 0)).astype(F32).astype(BF16)
    slot = jnp.dot(normal, tri, preferred_element_type=F32).astype(jnp.int32)
    slot_s[...] = jnp.where(hit, jnp.where(moved_me > 0, cap + rank_me, slot), -1)
    at_row = iota((size, rows), 0)
    at_extra = iota((EXTRA, rows), 0)
    for k in range(replicas):
        e = me ^ k
        block = pl.ds(k * size, size)
        row = slot_s[pl.ds(e, 1), :]
        leaving = jnp.where((moved_me > 0) & (to_me == e), rank_me, -100)
        place_ref[block, :] = onehot(at_row == row)
        more = pl.ds(k * EXTRA, EXTRA)
        extra_ref[more, 0:rows] = onehot(at_extra == leaving + MIG)
        extra_ref[more, rows:] = onehot(at_extra == leaving + 2 * MIG)
    lane = iota(wide_ref.shape, 1)
    eye = onehot(iota((rows, rows), 0) == iota((rows, rows), 1))
    facts = jnp.concatenate([ids_rows, jnp.zeros((6, rows), jnp.int32)], axis=0)
    columns = lax.dot_general(
        eye, facts.astype(F32).astype(BF16), NT, preferred_element_type=F32
    )
    wide = jnp.where(lane == 0, columns[:, 0:1], jnp.where(lane == 1, columns[:, 1:2], 0.0))
    wide_ref[...] = wide.astype(BF16)
    dest = jnp.max(jnp.where(moved, going_to, -1), axis=1, keepdims=True)
    dest = jnp.where(dest < 0, iota((replicas, 1), 0), dest)
    hot = (dest == iota((replicas, replicas), 1)).astype(F32).astype(BF16)
    span = replicas * EXTRA
    mixed_row = (iota((span, replicas), 0) // EXTRA) ^ me
    a = (mixed_row == iota((span, replicas), 1)).astype(F32).astype(BF16)
    by_source = lax.dot_general(a, hot, NT, preferred_element_type=F32).astype(BF16)
    pairs = lax.dot_general(by_source, a, NT, preferred_element_type=F32)
    same = iota((span, span), 0) % EXTRA == iota((span, span), 1) % EXTRA
    kron_ref[...] = jnp.where(same, pairs, 0.0).astype(BF16)
    sub1 = iota((replicas, 1), 0)

    def source_of(who):
        return jnp.sum(jnp.where(dest == who, sub1, 0), axis=0, keepdims=True)

    low_bits, low = low_part(replicas)
    diff = source_of(me) ^ me
    turn = diff & (low - 1)
    final = jnp.where(turn == 0, diff >> low_bits, (replicas >> low_bits) + turn - 1)
    lane8 = iota((8, LANES), 1)
    plan = jnp.where(lane8 == 0, final, -1)
    for j in range(1, low):
        apart = source_of(me ^ j) ^ me
        plan = jnp.where(lane8 == 24 + j, apart >> low_bits, plan)
    lane1 = iota((1, rows), 1)
    for m in range(MIG):
        is_m = (moved_me > 0) & (rank_me == m)
        mover = jnp.sum(jnp.where(is_m, lane1, 0), axis=1, keepdims=True)
        plan = jnp.where(lane8 == 8 + m, mover, plan)
        come = moved & (going_to == me) & (rank == m)
        to = jnp.sum(jnp.where(come, ns - me * rows + 1, 0), axis=1, keepdims=True)
        to = jnp.sum(to, axis=0, keepdims=True) - 1
        plan = jnp.where(lane8 == 16 + m, to, plan)
    plan_ref[...] = plan


def make_plan(slots, expert_ids, experts, cap, after):
    replicas, rows = slots.shape
    size = block_rows(cap)
    vm = pl.BlockSpec(memory_space=pltpu.VMEM)
    span = replicas * EXTRA
    return pl.pallas_call(
        functools.partial(plan_kernel, cap),
        out_shape=(
            jax.ShapeDtypeStruct((replicas * size, rows), BF16),
            jax.ShapeDtypeStruct((replicas * EXTRA, 2 * rows), BF16),
            jax.ShapeDtypeStruct((rows, LANES), BF16),
            jax.ShapeDtypeStruct((span, span), BF16),
            jax.ShapeDtypeStruct((8, LANES), jnp.int32),
        ),
        in_specs=[vm, vm] + [pl.BlockSpec(memory_space=pl.ANY)] * len(after),
        out_specs=(vm,) * 5,
        scratch_shapes=[pltpu.VMEM((experts, rows), jnp.int32)],
        compiler_params=pltpu.CompilerParams(vmem_limit_bytes=VMEM_BYTES),
        cost_estimate=pl.CostEstimate(flops=0, bytes_accessed=0, transcendentals=0),
        name="plan",
    )(slots, expert_ids.T, *after)


def load(sem, *pairs):
    made = [pltpu.make_async_copy(src, dst, sem.at[i]) for i, (src, dst) in enumerate(pairs)]
    for copy in made:
        copy.start()
    for copy in made:
        copy.wait()


def norm(values, gain):
    v = values.astype(F32)
    return (v * lax.rsqrt(jnp.mean(v * v, axis=-1, keepdims=True) + EPS) * gain).astype(BF16)


def far_part(replicas, pieces):
    return replicas // 2, replicas // pieces


def dispatch_kernel(pieces, replicas, *refs):
    near, each = far_part(replicas, pieces)
    count = near + each
    heads_hbm = refs[:pieces]
    wout_hbm = refs[pieces : 2 * pieces]
    hidden_hbm, gain_ref, place_hbm, extra_hbm, wide_hbm = refs[2 * pieces : 2 * pieces + 5]
    refs = refs[-11 - count :]
    resid_ref = refs[0]
    outs = refs[1 : 1 + count]
    head_v, wout_v, stack, hidden_ref, place_ref, extra_ref, wide_ref, extra_v, sem, more = refs[1 + count :]
    tp = lax.axis_index("tp")
    core = tp & 1
    rows, width = hidden_ref.shape
    cols = width // pieces
    half = width // 2

    def place_of(at):
        return pl.ds(pl.multiple_of(at * cols, cols), cols)

    made = [pltpu.make_async_copy(hidden_hbm, hidden_ref, more.at[0])]
    for k in range(pieces):
        at = tp ^ k
        made.append(
            pltpu.make_async_copy(heads_hbm[k], head_v.at[:, place_of(at)], sem.at[1, at])
        )
    for k in range(pieces):
        at = tp ^ k
        made.append(pltpu.make_async_copy(wout_hbm[k], wout_v.at[place_of(at)], sem.at[0, at]))
    late = [
        pltpu.make_async_copy(place_hbm, place_ref, more.at[1]),
        pltpu.make_async_copy(extra_hbm, extra_ref, more.at[2]),
        pltpu.make_async_copy(wide_hbm, wide_ref, more.at[3]),
    ]

    for copy in made + late:
        copy.start()
    made[0].wait()
    attn = jnp.zeros((rows, width), F32)
    for at in range(pieces):
        here = slice(at * cols, (at + 1) * cols)
        pltpu.make_async_copy(heads_hbm[0], head_v.at[:, here], sem.at[1, at]).wait()
        pltpu.make_async_copy(wout_hbm[0], wout_v.at[here], sem.at[0, at]).wait()
        attn = attn + jnp.dot(head_v[:, here], wout_v[here, :], preferred_element_type=F32)
    resid = (hidden_ref[...].astype(F32) + attn).astype(BF16)
    resid_ref[...] = resid
    normed = norm(resid, gain_ref[...])
    first = core == 0
    stack[0:rows, :] = jnp.where(first, normed[:, :half], normed[:, half:])
    stack[rows : 2 * rows, :] = jnp.where(first, resid[:, :half], resid[:, half:])
    for copy in late:
        copy.wait()
    size = place_ref.shape[0] // replicas
    extra_v[...] = jnp.dot(extra_ref[:, 0:rows], stack[rows:, :], preferred_element_type=F32)
    extra_v[:, 0:LANES] += jnp.dot(extra_ref[:, rows:], wide_ref[...], preferred_element_type=F32)
    for i in range(count):
        k = i if i < near else near + (tp >> 1) * each + (i - near)
        block = jnp.dot(
            place_ref[pl.ds(k * size, size), :], stack[0:rows, :], preferred_element_type=F32
        )
        outs[i][0 : size - EXTRA, :] = block[: size - EXTRA].astype(BF16)
        outs[i][size - EXTRA :, :] = (
            block[size - EXTRA :] + extra_v[pl.ds(k * EXTRA, EXTRA), :]
        ).astype(BF16)


def dispatch(heads, wouts, hidden, gain, place, extra, wide, after, replicas):
    rows, width = hidden.shape
    pieces = len(heads)
    count = sum(far_part(replicas, pieces))
    half = width // 2
    size = place.shape[0] // replicas
    vm = pl.BlockSpec(memory_space=pltpu.VMEM)
    hbm = pl.BlockSpec(memory_space=pl.ANY)
    return pl.pallas_call(
        functools.partial(dispatch_kernel, pieces, replicas),
        out_shape=(jax.ShapeDtypeStruct((rows, width), BF16),)
        + tuple(jax.ShapeDtypeStruct((size, half), BF16) for _ in range(count)),
        in_specs=[hbm] * (2 * pieces) + [hbm, vm, hbm, hbm, hbm] + [hbm] * len(after),
        out_specs=(vm,) * (1 + count),
        scratch_shapes=[
            pltpu.VMEM((rows, width), BF16),
            pltpu.VMEM((width, width), BF16),
            pltpu.VMEM((2 * rows, half), BF16),
            pltpu.VMEM((rows, width), BF16),
            pltpu.VMEM(place.shape, BF16),
            pltpu.VMEM(extra.shape, BF16),
            pltpu.VMEM(wide.shape, BF16),
            pltpu.VMEM((extra.shape[0], half), F32),
            pltpu.SemaphoreType.DMA((2, pieces)),
            pltpu.SemaphoreType.DMA((5,)),
        ],
        compiler_params=pltpu.CompilerParams(vmem_limit_bytes=VMEM_BYTES),
        cost_estimate=pl.CostEstimate(flops=1_200_000_000, bytes_accessed=6_000_000, transcendentals=0),
        name="dispatch",
    )(*heads, *wouts, hidden, gain[None, :], place, extra, wide, *after)


def pieces_of(total, step):
    return [(at, min(step, total - at)) for at in range(0, total, step)]


def expert_kernel(replicas, pieces, *refs):
    own = refs[:replicas]
    pair = refs[replicas : 2 * replicas]
    wg_hbm, wu_hbm, wd_hbm = refs[2 * replicas : 2 * replicas + 3]
    keep_hbm, give_hbm, keep_ref, give_ref, x_own, x_pair, wg, wu, wd, act, sem, xsem, osem = refs[-13:]
    tp = lax.axis_index("tp")
    core = tp & 1
    size, half = own[0].shape
    near, each = far_part(replicas, pieces)
    hidden = wg.shape[0]
    chunks = pieces_of(hidden, 256)
    blocks = []
    for k in range(replicas):
        there = k
        if k >= near:
            turn, f = divmod(k - near, each)
            there = near + ((tp >> 1) ^ turn) * each + f
        at = pl.ds(there * size, size)
        blocks.append(pltpu.make_async_copy(own[k], x_own.at[at], xsem.at[0, k]))
        blocks.append(pltpu.make_async_copy(pair[k], x_pair.at[at], xsem.at[1, k]))
    wide = [
        [
            pltpu.make_async_copy(src.at[0, pl.ds(at, n)], dst.at[pl.ds(at, n)], sem.at[side, c])
            for side, (src, dst) in enumerate(((wg_hbm, wg), (wu_hbm, wu)))
        ]
        for c, (at, n) in enumerate(chunks)
    ]
    down = pltpu.make_async_copy(wd_hbm.at[0], wd, sem.at[2, 0])
    for copy in wide[0] + blocks + sum(wide[1:], []) + [down]:
        copy.start()
    for copy in blocks:
        copy.wait()
    here = pl.ds(pl.multiple_of(core * half, half), half)
    there = pl.ds(pl.multiple_of((1 - core) * half, half), half)
    a, b = x_own[...], x_pair[...]

    def product(w, rows):
        return lax.dot_general(a, w[rows, here], NT, preferred_element_type=F32) + lax.dot_general(
            b, w[rows, there], NT, preferred_element_type=F32
        )

    for c, (at, n) in enumerate(chunks):
        for copy in wide[c]:
            copy.wait()
        rows = pl.ds(at, n)
        gate = product(wg, rows)
        act[:, at : at + n] = (jax.nn.gelu(gate, approximate=True) * product(wu, rows)).astype(BF16)
    down.wait()
    leave = [
        pltpu.make_async_copy(give_ref, give_hbm, osem.at[0]),
        pltpu.make_async_copy(keep_ref, keep_hbm, osem.at[1]),
    ]
    give_ref[...] = jnp.dot(act[...], wd[:, there], preferred_element_type=F32).astype(BF16)
    leave[0].start()
    keep_ref[...] = jnp.dot(act[...], wd[:, here], preferred_element_type=F32).astype(BF16)
    leave[1].start()
    for copy in leave:
        copy.wait()


def expert(own, pair, w_gate, w_up, w_down, pieces):
    replicas = len(own)
    size, half = own[0].shape
    _, width, hidden = w_gate.shape
    total = replicas * size
    hbm = pl.BlockSpec(memory_space=pl.ANY)
    shape = jax.ShapeDtypeStruct((total, half), BF16)
    return pl.pallas_call(
        functools.partial(expert_kernel, replicas, pieces),
        out_shape=(shape, shape),
        in_specs=[hbm] * (2 * replicas + 3),
        out_specs=(hbm, hbm),
        scratch_shapes=[
            pltpu.VMEM((total, half), BF16),
            pltpu.VMEM((total, half), BF16),
            pltpu.VMEM((total, half), BF16),
            pltpu.VMEM((total, half), BF16),
            pltpu.VMEM((hidden, width), BF16),
            pltpu.VMEM((hidden, width), BF16),
            pltpu.VMEM((hidden, width), BF16),
            pltpu.VMEM((total, hidden), BF16),
            pltpu.SemaphoreType.DMA((3, len(pieces_of(hidden, 256)))),
            pltpu.SemaphoreType.DMA((2, replicas)),
            pltpu.SemaphoreType.DMA((2,)),
        ],
        compiler_params=pltpu.CompilerParams(vmem_limit_bytes=VMEM_BYTES),
        cost_estimate=pl.CostEstimate(flops=3_400_000_000, bytes_accessed=8_000_000, transcendentals=600_000),
        name="expert",
    )(*own, *pair, jnp.swapaxes(w_gate, 1, 2), jnp.swapaxes(w_up, 1, 2), w_down)


def give_back_kernel(cap, keep_hbm, got_hbm, kron_hbm, *refs):
    replicas = len(refs) - 5
    outs = refs[:replicas]
    rows_v, keep_ref, got_ref, kron_ref, sem = refs[replicas:]
    load(sem, (keep_hbm, keep_ref), (got_hbm, got_ref), (kron_hbm, kron_ref))
    size = outs[0].shape[0]
    for k in range(replicas):
        at = slice(k * size, (k + 1) * size)
        both = keep_ref[at, :].astype(F32) + got_ref[at, :].astype(F32)
        outs[k][...] = both.astype(BF16)
        rows_v[k * EXTRA : (k + 1) * EXTRA, :] = both[size - EXTRA :].astype(BF16)
    moved = jnp.dot(kron_ref[...], rows_v[...], preferred_element_type=F32)
    first = iota((EXTRA, 1), 0) >= cap - (size - EXTRA)
    for k in range(replicas):
        at = slice(k * EXTRA, (k + 1) * EXTRA)
        outs[k][size - EXTRA :, :] = jnp.where(
            first, moved[at], rows_v[at, :].astype(F32)
        ).astype(BF16)


def give_back(keep, got, kron, cap, replicas):
    total, half = keep.shape
    size = total // replicas
    vm = pl.BlockSpec(memory_space=pltpu.VMEM)
    hbm = pl.BlockSpec(memory_space=pl.ANY)
    return pl.pallas_call(
        functools.partial(give_back_kernel, cap),
        out_shape=tuple(jax.ShapeDtypeStruct((size, half), BF16) for _ in range(replicas)),
        in_specs=[hbm] * 3,
        out_specs=(vm,) * replicas,
        scratch_shapes=[
            pltpu.VMEM((replicas * EXTRA, half), BF16),
            pltpu.VMEM((total, half), BF16),
            pltpu.VMEM((total, half), BF16),
            pltpu.VMEM(kron.shape, BF16),
            pltpu.SemaphoreType.DMA((3,)),
        ],
        compiler_params=pltpu.CompilerParams(vmem_limit_bytes=VMEM_BYTES),
        cost_estimate=pl.CostEstimate(flops=30_000_000, bytes_accessed=2_500_000, transcendentals=0),
        name="give_back",
    )(keep, got, kron)


def gates_kernel(cap, replicas, *refs):
    own = refs[:replicas]
    pair = refs[replicas : 2 * replicas]
    (after_hbm, resid_hbm, slots_ref, ids_ref, gain_ref, router_ref) = refs[
        2 * replicas : 2 * replicas + 6
    ]
    (first_ref, second_ref, gate_ref, new_ref, resid_ref, own_v, pair_v, sem) = refs[2 * replicas + 6 :]
    me = lax.axis_index("req")
    core = lax.axis_index("tp") & 1
    rows, width = resid_ref.shape
    half = width // 2
    size = own[0].shape[0]
    low = pl.ds(size - EXTRA, EXTRA)
    skip = 0
    load(
        sem,
        (resid_hbm, resid_ref),
        *[(own[k].at[low], own_v.at[k]) for k in range(replicas)],
        *[(pair[k].at[low], pair_v.at[k]) for k in range(replicas)],
    )
    ns = slots_ref[...]
    count = ns.shape[0]
    at_sub = iota((count, rows), 0)
    moved = ns != at_sub * rows + iota((count, rows), 1)
    before = (iota((rows, rows), 0) < iota((rows, rows), 1)).astype(BF16)
    movedf = moved.astype(F32)
    rank = jnp.dot(movedf.astype(BF16), before, preferred_element_type=F32)
    coming = moved & (ns // rows == me)
    slot_to = jnp.sum(jnp.where(coming, ns - me * rows + 1, 0), axis=0, keepdims=True) - 1
    rank_in = jnp.sum(jnp.where(coming, rank, 0.0), axis=0, keepdims=True).astype(jnp.int32)
    landing = (iota((rows, rows), 0) == slot_to).astype(F32).astype(BF16)
    at16 = iota((EXTRA, rows), 0)

    def taken(offset):
        hot = (at16 == rank_in + (skip + offset)) & (slot_to >= 0)
        return lax.dot_general(landing, hot.astype(F32).astype(BF16), NT, preferred_element_type=F32)

    take_resid = taken(MIG)
    take_ids = taken(2 * MIG)
    vacated = jnp.sum(take_resid, axis=1, keepdims=True) > 0.5
    in_own = own_v[0].astype(F32)
    in_pair = pair_v[0].astype(F32)
    for k in range(1, replicas):
        in_own = in_own + own_v[k].astype(F32)
        in_pair = in_pair + pair_v[k].astype(F32)
    in_own, in_pair = in_own.astype(BF16), in_pair.astype(BF16)
    first_core = core == 0
    in_low = jnp.where(first_core, in_own, in_pair)
    in_high = jnp.where(first_core, in_pair, in_own)
    picked = take_resid.astype(BF16)
    resid = resid_ref[...]
    new_low = jnp.where(
        vacated, jnp.dot(picked, in_low, preferred_element_type=F32), resid[:, :half].astype(F32)
    ).astype(BF16)
    new_high = jnp.where(
        vacated, jnp.dot(picked, in_high, preferred_element_type=F32), resid[:, half:].astype(F32)
    ).astype(BF16)
    new_ref[...] = jnp.where(first_core, new_low, new_high)
    normed = norm(jnp.concatenate([new_low, new_high], axis=1), gain_ref[...])
    logits = lax.dot_general(normed, router_ref[...], NT, preferred_element_type=F32)
    experts = logits.shape[1]
    ids_in = jnp.dot(take_ids.astype(BF16), in_low[:, :LANES], preferred_element_type=F32)
    eye = onehot(iota((rows, rows), 0) == iota((rows, rows), 1))
    mine = at_sub == me
    moved_me = jnp.sum(jnp.where(mine, movedf, 0.0), axis=0, keepdims=True)
    facts = jnp.concatenate(
        [ids_ref[...].astype(F32), moved_me, jnp.zeros((5, rows), F32)], axis=0
    ).astype(BF16)
    ids = lax.dot_general(eye, facts, NT, preferred_element_type=F32)
    moved_col = ids[:, 2:3]
    id1 = jnp.where(vacated, ids_in[:, 0:1], ids[:, 0:1]).astype(jnp.int32)
    id2 = jnp.where(vacated, ids_in[:, 1:2], ids[:, 1:2]).astype(jnp.int32)
    at_e = iota((rows, experts), 1)
    hit1, hit2 = id1 == at_e, id2 == at_e
    picked1 = jnp.sum(jnp.where(hit1, logits, 0.0), axis=1, keepdims=True)
    picked2 = jnp.sum(jnp.where(hit2, logits, 0.0), axis=1, keepdims=True)
    gate = jax.nn.sigmoid(picked1 - picked2)
    gate_ref[...] = jnp.broadcast_to(gate, gate_ref.shape)
    old1 = ids[:, 0:1].astype(jnp.int32) == at_e
    old2 = ids[:, 1:2].astype(jnp.int32) == at_e
    normal = ((old1 | old2) & (moved_col < 0.5)).astype(F32).astype(BF16)
    after = (iota((rows, rows), 0) > iota((rows, rows), 1)).astype(BF16)
    slot = jnp.dot(after, normal, preferred_element_type=F32)
    slot1 = jnp.sum(jnp.where(hit1, slot, 0.0), axis=1, keepdims=True)
    slot2 = jnp.sum(jnp.where(hit2, slot, 0.0), axis=1, keepdims=True)
    in_rank = jnp.sum(
        jnp.where(take_resid > 0.5, iota((rows, EXTRA), 1), 0), axis=1, keepdims=True
    ) - (skip + MIG)
    slot1 = jnp.where(vacated, cap + in_rank, slot1.astype(jnp.int32))
    slot2 = jnp.where(vacated, cap + in_rank, slot2.astype(jnp.int32))
    lane = iota((rows, replicas * size), 1)
    first_ref[...] = (lane == (id1 ^ me) * size + slot1).astype(F32).astype(BF16)
    second_ref[...] = (lane == (id2 ^ me) * size + slot2).astype(F32).astype(BF16)


def make_gates(own, pair, after, resid, slots, ids, gain, router, cap):
    replicas = len(own)
    size, half = own[0].shape
    rows, width = resid.shape
    vm = pl.BlockSpec(memory_space=pltpu.VMEM)
    hbm = pl.BlockSpec(memory_space=pl.ANY)
    hot = jax.ShapeDtypeStruct((rows, replicas * size), BF16)
    return pl.pallas_call(
        functools.partial(gates_kernel, cap, replicas),
        out_shape=(
            hot,
            hot,
            jax.ShapeDtypeStruct((rows, LANES), F32),
            jax.ShapeDtypeStruct((rows, half), BF16),
        ),
        in_specs=[hbm] * (2 * replicas + 2) + [vm] * 4,
        out_specs=(vm,) * 4,
        scratch_shapes=[
            pltpu.VMEM((rows, width), BF16),
            pltpu.VMEM((replicas, EXTRA, half), BF16),
            pltpu.VMEM((replicas, EXTRA, half), BF16),
            pltpu.SemaphoreType.DMA((2 * replicas + 1,)),
        ],
        compiler_params=pltpu.CompilerParams(vmem_limit_bytes=VMEM_BYTES),
        cost_estimate=pl.CostEstimate(flops=200_000_000, bytes_accessed=6_000_000, transcendentals=0),
        name="gates",
    )(*own, *pair, after, resid, slots, ids.T, gain[None, :], router.T)


def combine_kernel(replicas, *refs):
    blocks = refs[:replicas]
    first_hbm, second_hbm, gate_hbm, after_hbm, out_ref, all_v, first_ref, second_ref, gate_ref, sem = refs[
        replicas:
    ]
    size = blocks[0].shape[0]
    load(
        sem,
        (first_hbm, first_ref),
        (second_hbm, second_ref),
        (gate_hbm, gate_ref),
        *[(blocks[k], all_v.at[pl.ds(k * size, size)]) for k in range(replicas)],
    )
    gate = gate_ref[:, 0:1]
    one = jnp.dot(first_ref[...], all_v[...], preferred_element_type=F32)
    two = jnp.dot(second_ref[...], all_v[...], preferred_element_type=F32)
    out_ref[...] = (gate * one + (1.0 - gate) * two).astype(BF16)


def combine(blocks, first, second, gate, after):
    replicas = len(blocks)
    size, half = blocks[0].shape
    rows = first.shape[0]
    vm = pl.BlockSpec(memory_space=pltpu.VMEM)
    hbm = pl.BlockSpec(memory_space=pl.ANY)
    return pl.pallas_call(
        functools.partial(combine_kernel, replicas),
        out_shape=jax.ShapeDtypeStruct((rows, half), BF16),
        in_specs=[hbm] * (replicas + 4),
        out_specs=vm,
        scratch_shapes=[
            pltpu.VMEM((replicas * size, half), BF16),
            pltpu.VMEM(first.shape, BF16),
            pltpu.VMEM(second.shape, BF16),
            pltpu.VMEM(gate.shape, F32),
            pltpu.SemaphoreType.DMA((replicas + 3,)),
        ],
        compiler_params=pltpu.CompilerParams(vmem_limit_bytes=VMEM_BYTES),
        cost_estimate=pl.CostEstimate(flops=400_000_000, bytes_accessed=2_500_000, transcendentals=0),
        name="combine",
    )(*blocks, first, second, gate, after)


def choose_kernel(turn, plan_hbm, *refs):
    choices = refs[:-4]
    out_ref, plan_sm, sem, plan_sem = refs[-4:]
    load(plan_sem, (plan_hbm, plan_sm))
    index = plan_sm[0, 24 + turn]
    for i, choice in enumerate(choices):
        @pl.when(index == i)
        def _():
            load(sem, (choice, out_ref))


def choose(plan, held, turn):
    hbm = pl.BlockSpec(memory_space=pl.ANY)
    return pl.pallas_call(
        functools.partial(choose_kernel, turn),
        out_shape=jax.ShapeDtypeStruct(held[0].shape, BF16),
        in_specs=[hbm] * (1 + len(held)),
        out_specs=pl.BlockSpec(memory_space=pltpu.VMEM),
        scratch_shapes=[
            pltpu.SMEM(plan.shape, jnp.int32),
            pltpu.SemaphoreType.DMA((1,)),
            pltpu.SemaphoreType.DMA((1,)),
        ],
        compiler_params=pltpu.CompilerParams(vmem_limit_bytes=VMEM_BYTES),
        cost_estimate=pl.CostEstimate(flops=0, bytes_accessed=0, transcendentals=0),
        name="choose",
    )(plan, *held)


def patch_kernel(count, plan_hbm, *refs):
    choices = refs[:count]
    tail_hbm, out_hbm, token_ref, plan_sm, slabs, sem, slab_sem, out_sem = refs[count:]
    load(sem, (plan_hbm, plan_sm))
    index = plan_sm[0, 0]
    for i, choice in enumerate(choices):
        @pl.when(index == i)
        def _():
            load(slab_sem, (choice, slabs))
    def moves(m):
        to = plan_sm[0, 16 + m]
        return to, [
            pltpu.make_async_copy(
                slabs.at[2 * m + side],
                out_hbm.at[side, jnp.maximum(to, 0)],
                out_sem.at[2 * m + side],
            )
            for side in range(2)
        ]

    for m in range(MIG):
        to, copies = moves(m)

        @pl.when(to >= 0)
        def _():
            for copy in copies:
                copy.start()
    for m in range(MIG):
        to, copies = moves(m)

        @pl.when(to >= 0)
        def _():
            for copy in copies:
                copy.wait()
    token_ref[...] = jnp.zeros(token_ref.shape, F32)


def patch(plan, held, tail_new):
    hbm = pl.BlockSpec(memory_space=pl.ANY)
    count = len(held)
    return pl.pallas_call(
        functools.partial(patch_kernel, count),
        out_shape=(
            jax.ShapeDtypeStruct(tail_new.shape, BF16),
            jax.ShapeDtypeStruct((8, LANES), F32),
        ),
        in_specs=[hbm] * (2 + count),
        out_specs=(hbm, pl.BlockSpec(memory_space=pltpu.VMEM)),
        scratch_shapes=[
            pltpu.SMEM(plan.shape, jnp.int32),
            pltpu.VMEM(held[0].shape, BF16),
            pltpu.SemaphoreType.DMA((1,)),
            pltpu.SemaphoreType.DMA((1,)),
            pltpu.SemaphoreType.DMA((2 * MIG,)),
        ],
        input_output_aliases={1 + count: 0},
        compiler_params=pltpu.CompilerParams(vmem_limit_bytes=VMEM_BYTES),
        cost_estimate=pl.CostEstimate(flops=0, bytes_accessed=0, transcendentals=0),
        name="patch",
    )(plan, *held, tail_new)


def body(
    hidden_in, prompt_kv, tail_kv, group_of, prompt_len, tail_len, bucket_of, bias_table,
    attn_gain, w_query, w_key, w_value, w_out, ffn_gain, router_weight, expert_ids,
    w_gate, w_up, w_down, new_slot,
):
    rows, width = hidden_in.shape
    replicas = lax.axis_size("req")
    pieces = lax.axis_size("tp")
    experts = router_weight.shape[1]
    cap = -(-(5 * rows * TOP // (4 * experts)) // 16) * 16
    half = width // 2

    def across(axis, size, k):
        return lambda v: lax.ppermute(v, axis, [(i, i ^ k) for i in range(size)])

    def over_req(k):
        return across("req", replicas, k)

    def over_tp(k):
        return across("tp", pieces, k)

    low_bits, low = low_part(replicas)
    query, key_new, value_new, packet = project(
        new_slot, tail_len, hidden_in, attn_gain, w_query, w_key, w_value, tail_kv
    )
    held = [packet] + [
        over_req(h << low_bits)(packet) for h in range(1, replicas >> low_bits)
    ]
    wouts = [w_out, over_tp(1)(w_out)]
    for k in range(2, pieces, 2):
        wouts += [over_tp(k)(w) for w in wouts[:2]]
    head_out, tail_new = attention(
        query, key_new, value_new, prompt_kv, tail_kv, group_of, prompt_len, tail_len, bucket_of,
        bias_table,
    )
    heads = [head_out] + [over_tp(k)(head_out) for k in range(1, pieces)]
    slots = new_slot.reshape(replicas, rows)
    place, extra, wide, kron, plan = make_plan(
        slots, expert_ids, experts, cap, [head_out] + held[1:] + wouts[2:]
    )
    chosen = [choose(plan, held, j) for j in range(1, low)]
    resid, *blocks = dispatch(
        heads, wouts, hidden_in, ffn_gain, place, extra, wide, chosen, replicas
    )
    near, each = far_part(replicas, pieces)

    def far(f):
        pairs = []
        for r in range(replicas):
            for t in range(pieces):
                to = r ^ (near + (t >> 1) * each + f)
                pairs.append((r * pieces + t, to * pieces + t))
        return lax.ppermute(blocks[near + f], ("req", "tp"), pairs)

    distant = [far(f) for f in range(each)]
    own = [blocks[0]] + [over_req(k)(blocks[k]) for k in range(1, near)] + distant
    for turn in range(1, pieces // 2):
        own += [over_tp(2 * turn)(b) for b in distant]
    pair = [over_tp(1)(b) for b in own]
    keep, give = expert(own, pair, w_gate, w_up, w_down, pieces)
    held = held + [over_req(j + 1)(p) for j, p in enumerate(chosen)]
    back = give_back(keep, over_tp(1)(give), kron, cap, replicas)
    first, second, gate, resid_new = make_gates(
        own, pair, plan, resid, slots, expert_ids, ffn_gain, router_weight, cap
    )
    result = [back[0]] + [over_req(k)(back[k]) for k in range(1, replicas)]
    new_tail_kv, token = patch(plan, held, tail_new)
    mixed = combine(result, first, second, gate, token)
    k = 2
    while k < pieces:
        other = over_tp(k)(mixed)
        mixed = mixed.astype(F32) + other.astype(F32)
        k *= 2
        if k < pieces:
            mixed = mixed.astype(BF16)
    out_half = (resid_new.astype(F32) + mixed.astype(F32)).astype(BF16)
    out_other = over_tp(1)(out_half)
    core = lax.axis_index("tp") & 1
    out_hidden = jnp.where(
        core == 0,
        jnp.concatenate([out_half, out_other], axis=1),
        jnp.concatenate([out_other, out_half], axis=1),
    )
    return (out_hidden, new_tail_kv)


def solution(mesh):
    return jax.shard_map(
        body,
        mesh=mesh,
        in_specs=(
            P("req", None), P(None, "req", None, "tp"), P(None, "req", None, "tp"),
            P("req"), P("req"), P("req"), P(), P(None, "tp"), P(),
            P(None, "tp"), P(None, "tp"), P(None, "tp"), P("tp", None), P(), P(),
            P("req", None), P("req", None, "tp"), P("req", None, "tp"), P("req", "tp", None), P(),
        ),
        out_specs=(P("req", None), P(None, "req", None, "tp")),
        check_vma=False,
    )
```
